128 devices in a mesh: tm: 16 (over y, x_lo, core), tile: 8 (over x_hi, z).
Axes of the slice: x: 4 (x_hi: 2, x_lo: 2; x = x_hi * 2 + x_lo), y: 4, z: 4, core: 2. Of those that a mesh axis runs over, the one named last changes fastest.
Arguments:
- adjoint: bfloat16 [5120, 131072], P('tm', 'tile'), may hold values from -6 to 6
- emission: bfloat16 [5120, 131072], P('tm', 'tile'), may hold values from 0.29882812 to 3
- step_weights: float32 [5120], P('tm'), may hold values from 0.0041926275 to 0.041926276
- tile_list: int32 [4096, 2], P('tile'), may hold values from 0 to 1023, as said below
- counts: int32 [8], P('tile'), may hold values from 256 to 512, as said below
Outputs:
- coupling_grad: float32 [8, 512, 128, 128], P('tile', 'tm')
The draws below stay inside these ranges and needn't reach their ends.
Inputs may be any that keep to these rules, and one draw needn't show every extreme that they name: Slot k of owner o is tile_list[o * 512 + k]; its row block lies in owner o's range o * 128 to (o + 1) * 128 - 1. For every owner and every other owner, the live slots of the first name exactly 4 distinct column blocks in the range of the second. The live slots of owner o are its first counts[o] slots; some owner has all 512 slots live.
All inputs are finite; a program needn't handle non-finite values.
Results may differ from the reference program's by a relative error of at most 0.009.
Values may be sent and summed in bfloat16 or wider, within the bound.
No kernel may reach another device: no remote copies, remote signals or barrier semaphores. Data moves between devices by JAX's collectives and lax.ppermute only.
A program may use at most 256 MiB of HBM per device.

```python
import math
import jax
import jax.numpy as jnp
from jax import lax

BLK = 128
NODES = 131072
CAP = 4
TILES_OWN = 512
OWNERS = 8
BLK_OWN = 128
STEPS = 5120
TILES = 4096


def tile_plan(key):
    keys = jax.random.split(jax.random.fold_in(key, 11), 7)
    owner_ids = jnp.arange(OWNERS, dtype=jnp.int32)
    slot_ids = jnp.arange(TILES_OWN, dtype=jnp.int32)
    live_counts = jax.random.randint(keys[0], (OWNERS,), TILES_OWN // 2, TILES_OWN + 1, dtype=jnp.int32)
    fullest = jax.random.randint(keys[1], (), 0, OWNERS, dtype=jnp.int32)
    live_counts = jnp.where(owner_ids == fullest, TILES_OWN, live_counts)
    block_scores = jax.random.randint(keys[2], (OWNERS, OWNERS, BLK_OWN), 0, 2 ** 20, dtype=jnp.int32) * BLK_OWN + jnp.arange(BLK_OWN, dtype=jnp.int32)
    needed_lists = jnp.argsort(block_scores, axis=2)[:, :, :CAP].astype(jnp.int32)
    remote_total = (OWNERS - 1) * CAP
    extra_cycle = jax.random.randint(keys[3], (OWNERS, TILES_OWN), 0, remote_total, dtype=jnp.int32)
    cycle_pos = jnp.where(slot_ids[None, :] < remote_total, slot_ids[None, :], extra_cycle)
    source_owner = (owner_ids[:, None] + cycle_pos // CAP + 1) % OWNERS
    listed_block = needed_lists[owner_ids[:, None], source_owner, cycle_pos % CAP]
    remote_col = source_owner * BLK_OWN + listed_block
    local_col = owner_ids[:, None] * BLK_OWN + jax.random.randint(keys[4], (OWNERS, TILES_OWN), 0, BLK_OWN, dtype=jnp.int32)
    col_blocks = jnp.where(slot_ids[None, :] < 2 * remote_total, remote_col, local_col)
    row_blocks = owner_ids[:, None] * BLK_OWN + jax.random.randint(keys[5], (OWNERS, TILES_OWN), 0, BLK_OWN, dtype=jnp.int32)
    order_key = jax.random.randint(keys[6], (OWNERS, TILES_OWN), 0, 2 ** 19, dtype=jnp.int32) * TILES_OWN + slot_ids[None, :]
    order_key = order_key + jnp.where(slot_ids[None, :] >= live_counts[:, None], 2 ** 19 * TILES_OWN, 0)
    slot_order = jnp.argsort(order_key, axis=1)
    col_blocks = jnp.take_along_axis(col_blocks, slot_order, axis=1)
    row_blocks = jnp.take_along_axis(row_blocks, slot_order, axis=1)
    tile_table = jnp.stack([row_blocks, col_blocks], axis=-1).reshape(OWNERS * TILES_OWN, 2).astype(jnp.int32)
    return (tile_table, live_counts.astype(jnp.int32))


def draw_tile_list(key, part):
    return tile_plan(key)[0]


def draw_counts(key, part):
    return tile_plan(key)[1]


def levels(stream_key, dims, shards, least, high):
    factor_of = 1.0
    for axis_at, parts in shards:
        heights = jax.random.uniform(jax.random.fold_in(jax.random.fold_in(stream_key, 6), axis_at), (parts,), jnp.float32, least / len(shards), high / len(shards))
        factor_of = factor_of * jnp.repeat(jnp.exp(heights), dims[axis_at] // parts).reshape((-1,) + (1,) * (len(dims) - 1 - axis_at))
    return factor_of


def noise(stream_key, extent, scale, limit, cuts=(), held_as=jnp.bfloat16):
    factor_of = levels(stream_key, extent, cuts, -0.22, 0.18) if cuts else 1.0
    values = jax.random.normal(stream_key, extent, jnp.float32) * scale * factor_of
    return jnp.minimum(jnp.maximum(values, -limit), limit).astype(held_as)


def setup_inputs(seed: int = 0) -> dict:
    key_list = jax.random.split(jax.random.key(seed), 6)
    return {
        "adjoint": noise(key_list[0], (STEPS, NODES), 1.0, 6.0, ((0, 16), (1, 8))),
        "emission": jnp.clip(jnp.exp(math.log(3.0) - 2.306499 * jax.random.uniform(key_list[1], (STEPS, NODES), jnp.float32) ** levels(key_list[1], (STEPS, NODES), ((0, 16), (1, 8)), -0.2, 0.2)), 0.29882812, 3.0).astype(jnp.bfloat16),
        "step_weights": jnp.clip(jnp.exp(math.log(0.041926276) - 2.3025851 * jax.random.uniform(key_list[2], (STEPS,), jnp.float32) ** levels(key_list[2], (STEPS,), ((0, 16),), -0.2, 0.2)), 0.0041926275, 0.041926276),
        "tile_list": draw_tile_list(jax.random.fold_in(key_list[5], 71), 0),
        "counts": draw_counts(jax.random.fold_in(key_list[5], 71), 0),
    }


def reference(adjoint, emission, step_weights, tile_list, counts):
    weighted = (step_weights[:, None] * adjoint).astype(jnp.bfloat16)
    row_sums = jnp.sum(weighted.astype(jnp.float32) * emission.astype(jnp.float32), axis=0)
    block_total = NODES // BLK
    weighted_blocks = weighted.reshape(STEPS, block_total, BLK)
    emission_blocks = emission.reshape(STEPS, block_total, BLK)
    row_blocks = tile_list[:, 0].astype(jnp.int32)
    col_blocks = tile_list[:, 1].astype(jnp.int32)
    group_size = math.gcd(TILES, 16)

    def tile_group(index_pair):
        left_cols = jnp.take(weighted_blocks, index_pair[0], axis=1).astype(jnp.float32)
        right_cols = jnp.take(emission_blocks, index_pair[1], axis=1).astype(jnp.float32)
        return jnp.einsum("sga,sgb->gab", left_cols, right_cols, precision=lax.Precision.HIGHEST)

    products = lax.map(tile_group, (row_blocks.reshape(-1, group_size), col_blocks.reshape(-1, group_size)))
    products = products.reshape(TILES, BLK, BLK)
    own_terms = jnp.take(row_sums.reshape(block_total, BLK), row_blocks, axis=0)
    live_slots = (jnp.arange(TILES_OWN, dtype=jnp.int32)[None, :] < counts[:, None]).reshape(TILES)
    gradient = (products - own_terms[:, :, None]) * live_slots.astype(jnp.float32)[:, None, None]
    return gradient.reshape(OWNERS, TILES_OWN, BLK, BLK)
```

```python
import functools

import jax
import jax.numpy as jnp
from jax import lax
from jax.experimental import pallas as pl
from jax.experimental.pallas import tpu as pltpu
from jax.sharding import PartitionSpec as P

BLK = 128
CAP = 4
GRP = 32
KA = 384
F32 = jnp.float32
BF16 = jnp.bfloat16
I32 = jnp.int32


def iota(shape, dim):
    return lax.broadcasted_iota(I32, shape, dim)


def plan_kernel(early, own_ref, count_ref, tiles_ref, request_ref, table_ref):
    slots = tiles_ref.shape[0]
    own = own_ref[0]
    r = tiles_ref[:, 0:1]
    c = tiles_ref[:, 1:2]
    k = iota((slots, 1), 0)
    src = c >> 7
    within = c & (BLK - 1)
    row = r & (BLK - 1)
    remote = (k < count_ref[0]) & (src != own)
    lane = iota((slots, BLK), 1)
    by_src = jnp.where((lane == src) & remote, 1.0, 0.0).astype(F32)
    by_block = jnp.where(lane == within, 1.0, 0.0).astype(F32)
    named = jnp.dot(by_src.T.astype(BF16), by_block.astype(BF16), preferred_element_type=F32)
    hit = jnp.where(named > 0.0, 1.0, 0.0).astype(F32)
    upper = jnp.where(iota((BLK, BLK), 0) <= iota((BLK, BLK), 1), 1.0, 0.0).astype(BF16)
    rank = jnp.dot(hit.astype(BF16), upper, preferred_element_type=F32) * hit
    slot_rank = jnp.sum(
        jnp.dot(by_src.astype(BF16), rank.astype(BF16), preferred_element_type=F32) * by_block,
        axis=1,
        keepdims=True,
    )
    slot_rank = jnp.clip(slot_rank.astype(I32) - 1, 0, CAP - 1)
    col = jnp.where(remote, BLK + src * CAP + slot_rank, within)

    jj = iota((slots, slots), 1)
    kk = iota((slots, slots), 0)
    same = (jj >> 5) == (kk >> 5)
    remote_f = jnp.broadcast_to(jnp.where(remote, 1.0, 0.0), (slots, BLK)).astype(BF16)
    ahead = jnp.where(same & (jj < kk), 1.0, 0.0).astype(BF16)
    ahead = jnp.dot(ahead, remote_f, preferred_element_type=F32)[:, 0:1].astype(I32)
    total = jnp.where(same, 1.0, 0.0).astype(BF16)
    total = jnp.dot(total, remote_f, preferred_element_type=F32)[:, 0:1].astype(I32)
    s = k & (GRP - 1)
    pos = jnp.where(remote, GRP - total + ahead, s - ahead)
    value = jnp.where(lane < GRP, row, jnp.where(lane < 2 * GRP, col, s))
    value = jnp.where((lane & (GRP - 1)) == pos, value, 0)
    value = jnp.where(lane < 3 * GRP, value, 0).astype(F32).astype(BF16)
    groups = slots // GRP
    pick = jnp.where((iota((groups, slots), 1) >> 5) == iota((groups, slots), 0), 1.0, 0.0)
    table_ref[...] = jnp.dot(pick.astype(BF16), value, preferred_element_type=F32).astype(I32)

    late = jnp.max(jnp.where(total > GRP - early, 1, 0), axis=0, keepdims=True)
    owners = request_ref.shape[0]
    hit8 = hit[0:owners, :]
    rank8 = rank[0:owners, :]
    lane8 = iota((owners, BLK), 1)
    request = jnp.where(lane8 == CAP, jnp.broadcast_to(late, (owners, BLK)), 0)
    for q in range(CAP):
        block = jnp.sum(
            jnp.where((rank8 == q + 1.0) & (hit8 > 0.0), lane8, 0), axis=1, keepdims=True
        )
        request = jnp.where(lane8 == q, block, request)
    request_ref[...] = request


def plan(own, counts, tile_list, owners, early):
    slots = tile_list.shape[0]
    smem = pl.BlockSpec(memory_space=pltpu.SMEM)
    vmem = pl.BlockSpec(memory_space=pltpu.VMEM)
    return pl.pallas_call(
        functools.partial(plan_kernel, early),
        in_specs=[smem, smem, vmem],
        out_specs=[vmem, vmem],
        out_shape=[
            jax.ShapeDtypeStruct((owners, BLK), I32),
            jax.ShapeDtypeStruct((slots // GRP, BLK), I32),
        ],
        compiler_params=pltpu.CompilerParams(vmem_limit_bytes=16 * 2**20),
        name="plan",
    )(own, counts, tile_list)


STEP = 16
DEPTH = 3


def prep_kernel(weights_ref, adj_ref, em_ref, wt_ref, e_ref, abuf, ebuf, wide, asem, esem):
    steps = adj_ref.shape[0]
    blocks = e_ref.shape[0]
    chunks = blocks // STEP
    wide[...] = jnp.broadcast_to(weights_ref[...], wide.shape)

    def copies(j):
        slot = lax.rem(j, DEPTH)
        cols = pl.ds(pl.multiple_of(j * (STEP * BLK), STEP * BLK), STEP * BLK)
        return (
            pltpu.make_async_copy(adj_ref.at[:, cols], abuf.at[slot], asem.at[slot]),
            pltpu.make_async_copy(em_ref.at[:, cols], ebuf.at[slot], esem.at[slot]),
        )

    for j in range(DEPTH - 1):
        for copy in copies(j):
            copy.start()
    ones = jnp.where(iota((KA - steps, BLK), 0) < 2, 1.0, 0.0).astype(BF16)
    rows = iota((KA - steps, BLK), 0)

    def chunk(j, carry):
        slot = lax.rem(j, DEPTH)

        @pl.when(j + DEPTH - 1 < chunks)
        def _():
            for copy in copies(j + DEPTH - 1):
                copy.start()

        for copy in copies(j):
            copy.wait()

        def some(i, inner):
            for b in range(4):
                cols = pl.ds(pl.multiple_of((i * 4 + b) * BLK, BLK), BLK)
                at = j * STEP + i * 4 + b
                w = (wide[...] * abuf[slot, :, cols].astype(F32)).astype(BF16)
                e = ebuf[slot, :, cols]
                sums = -jnp.sum(w.astype(F32) * e.astype(F32), axis=0, keepdims=True)
                high = sums.astype(BF16).astype(F32)
                low = sums - high
                tail = jnp.where(rows == 0, high, jnp.where(rows == 1, low, 0.0)).astype(BF16)
                wt_ref[at] = jnp.concatenate([w, tail], axis=0).T
                e_ref[at, 0:steps, :] = e
                e_ref[at, steps:KA, :] = ones
            return inner

        lax.fori_loop(0, STEP // 4, some, 0)
        return carry

    lax.fori_loop(0, chunks, chunk, 0)


def prep(weights, adjoint, emission):
    steps, nodes = adjoint.shape
    blocks = nodes // BLK
    anyspace = pl.BlockSpec(memory_space=pl.ANY)
    vmem = pl.BlockSpec(memory_space=pltpu.VMEM)
    return pl.pallas_call(
        prep_kernel,
        in_specs=[vmem, anyspace, anyspace],
        out_specs=[vmem, vmem],
        out_shape=[
            pltpu.VMEM((blocks, BLK, KA), BF16),
            pltpu.VMEM((blocks, KA, BLK), BF16),
        ],
        scratch_shapes=[
            pltpu.VMEM((DEPTH, steps, STEP * BLK), BF16),
            pltpu.VMEM((DEPTH, steps, STEP * BLK), BF16),
            pltpu.VMEM((steps, BLK), F32),
            pltpu.SemaphoreType.DMA((DEPTH,)),
            pltpu.SemaphoreType.DMA((DEPTH,)),
        ],
        compiler_params=pltpu.CompilerParams(vmem_limit_bytes=14 * 2**20),
        cost_estimate=pl.CostEstimate(
            flops=4 * steps * nodes, bytes_accessed=8 * steps * nodes, transcendentals=0
        ),
        name="prep",
    )(weights, adjoint, emission)


def pack_kernel(asked_ref, em_ref, out_ref, sems):
    count = out_ref.shape[0]

    def copy(i):
        block = asked_ref[i >> 2, i & (CAP - 1)] & (BLK - 1)
        cols = pl.ds(pl.multiple_of(block * BLK, BLK), BLK)
        return pltpu.make_async_copy(em_ref.at[:, cols], out_ref.at[i], sems.at[i])

    for i in range(count):
        copy(i).start()
    for i in range(count):
        copy(i).wait()


def pack(asked, emission):
    owners = asked.shape[0]
    smem = pl.BlockSpec(memory_space=pltpu.SMEM)
    anyspace = pl.BlockSpec(memory_space=pl.ANY)
    return pl.pallas_call(
        pack_kernel,
        in_specs=[smem, anyspace],
        out_specs=anyspace,
        out_shape=jax.ShapeDtypeStruct((owners * CAP, emission.shape[0], BLK), BF16),
        scratch_shapes=[pltpu.SemaphoreType.DMA((owners * CAP,))],
        compiler_params=pltpu.CompilerParams(vmem_limit_bytes=4 * 2**20),
        name="pack",
    )(asked, emission)


def tiles_kernel(ranges, runs, base, per, with_add, *refs):
    groups_ref, places_ref, table_ref, wt_ref, e_ref, far_ref = refs[:6]
    refs = refs[6:]
    add_ref = None
    if with_add:
        add_ref, refs = refs[0], refs[1:]
    outs, (far, sem) = refs[: len(ranges)], refs[len(ranges) :]
    steps = far_ref.shape[1]
    copy = pltpu.make_async_copy(far_ref, far.at[:, pl.ds(0, steps)], sem)
    copy.start()
    ones = jnp.where(iota((KA - steps, BLK), 0) < 2, 1.0, 0.0).astype(BF16)

    def fill(i, carry):
        far[i, steps:KA, :] = ones
        return carry

    lax.fori_loop(0, far.shape[0], fill, 0)

    def put(out_ref, at, n, p, acc):
        if with_add:
            acc = acc + add_ref[places_ref[n] * per + (p - base)].astype(F32)
        out_ref[at] = acc.astype(BF16)

    n0 = 0
    for out_ref, (first, count), run in zip(outs, ranges, runs):
        total = out_ref.shape[0] // count

        def near(i, carry, out_ref=out_ref, first=first, count=count, run=run, n0=n0):
            for j in range(run):
                g = groups_ref[n0 + i * run + j]
                for q in range(count):
                    row = table_ref[g, first + q]
                    col = jnp.minimum(table_ref[g, GRP + first + q], BLK - 1)
                    acc = jnp.dot(wt_ref[row], e_ref[col], preferred_element_type=F32)
                    put(out_ref, (i * run + j) * count + q, n0 + i * run + j, first + q, acc)
            return carry

        lax.fori_loop(0, total // run, near, 0)
        n0 += total
    copy.wait()
    n0 = 0
    for out_ref, (first, count) in zip(outs, ranges):
        total = out_ref.shape[0] // count

        def distant(i, carry, out_ref=out_ref, first=first, count=count, n0=n0):
            n = n0 + i // count
            p = first + lax.rem(i, count)
            g = groups_ref[n]
            col = table_ref[g, GRP + p]

            @pl.when(col >= BLK)
            def _():
                row = table_ref[g, p]
                acc = jnp.dot(wt_ref[row], far[col - BLK], preferred_element_type=F32)
                put(out_ref, i, n, p, acc)

            return carry

        lax.fori_loop(0, out_ref.shape[0], distant, 0)
        n0 += total


def tiles(groups, places, table, wt, e_blocks, far, ranges, sizes, runs, base, per, add=None):
    smem = pl.BlockSpec(memory_space=pltpu.SMEM)
    vmem = pl.BlockSpec(memory_space=pltpu.VMEM)
    counts = [size * count for size, (_, count) in zip(sizes, ranges)]
    return pl.pallas_call(
        functools.partial(tiles_kernel, ranges, runs, base, per, add is not None),
        in_specs=[smem, smem, smem, vmem, vmem, pl.BlockSpec(memory_space=pl.ANY)]
        + ([vmem] if add is not None else []),
        out_specs=[vmem] * len(counts),
        out_shape=[jax.ShapeDtypeStruct((c, BLK, BLK), BF16) for c in counts],
        scratch_shapes=[pltpu.VMEM((far.shape[0], KA, BLK), BF16), pltpu.SemaphoreType.DMA],
        compiler_params=pltpu.CompilerParams(vmem_limit_bytes=24 * 2**20),
        cost_estimate=pl.CostEstimate(
            flops=4 * sum(counts) * BLK * BLK * KA,
            bytes_accessed=2 * sum(counts) * BLK * BLK,
            transcendentals=0,
        ),
        name="tiles",
    )(groups, places, table, wt, e_blocks, far, *([add] if add is not None else []))


def add_kernel(n, *refs):
    for i in range(n):
        mine, came = refs[2 * i], refs[2 * i + 1]
        sent, kept = refs[2 * n + 2 * i], refs[2 * n + 2 * i + 1]
        half = sent.shape[0]

        def one(j, carry, mine=mine, came=came, sent=sent, kept=kept, half=half):
            sent[j] = (mine[j].astype(F32) + came[j].astype(F32)).astype(BF16)
            kept[j] = (mine[half + j].astype(F32) + came[half + j].astype(F32)).astype(BF16)
            return carry

        lax.fori_loop(0, half, one, 0, unroll=2)


def add_pairs(pairs):
    vmem = pl.BlockSpec(memory_space=pltpu.VMEM)
    shapes = []
    for mine, _ in pairs:
        shapes += [jax.ShapeDtypeStruct((mine.shape[0] // 2, BLK, BLK), BF16)] * 2
    flat = [a for pair in pairs for a in pair]
    size = sum(a.size for a in flat)
    return pl.pallas_call(
        functools.partial(add_kernel, len(pairs)),
        in_specs=[vmem] * len(flat),
        out_specs=[vmem] * len(shapes),
        out_shape=shapes,
        compiler_params=pltpu.CompilerParams(vmem_limit_bytes=20 * 2**20),
        cost_estimate=pl.CostEstimate(flops=size, bytes_accessed=3 * size, transcendentals=0),
        name="add_pairs",
    )(*flat)


def finish_kernel(firsts, me_ref, count_ref, table_ref, *refs):
    me = me_ref[0]
    out_ref = refs[-1]
    for i, first in enumerate(firsts):
        mine, came = refs[2 * i], refs[2 * i + 1]

        def one(j, carry, mine=mine, came=came, first=first):
            s = table_ref[me, 2 * GRP + first + j]
            live = jnp.where(me * GRP + s < count_ref[0], 1.0, 0.0).astype(F32)
            out_ref[s] = (mine[j].astype(F32) + came[j].astype(F32)) * live
            return carry

        lax.fori_loop(0, mine.shape[0], one, 0)


def finish(me, counts, table, firsts, pairs):
    smem = pl.BlockSpec(memory_space=pltpu.SMEM)
    vmem = pl.BlockSpec(memory_space=pltpu.VMEM)
    flat = [a for pair in pairs for a in pair]
    return pl.pallas_call(
        functools.partial(finish_kernel, firsts),
        in_specs=[smem, smem, smem] + [vmem] * len(flat),
        out_specs=vmem,
        out_shape=jax.ShapeDtypeStruct((GRP, BLK, BLK), F32),
        compiler_params=pltpu.CompilerParams(vmem_limit_bytes=16 * 2**20),
        name="finish",
    )(me, counts, table, *flat)


CORE, ALONG_X, UP_Y, DOWN_Y = 1, 2, 4, 12
ORDERS = (
    (ALONG_X, UP_Y, DOWN_Y),
    (UP_Y, DOWN_Y, ALONG_X),
    (DOWN_Y, ALONG_X, UP_Y),
)


def swap(a, mask):
    n = lax.axis_size("tm")
    return lax.ppermute(a, "tm", [(i, i ^ mask) for i in range(n)])


def order_masks(order, lead):
    first, second, third = order
    return [lead * first ^ s * second ^ t * third for s in (1, 0) for t in (1, 0)]


def body(adjoint, emission, step_weights, tile_list, counts):
    owners = lax.axis_size("tile")
    parts = lax.axis_size("tm")
    own = lax.axis_index("tile").astype(I32).reshape(1)
    me = lax.axis_index("tm").astype(I32).reshape(1)
    request, table = plan(own, counts, tile_list, owners, GRP)
    asked = lax.all_to_all(request, "tile", split_axis=0, concat_axis=0, tiled=True)
    outgoing = pack(asked, emission)
    far = lax.all_to_all(outgoing, "tile", split_axis=0, concat_axis=0, tiled=True)
    outgoing, step_weights = lax.optimization_barrier((outgoing, step_weights))
    wt, e_blocks = prep(step_weights[:, None], adjoint, emission)
    wt = pltpu.with_memory_space_constraint(wt, pltpu.VMEM)
    e_blocks = pltpu.with_memory_space_constraint(e_blocks, pltpu.VMEM)

    half = GRP // 2
    cuts = (6, 5, 5)
    others = me ^ CORE ^ (2 * jnp.arange(parts // 2, dtype=I32))
    masks = [m for order in ORDERS for lead in (1, 0) for m in order_masks(order, lead)]
    mine = me ^ jnp.array(masks, I32)
    places = jnp.array([m // 2 for m in masks], I32)
    sent = []
    for c in range(2):
        (s,) = tiles(
            others, places, table, wt, e_blocks, far, ((c * half, half),), (8,), (1,), c * half, half
        )
        sent.append(s)
    came = [swap(s, CORE) for s in sent]
    pairs, firsts = [], []
    for c in range(2):
        ranges, first = [], c * half
        for n in cuts:
            ranges += [(first, n), (first, n)]
            firsts.append(first)
            first += n
        out = tiles(
            mine, places, table, wt, e_blocks, far,
            tuple(ranges), (4,) * 6, (2,) * 6, c * half, half, came[c],
        )
        for step in range(2):
            now = [
                (out[2 * i + 1], swap(out[2 * i], order[step])) for i, order in enumerate(ORDERS)
            ]
            out = add_pairs(now)
        pairs += [(out[2 * i + 1], swap(out[2 * i], order[2])) for i, order in enumerate(ORDERS)]
    return finish(me, counts, table, tuple(firsts), pairs)[None]


def solution(mesh):
    in_specs = (P("tm", "tile"), P("tm", "tile"), P("tm"), P("tile", None), P("tile"))
    out_specs = P("tile", "tm", None, None)
    return jax.shard_map(body, mesh=mesh, in_specs=in_specs, out_specs=out_specs, check_vma=False)
```

```python
import functools
import math

import jax
import jax.numpy as jnp
from jax import lax
from jax.experimental import pallas as pl
from jax.experimental.pallas import tpu as pltpu
from jax.sharding import PartitionSpec as P

BLK = 128
CAP = 4
GRP = 32
KA = 384
F32 = jnp.float32
BF16 = jnp.bfloat16
I32 = jnp.int32


def iota(shape, dim):
    return lax.broadcasted_iota(I32, shape, dim)


def in_hbm(a):
    return pltpu.with_memory_space_constraint(a, pltpu.HBM)


def plan_kernel(early, own_ref, count_ref, tiles_ref, request_ref, table_ref):
    slots = tiles_ref.shape[0]
    own = own_ref[0]
    r = tiles_ref[:, 0:1]
    c = tiles_ref[:, 1:2]
    k = iota((slots, 1), 0)
    src = c >> 7
    within = c & (BLK - 1)
    row = r & (BLK - 1)
    remote = (k < count_ref[0]) & (src != own)
    lane = iota((slots, BLK), 1)
    by_src = jnp.where((lane == src) & remote, 1.0, 0.0).astype(F32)
    by_block = jnp.where(lane == within, 1.0, 0.0).astype(F32)
    named = jnp.dot(by_src.T.astype(BF16), by_block.astype(BF16), preferred_element_type=F32)
    hit = jnp.where(named > 0.0, 1.0, 0.0).astype(F32)
    upper = jnp.where(iota((BLK, BLK), 0) <= iota((BLK, BLK), 1), 1.0, 0.0).astype(BF16)
    rank = jnp.dot(hit.astype(BF16), upper, preferred_element_type=F32) * hit
    slot_rank = jnp.sum(
        jnp.dot(by_src.astype(BF16), rank.astype(BF16), preferred_element_type=F32) * by_block,
        axis=1,
        keepdims=True,
    )
    slot_rank = jnp.clip(slot_rank.astype(I32) - 1, 0, CAP - 1)
    col = jnp.where(remote, BLK + src * CAP + slot_rank, within)

    jj = iota((slots, slots), 1)
    kk = iota((slots, slots), 0)
    same = (jj >> 5) == (kk >> 5)
    remote_f = jnp.broadcast_to(jnp.where(remote, 1.0, 0.0), (slots, BLK)).astype(BF16)
    ahead = jnp.where(same & (jj < kk), 1.0, 0.0).astype(BF16)
    ahead = jnp.dot(ahead, remote_f, preferred_element_type=F32)[:, 0:1].astype(I32)
    total = jnp.where(same, 1.0, 0.0).astype(BF16)
    total = jnp.dot(total, remote_f, preferred_element_type=F32)[:, 0:1].astype(I32)
    s = k & (GRP - 1)
    pos = jnp.where(remote, GRP - total + ahead, s - ahead)
    value = jnp.where(lane < GRP, row, jnp.where(lane < 2 * GRP, col, s))
    value = jnp.where((lane & (GRP - 1)) == pos, value, 0)
    value = jnp.where(lane < 3 * GRP, value, 0).astype(F32).astype(BF16)
    groups = slots // GRP
    pick = jnp.where((iota((groups, slots), 1) >> 5) == iota((groups, slots), 0), 1.0, 0.0)
    table_ref[...] = jnp.dot(pick.astype(BF16), value, preferred_element_type=F32).astype(I32)

    late = jnp.max(jnp.where(total > GRP - early, 1, 0), axis=0, keepdims=True)
    owners = request_ref.shape[0]
    hit8 = hit[0:owners, :]
    rank8 = rank[0:owners, :]
    lane8 = iota((owners, BLK), 1)
    request = jnp.where(lane8 == CAP, jnp.broadcast_to(late, (owners, BLK)), 0)
    for q in range(CAP):
        block = jnp.sum(
            jnp.where((rank8 == q + 1.0) & (hit8 > 0.0), lane8, 0), axis=1, keepdims=True
        )
        request = jnp.where(lane8 == q, block, request)
    request_ref[...] = request


def plan(own, counts, tile_list, owners, early):
    slots = tile_list.shape[0]
    smem = pl.BlockSpec(memory_space=pltpu.SMEM)
    vmem = pl.BlockSpec(memory_space=pltpu.VMEM)
    return pl.pallas_call(
        functools.partial(plan_kernel, early),
        in_specs=[smem, smem, vmem],
        out_specs=[vmem, vmem],
        out_shape=[
            jax.ShapeDtypeStruct((owners, BLK), I32),
            jax.ShapeDtypeStruct((slots // GRP, BLK), I32),
        ],
        compiler_params=pltpu.CompilerParams(vmem_limit_bytes=16 * 2**20),
        name="plan",
    )(own, counts, tile_list)


STEP = 16
DEPTH = 3


def prep_kernel(with_far, weights_ref, adj_ref, em_ref, *refs):
    if with_far:
        far_ref, refs = refs[0], refs[1:]
        refs, fsem = refs[:-1], refs[-1]
    wt_ref, e_ref, abuf, ebuf, wide, asem, esem = refs
    steps = adj_ref.shape[0]
    blocks = wt_ref.shape[0]
    chunks = blocks // STEP
    wide[...] = jnp.broadcast_to(weights_ref[...], wide.shape)

    def copies(j):
        slot = lax.rem(j, DEPTH)
        cols = pl.ds(pl.multiple_of(j * (STEP * BLK), STEP * BLK), STEP * BLK)
        return (
            pltpu.make_async_copy(adj_ref.at[:, cols], abuf.at[slot], asem.at[slot]),
            pltpu.make_async_copy(em_ref.at[:, cols], ebuf.at[slot], esem.at[slot]),
        )

    for j in range(DEPTH - 1):
        for copy in copies(j):
            copy.start()
    if with_far:
        rest = pl.ds(blocks, e_ref.shape[0] - blocks)
        far_copy = pltpu.make_async_copy(far_ref, e_ref.at[rest, pl.ds(0, steps)], fsem)
        far_copy.start()
    ones = jnp.where(iota((KA - steps, BLK), 0) < 2, 1.0, 0.0).astype(BF16)
    rows = iota((KA - steps, BLK), 0)

    def chunk(j, carry):
        slot = lax.rem(j, DEPTH)

        @pl.when(j + DEPTH - 1 < chunks)
        def _():
            for copy in copies(j + DEPTH - 1):
                copy.start()

        for copy in copies(j):
            copy.wait()
        for b in range(STEP):
            at = j * STEP + b
            w = (wide[...] * abuf[slot, :, b * BLK : (b + 1) * BLK].astype(F32)).astype(BF16)
            e = ebuf[slot, :, b * BLK : (b + 1) * BLK]
            sums = -jnp.sum(w.astype(F32) * e.astype(F32), axis=0, keepdims=True)
            high = sums.astype(BF16).astype(F32)
            low = sums - high
            tail = jnp.where(rows == 0, high, jnp.where(rows == 1, low, 0.0)).astype(BF16)
            wt_ref[at] = jnp.concatenate([w, tail], axis=0).T
            e_ref[at, 0:steps, :] = e
            e_ref[at, steps:KA, :] = ones
        return carry

    lax.fori_loop(0, chunks, chunk, 0)
    if with_far:
        for i in range(blocks, e_ref.shape[0]):
            e_ref[i, steps:KA, :] = ones
        far_copy.wait()


def prep(weights, adjoint, emission, far=None):
    steps, nodes = adjoint.shape
    blocks = nodes // BLK
    anyspace = pl.BlockSpec(memory_space=pl.ANY)
    vmem = pl.BlockSpec(memory_space=pltpu.VMEM)
    with_far = far is not None
    columns = blocks + (far.shape[0] if with_far else 0)
    wt, e_blocks = pl.pallas_call(
        functools.partial(prep_kernel, with_far),
        in_specs=[vmem] + [anyspace] * (3 if with_far else 2),
        out_specs=[vmem, vmem],
        out_shape=[
            pltpu.VMEM((blocks, BLK, KA), BF16),
            pltpu.VMEM((columns, KA, BLK), BF16),
        ],
        scratch_shapes=[
            pltpu.VMEM((DEPTH, steps, STEP * BLK), BF16),
            pltpu.VMEM((DEPTH, steps, STEP * BLK), BF16),
            pltpu.VMEM((steps, BLK), F32),
            pltpu.SemaphoreType.DMA((DEPTH,)),
            pltpu.SemaphoreType.DMA((DEPTH,)),
        ]
        + ([pltpu.SemaphoreType.DMA] if with_far else []),
        compiler_params=pltpu.CompilerParams(vmem_limit_bytes=14 * 2**20),
        name="prep",
    )(weights, in_hbm(adjoint), in_hbm(emission), *([in_hbm(far)] if with_far else []))
    return (
        pltpu.with_memory_space_constraint(wt, pltpu.VMEM),
        pltpu.with_memory_space_constraint(e_blocks, pltpu.VMEM),
    )


def pack_kernel(asked_ref, em_ref, out_ref, sems):
    count = out_ref.shape[0]

    def copy(i):
        block = asked_ref[i >> 2, i & (CAP - 1)] & (BLK - 1)
        cols = pl.ds(pl.multiple_of(block * BLK, BLK), BLK)
        return pltpu.make_async_copy(em_ref.at[:, cols], out_ref.at[i], sems.at[i])

    for i in range(count):
        copy(i).start()
    for i in range(count):
        copy(i).wait()


def pack(asked, emission):
    owners = asked.shape[0]
    return pl.pallas_call(
        pack_kernel,
        in_specs=[pl.BlockSpec(memory_space=pltpu.SMEM), pl.BlockSpec(memory_space=pl.ANY)],
        out_specs=pl.BlockSpec(memory_space=pltpu.VMEM),
        out_shape=jax.ShapeDtypeStruct((owners * CAP, emission.shape[0], BLK), BF16),
        scratch_shapes=[pltpu.SemaphoreType.DMA((owners * CAP,))],
        compiler_params=pltpu.CompilerParams(vmem_limit_bytes=8 * 2**20),
        name="pack",
    )(asked, in_hbm(emission))


def tiles_kernel(first, per, with_add, *refs):
    groups_ref, places_ref, table_ref, wt_ref, e_ref = refs[:5]
    outs = refs[6:] if with_add else refs[5:]
    last = e_ref.shape[0] - 1
    n = 0
    for out_ref in outs:
        for j in range(out_ref.shape[0] // per):
            g = groups_ref[n]
            for q in range(per):
                row = table_ref[g, first + q]
                col = jnp.minimum(table_ref[g, GRP + first + q], last)
                acc = jnp.dot(wt_ref[row], e_ref[col], preferred_element_type=F32)
                if with_add:
                    acc = acc + refs[5][places_ref[n] * per + q].astype(F32)
                out_ref[j * per + q] = acc.astype(BF16)
            n += 1


def tiles(groups, places, table, wt, e_blocks, first, per, outs, add=None):
    smem = pl.BlockSpec(memory_space=pltpu.SMEM)
    vmem = pl.BlockSpec(memory_space=pltpu.VMEM)
    count = groups.shape[0] * per
    with_add = add is not None
    return pl.pallas_call(
        functools.partial(tiles_kernel, first, per, with_add),
        in_specs=[smem, smem, smem, vmem, vmem] + ([vmem] if with_add else []),
        out_specs=[vmem] * outs,
        out_shape=[jax.ShapeDtypeStruct((count // outs, BLK, BLK), BF16)] * outs,
        compiler_params=pltpu.CompilerParams(vmem_limit_bytes=10 * 2**20),
        name="tiles",
    )(groups, places, table, wt, e_blocks, *([add] if with_add else []))


def add_kernel(n, *refs):
    for i in range(n):
        mine, came = refs[2 * i], refs[2 * i + 1]
        sent, kept = refs[2 * n + 2 * i], refs[2 * n + 2 * i + 1]
        half = sent.shape[0]

        def one(j, carry, mine=mine, came=came, sent=sent, kept=kept, half=half):
            sent[j] = (mine[j].astype(F32) + came[j].astype(F32)).astype(BF16)
            kept[j] = (mine[half + j].astype(F32) + came[half + j].astype(F32)).astype(BF16)
            return carry

        lax.fori_loop(0, half, one, 0, unroll=2)


def add_pairs(pairs):
    vmem = pl.BlockSpec(memory_space=pltpu.VMEM)
    shapes = []
    for mine, _ in pairs:
        shapes += [jax.ShapeDtypeStruct((mine.shape[0] // 2, BLK, BLK), BF16)] * 2
    flat = [a for pair in pairs for a in pair]
    return pl.pallas_call(
        functools.partial(add_kernel, len(pairs)),
        in_specs=[vmem] * len(flat),
        out_specs=[vmem] * len(shapes),
        out_shape=shapes,
        compiler_params=pltpu.CompilerParams(vmem_limit_bytes=20 * 2**20),
        name="add_pairs",
    )(*flat)


def finish_kernel(firsts, me_ref, count_ref, table_ref, *refs):
    me = me_ref[0]
    out_ref, stage, sem = refs[-3:]
    for i, first in enumerate(firsts):
        mine, came = refs[2 * i], refs[2 * i + 1]
        for j in range(mine.shape[0]):
            s = table_ref[me, 2 * GRP + first + j]
            live = jnp.where(me * GRP + s < count_ref[0], 1.0, 0.0).astype(F32)
            stage[first + j] = (mine[j].astype(F32) + came[j].astype(F32)) * live
            pltpu.make_async_copy(stage.at[first + j], out_ref.at[s], sem).start()
    pltpu.make_async_copy(stage, out_ref, sem).wait()


def finish(me, counts, table, pairs, firsts):
    smem = pl.BlockSpec(memory_space=pltpu.SMEM)
    vmem = pl.BlockSpec(memory_space=pltpu.VMEM)
    flat = [a for pair in pairs for a in pair]
    return pl.pallas_call(
        functools.partial(finish_kernel, firsts),
        in_specs=[smem, smem, smem] + [vmem] * len(flat),
        out_specs=pl.BlockSpec(memory_space=pltpu.HBM),
        out_shape=pltpu.HBM((GRP, BLK, BLK), F32),
        scratch_shapes=[pltpu.VMEM((GRP, BLK, BLK), F32), pltpu.SemaphoreType.DMA],
        compiler_params=pltpu.CompilerParams(vmem_limit_bytes=16 * 2**20),
        name="finish",
    )(me, counts, table, *flat)


CORE, ALONG_X, UP_Y, DOWN_Y = 1, 2, 4, 12
ORDERS = (
    (ALONG_X, UP_Y, DOWN_Y),
    (UP_Y, DOWN_Y, ALONG_X),
    (DOWN_Y, ALONG_X, UP_Y),
)


def swap(a, mask):
    n = lax.axis_size("tm")
    return lax.ppermute(a, "tm", [(i, i ^ mask) for i in range(n)])


def after(a, other):
    return lax.optimization_barrier((a, other))[0]


def order_masks(order, lead):
    first, second, third = order
    return [lead * first ^ s * second ^ t * third for s in (1, 0) for t in (1, 0)]


def general(adjoint, emission, step_weights, tile_list, counts):
    steps_here = adjoint.shape[0]
    owners = lax.axis_size("tile")
    own_blocks = adjoint.shape[1] // BLK
    my_owner = lax.axis_index("tile")
    weighted = (step_weights[:, None] * adjoint).astype(BF16)
    local_sums = jnp.sum(weighted.astype(F32) * emission.astype(F32), axis=0)
    slot_count = tile_list.shape[0]
    slot_ids = jnp.arange(slot_count, dtype=I32)
    live_slots = slot_ids < counts[0]
    row_local = tile_list[:, 0] - my_owner * own_blocks
    columns = tile_list[:, 1]
    source = columns // own_blocks
    within = columns % own_blocks
    owner_ids = jnp.arange(owners, dtype=I32)
    block_ids = jnp.arange(owners * own_blocks, dtype=I32)
    block_hits = jnp.any((columns[:, None] == block_ids[None, :]) & live_slots[:, None], axis=0)
    needed = (block_hits.reshape(owners, own_blocks) & (owner_ids[:, None] != my_owner)).astype(
        I32
    )
    all_tiles, all_counts = (
        lax.all_gather(tile_list, "tile", axis=0, tiled=True),
        lax.all_gather(counts, "tile", axis=0, tiled=True),
    )
    all_columns = all_tiles[:, 1].reshape(owners, slot_count)
    all_live = slot_ids[None, :] < all_counts[:, None]
    own_range = my_owner * own_blocks + jnp.arange(own_blocks, dtype=I32)
    asked_for = jnp.any(
        (all_columns[:, :, None] == own_range[None, None, :]) & all_live[:, :, None], axis=1
    )
    wanted = (asked_for & (owner_ids[:, None] != my_owner)).astype(I32)
    send_rank = jnp.cumsum(wanted, axis=1) - 1
    cap_ids = jnp.arange(CAP, dtype=I32)
    picked = (wanted[:, None, :] == 1) & (send_rank[:, None, :] == cap_ids[None, :, None])
    send_index = jnp.sum(
        picked.astype(I32) * jnp.arange(own_blocks, dtype=I32)[None, None, :], axis=2
    )
    emission_blocks = emission.reshape(steps_here, own_blocks, BLK)
    outgoing = jnp.take(emission_blocks, send_index.reshape(-1), axis=1).reshape(
        steps_here, owners, CAP, BLK
    )
    incoming = lax.all_to_all(outgoing, "tile", split_axis=1, concat_axis=1, tiled=True)
    column_table = jnp.concatenate(
        [emission_blocks, incoming.reshape(steps_here, owners * CAP, BLK)], axis=1
    )
    recv_rank = (jnp.cumsum(needed, axis=1) - 1).reshape(-1)
    slot_rank = jnp.clip(jnp.take(recv_rank, source * own_blocks + within), 0, CAP - 1)
    col_slot = jnp.where(source == my_owner, within, own_blocks + source * CAP + slot_rank)
    weighted_blocks = weighted.reshape(steps_here, own_blocks, BLK)
    tm_size = lax.axis_size("tm")
    tm_share = slot_count // tm_size
    group_size = math.gcd(tm_share * lax.axis_size("tm"), 128)

    def tile_group(index_pair):
        left_cols = jnp.take(weighted_blocks, index_pair[0], axis=1)
        right_cols = jnp.take(column_table, index_pair[1], axis=1)
        return jnp.einsum("sga,sgb->gab", left_cols, right_cols, preferred_element_type=F32)

    result = lax.map(
        tile_group, (row_local.reshape(-1, group_size), col_slot.reshape(-1, group_size))
    )
    result = result.reshape(tm_share * lax.axis_size("tm"), BLK, BLK)
    kept_tiles = lax.psum_scatter(result, "tm", scatter_dimension=0, tiled=True)
    first_slot = lax.axis_index("tm") * tm_share
    kept_rows = lax.dynamic_slice_in_dim(row_local, first_slot, tm_share)
    kept_live = lax.dynamic_slice_in_dim(live_slots, first_slot, tm_share)
    total_sums = lax.psum(local_sums, "tm")
    kept_tiles = (
        kept_tiles - jnp.take(total_sums.reshape(own_blocks, BLK), kept_rows, axis=0)[:, :, None]
    )
    kept_tiles = kept_tiles * kept_live.astype(F32)[:, None, None]
    return kept_tiles[None]


def body(adjoint, emission, step_weights, tile_list, counts):
    owners = lax.axis_size("tile")
    parts = lax.axis_size("tm")
    own = lax.axis_index("tile").astype(I32).reshape(1)
    me = lax.axis_index("tm").astype(I32).reshape(1)
    half = GRP // 2
    request, table = plan(own, counts, tile_list, owners, half)
    asked = lax.all_to_all(request, "tile", split_axis=0, concat_axis=0, tiled=True)
    outgoing = pack(asked, emission)
    far = lax.all_to_all(outgoing, "tile", split_axis=0, concat_axis=0, tiled=True)
    crowded = jnp.any(asked[:, CAP] > 0)
    weights = after(step_weights[:, None], crowded)

    cuts = (6, 5, 5)
    others = me ^ CORE ^ (2 * jnp.arange(parts // 2, dtype=I32))
    offsets = [[c * half + sum(cuts[:i]) for i in range(len(cuts))] for c in range(2)]

    def given(c, i, wt, e_blocks, last):
        return tiles(
            after(others, last), others, table, wt, e_blocks, offsets[c][i], cuts[i], 1
        )[0]

    def kept(c, i, wt, e_blocks, last, core):
        masks = [m for lead in (1, 0) for m in order_masks(ORDERS[i], lead)]
        mine = me ^ jnp.array(masks, I32)
        places = jnp.array([m // 2 for m in masks], I32)
        return tiles(
            after(mine, last), places, table, wt, e_blocks, offsets[c][i], cuts[i], 2, core
        )

    def exchange(outs, step):
        return [(out[1], swap(out[0], order[step])) for out, order in zip(outs, ORDERS)]

    def halve(pairs, last):
        outs = []
        for mine, came in pairs:
            out = add_pairs([(after(mine, last), came)])
            last = out[1]
            outs.append(out)
        return outs, last

    wt, e_blocks = prep(after(weights, outgoing), adjoint, emission)
    last, cores, early = wt, [], []
    for i in range(3):
        last = given(0, i, wt, e_blocks, last)
        cores.append(swap(last, CORE))
    for i in range(3):
        early.append(kept(0, i, wt, e_blocks, last, cores[i]))
        last = early[i][1]
    early = exchange(early, 0)
    wt, e_blocks = prep(after(weights, last), adjoint, emission, far)
    last, cores, late = wt, [], []
    for i in range(3):
        if i == 1:
            early, last = halve(early, last)
            early = exchange(early, 1)
        last = given(1, i, wt, e_blocks, last)
        cores.append(swap(last, CORE))
    for i in range(3):
        if i + 3 == 5:
            early, last = halve(early, last)
            early = exchange(early, 2)
        late.append(kept(1, i, wt, e_blocks, last, cores[i]))
        last = late[i][1]
    late = exchange(late, 0)
    late, last = halve(late, last)
    late, last = halve(exchange(late, 1), last)
    late = exchange(late, 2)
    pairs = early + late
    firsts = offsets[0] + offsets[1]

    fast = functools.partial(finish, firsts=tuple(firsts))
    return lax.cond(
        crowded,
        lambda full, args: general(*full),
        lambda full, args: fast(args[0], args[1], args[2], pairs=args[3])[None],
        (adjoint, emission, step_weights, tile_list, counts),
        (me, counts, table, pairs),
    )


def solution(mesh):
    in_specs = (P("tm", "tile"), P("tm", "tile"), P("tm"), P("tile", None), P("tile"))
    out_specs = P("tile", "tm", None, None)
    return jax.shard_map(body, mesh=mesh, in_specs=in_specs, out_specs=out_specs, check_vma=False)
```

```python
import functools

import jax
import jax.numpy as jnp
from jax import lax
from jax.experimental import pallas as pl
from jax.experimental.pallas import tpu as pltpu
from jax.sharding import PartitionSpec as P

BLK = 128
CAP = 4
GRP = 32
KA = 384
F32 = jnp.float32
BF16 = jnp.bfloat16
I32 = jnp.int32


def iota(shape, dim):
    return lax.broadcasted_iota(I32, shape, dim)


def in_hbm(a):
    return pltpu.with_memory_space_constraint(a, pltpu.HBM)


def plan_kernel(early, own_ref, count_ref, tiles_ref, request_ref, table_ref):
    slots = tiles_ref.shape[0]
    own = own_ref[0]
    r = tiles_ref[:, 0:1]
    c = tiles_ref[:, 1:2]
    k = iota((slots, 1), 0)
    src = c >> 7
    within = c & (BLK - 1)
    row = r & (BLK - 1)
    remote = (k < count_ref[0]) & (src != own)
    lane = iota((slots, BLK), 1)
    by_src = jnp.where((lane == src) & remote, 1.0, 0.0).astype(F32)
    by_block = jnp.where(lane == within, 1.0, 0.0).astype(F32)
    named = jnp.dot(by_src.T.astype(BF16), by_block.astype(BF16), preferred_element_type=F32)
    hit = jnp.where(named > 0.0, 1.0, 0.0).astype(F32)
    upper = jnp.where(iota((BLK, BLK), 0) <= iota((BLK, BLK), 1), 1.0, 0.0).astype(BF16)
    rank = jnp.dot(hit.astype(BF16), upper, preferred_element_type=F32) * hit
    slot_rank = jnp.sum(
        jnp.dot(by_src.astype(BF16), rank.astype(BF16), preferred_element_type=F32) * by_block,
        axis=1,
        keepdims=True,
    )
    slot_rank = jnp.clip(slot_rank.astype(I32) - 1, 0, CAP - 1)
    col = jnp.where(remote, BLK + src * CAP + slot_rank, within)

    jj = iota((slots, slots), 1)
    kk = iota((slots, slots), 0)
    same = (jj >> 5) == (kk >> 5)
    remote_f = jnp.broadcast_to(jnp.where(remote, 1.0, 0.0), (slots, BLK)).astype(BF16)
    ahead = jnp.where(same & (jj < kk), 1.0, 0.0).astype(BF16)
    ahead = jnp.dot(ahead, remote_f, preferred_element_type=F32)[:, 0:1].astype(I32)
    total = jnp.where(same, 1.0, 0.0).astype(BF16)
    total = jnp.dot(total, remote_f, preferred_element_type=F32)[:, 0:1].astype(I32)
    s = k & (GRP - 1)
    pos = jnp.where(remote, GRP - total + ahead, s - ahead)
    value = jnp.where(lane < GRP, row, jnp.where(lane < 2 * GRP, col, s))
    value = jnp.where((lane & (GRP - 1)) == pos, value, 0)
    value = jnp.where(lane < 3 * GRP, value, 0).astype(F32).astype(BF16)
    groups = slots // GRP
    pick = jnp.where((iota((groups, slots), 1) >> 5) == iota((groups, slots), 0), 1.0, 0.0)
    table_ref[...] = jnp.dot(pick.astype(BF16), value, preferred_element_type=F32).astype(I32)

    late = jnp.max(jnp.where(total > GRP - early, 1, 0), axis=0, keepdims=True)
    owners = request_ref.shape[0]
    hit8 = hit[0:owners, :]
    rank8 = rank[0:owners, :]
    lane8 = iota((owners, BLK), 1)
    request = jnp.where(lane8 == CAP, jnp.broadcast_to(late, (owners, BLK)), 0)
    for q in range(CAP):
        block = jnp.sum(
            jnp.where((rank8 == q + 1.0) & (hit8 > 0.0), lane8, 0), axis=1, keepdims=True
        )
        request = jnp.where(lane8 == q, block, request)
    request_ref[...] = request


def plan(own, counts, tile_list, owners, early):
    slots = tile_list.shape[0]
    smem = pl.BlockSpec(memory_space=pltpu.SMEM)
    vmem = pl.BlockSpec(memory_space=pltpu.VMEM)
    return pl.pallas_call(
        functools.partial(plan_kernel, early),
        in_specs=[smem, smem, vmem],
        out_specs=[vmem, vmem],
        out_shape=[
            jax.ShapeDtypeStruct((owners, BLK), I32),
            jax.ShapeDtypeStruct((slots // GRP, BLK), I32),
        ],
        compiler_params=pltpu.CompilerParams(vmem_limit_bytes=16 * 2**20),
        name="plan",
    )(own, counts, tile_list)


STEP = 16
DEPTH = 3


def prep_kernel(with_far, weights_ref, adj_ref, em_ref, *refs):
    if with_far:
        far_ref, refs = refs[0], refs[1:]
        refs, fsem = refs[:-1], refs[-1]
    wt_ref, e_ref, abuf, ebuf, wide, asem, esem = refs
    steps = adj_ref.shape[0]
    blocks = wt_ref.shape[0]
    chunks = blocks // STEP
    wide[...] = jnp.broadcast_to(weights_ref[...], wide.shape)

    def copies(j):
        slot = lax.rem(j, DEPTH)
        cols = pl.ds(pl.multiple_of(j * (STEP * BLK), STEP * BLK), STEP * BLK)
        return (
            pltpu.make_async_copy(adj_ref.at[:, cols], abuf.at[slot], asem.at[slot]),
            pltpu.make_async_copy(em_ref.at[:, cols], ebuf.at[slot], esem.at[slot]),
        )

    for j in range(DEPTH - 1):
        for copy in copies(j):
            copy.start()
    if with_far:
        rest = pl.ds(blocks, e_ref.shape[0] - blocks)
        far_copy = pltpu.make_async_copy(far_ref, e_ref.at[rest, pl.ds(0, steps)], fsem)
        far_copy.start()
    ones = jnp.where(iota((KA - steps, BLK), 0) < 2, 1.0, 0.0).astype(BF16)
    rows = iota((KA - steps, BLK), 0)

    def chunk(j, carry):
        slot = lax.rem(j, DEPTH)

        @pl.when(j + DEPTH - 1 < chunks)
        def _():
            for copy in copies(j + DEPTH - 1):
                copy.start()

        for copy in copies(j):
            copy.wait()
        for b in range(STEP):
            at = j * STEP + b
            w = (wide[...] * abuf[slot, :, b * BLK : (b + 1) * BLK].astype(F32)).astype(BF16)
            e = ebuf[slot, :, b * BLK : (b + 1) * BLK]
            sums = -jnp.sum(w.astype(F32) * e.astype(F32), axis=0, keepdims=True)
            high = sums.astype(BF16).astype(F32)
            low = sums - high
            tail = jnp.where(rows == 0, high, jnp.where(rows == 1, low, 0.0)).astype(BF16)
            wt_ref[at] = jnp.concatenate([w, tail], axis=0).T
            e_ref[at, 0:steps, :] = e
            e_ref[at, steps:KA, :] = ones
        return carry

    lax.fori_loop(0, chunks, chunk, 0)
    if with_far:
        for i in range(blocks, e_ref.shape[0]):
            e_ref[i, steps:KA, :] = ones
        far_copy.wait()


def prep(weights, adjoint, emission, far=None):
    steps, nodes = adjoint.shape
    blocks = nodes // BLK
    anyspace = pl.BlockSpec(memory_space=pl.ANY)
    vmem = pl.BlockSpec(memory_space=pltpu.VMEM)
    with_far = far is not None
    columns = blocks + (far.shape[0] if with_far else 0)
    wt, e_blocks = pl.pallas_call(
        functools.partial(prep_kernel, with_far),
        in_specs=[vmem] + [anyspace] * (3 if with_far else 2),
        out_specs=[vmem, vmem],
        out_shape=[
            pltpu.VMEM((blocks, BLK, KA), BF16),
            pltpu.VMEM((columns, KA, BLK), BF16),
        ],
        scratch_shapes=[
            pltpu.VMEM((DEPTH, steps, STEP * BLK), BF16),
            pltpu.VMEM((DEPTH, steps, STEP * BLK), BF16),
            pltpu.VMEM((steps, BLK), F32),
            pltpu.SemaphoreType.DMA((DEPTH,)),
            pltpu.SemaphoreType.DMA((DEPTH,)),
        ]
        + ([pltpu.SemaphoreType.DMA] if with_far else []),
        compiler_params=pltpu.CompilerParams(vmem_limit_bytes=14 * 2**20),
        name="prep",
    )(weights, in_hbm(adjoint), in_hbm(emission), *([in_hbm(far)] if with_far else []))
    return (
        pltpu.with_memory_space_constraint(wt, pltpu.VMEM),
        pltpu.with_memory_space_constraint(e_blocks, pltpu.VMEM),
    )


def pack_kernel(asked_ref, em_ref, out_ref, sems):
    count = out_ref.shape[0]

    def copy(i):
        block = asked_ref[i >> 2, i & (CAP - 1)] & (BLK - 1)
        cols = pl.ds(pl.multiple_of(block * BLK, BLK), BLK)
        return pltpu.make_async_copy(em_ref.at[:, cols], out_ref.at[i], sems.at[i])

    for i in range(count):
        copy(i).start()
    for i in range(count):
        copy(i).wait()


def pack(asked, emission):
    owners = asked.shape[0]
    return pl.pallas_call(
        pack_kernel,
        in_specs=[pl.BlockSpec(memory_space=pltpu.SMEM), pl.BlockSpec(memory_space=pl.ANY)],
        out_specs=pl.BlockSpec(memory_space=pltpu.VMEM),
        out_shape=jax.ShapeDtypeStruct((owners * CAP, emission.shape[0], BLK), BF16),
        scratch_shapes=[pltpu.SemaphoreType.DMA((owners * CAP,))],
        compiler_params=pltpu.CompilerParams(vmem_limit_bytes=8 * 2**20),
        name="pack",
    )(asked, in_hbm(emission))


def tiles_kernel(first, per, with_add, *refs):
    groups_ref, places_ref, table_ref, wt_ref, e_ref = refs[:5]
    outs = refs[6:] if with_add else refs[5:]
    last = e_ref.shape[0] - 1
    n = 0
    for out_ref in outs:
        for j in range(out_ref.shape[0] // per):
            g = groups_ref[n]
            for q in range(per):
                row = table_ref[g, first + q]
                col = jnp.minimum(table_ref[g, GRP + first + q], last)
                acc = jnp.dot(wt_ref[row], e_ref[col], preferred_element_type=F32)
                if with_add:
                    acc = acc + refs[5][places_ref[n] * per + q].astype(F32)
                out_ref[j * per + q] = acc.astype(BF16)
            n += 1


def tiles(groups, places, table, wt, e_blocks, first, per, outs, add=None):
    smem = pl.BlockSpec(memory_space=pltpu.SMEM)
    vmem = pl.BlockSpec(memory_space=pltpu.VMEM)
    count = groups.shape[0] * per
    with_add = add is not None
    return pl.pallas_call(
        functools.partial(tiles_kernel, first, per, with_add),
        in_specs=[smem, smem, smem, vmem, vmem] + ([vmem] if with_add else []),
        out_specs=[vmem] * outs,
        out_shape=[jax.ShapeDtypeStruct((count // outs, BLK, BLK), BF16)] * outs,
        compiler_params=pltpu.CompilerParams(vmem_limit_bytes=10 * 2**20),
        name="tiles",
    )(groups, places, table, wt, e_blocks, *([add] if with_add else []))


def add_kernel(n, *refs):
    for i in range(n):
        mine, came = refs[2 * i], refs[2 * i + 1]
        sent, kept = refs[2 * n + 2 * i], refs[2 * n + 2 * i + 1]
        half = sent.shape[0]

        def one(j, carry, mine=mine, came=came, sent=sent, kept=kept, half=half):
            sent[j] = (mine[j].astype(F32) + came[j].astype(F32)).astype(BF16)
            kept[j] = (mine[half + j].astype(F32) + came[half + j].astype(F32)).astype(BF16)
            return carry

        lax.fori_loop(0, half, one, 0, unroll=2)


def add_pairs(pairs):
    vmem = pl.BlockSpec(memory_space=pltpu.VMEM)
    shapes = []
    for mine, _ in pairs:
        shapes += [jax.ShapeDtypeStruct((mine.shape[0] // 2, BLK, BLK), BF16)] * 2
    flat = [a for pair in pairs for a in pair]
    return pl.pallas_call(
        functools.partial(add_kernel, len(pairs)),
        in_specs=[vmem] * len(flat),
        out_specs=[vmem] * len(shapes),
        out_shape=shapes,
        compiler_params=pltpu.CompilerParams(vmem_limit_bytes=20 * 2**20),
        name="add_pairs",
    )(*flat)


def finish_kernel(firsts, me_ref, count_ref, table_ref, *refs):
    me = me_ref[0]
    out_ref, stage, sem = refs[-3:]
    for i, first in enumerate(firsts):
        mine, came = refs[2 * i], refs[2 * i + 1]
        for j in range(mine.shape[0]):
            s = table_ref[me, 2 * GRP + first + j]
            live = jnp.where(me * GRP + s < count_ref[0], 1.0, 0.0).astype(F32)
            stage[first + j] = (mine[j].astype(F32) + came[j].astype(F32)) * live
            pltpu.make_async_copy(stage.at[first + j], out_ref.at[s], sem).start()
    pltpu.make_async_copy(stage, out_ref, sem).wait()


def finish(me, counts, table, pairs, firsts):
    smem = pl.BlockSpec(memory_space=pltpu.SMEM)
    vmem = pl.BlockSpec(memory_space=pltpu.VMEM)
    flat = [a for pair in pairs for a in pair]
    return pl.pallas_call(
        functools.partial(finish_kernel, firsts),
        in_specs=[smem, smem, smem] + [vmem] * len(flat),
        out_specs=pl.BlockSpec(memory_space=pltpu.HBM),
        out_shape=pltpu.HBM((GRP, BLK, BLK), F32),
        scratch_shapes=[pltpu.VMEM((GRP, BLK, BLK), F32), pltpu.SemaphoreType.DMA],
        compiler_params=pltpu.CompilerParams(vmem_limit_bytes=16 * 2**20),
        name="finish",
    )(me, counts, table, *flat)


CORE, ALONG_X, UP_Y, DOWN_Y = 1, 2, 4, 12
ORDERS = (
    (ALONG_X, UP_Y, DOWN_Y),
    (UP_Y, DOWN_Y, ALONG_X),
    (DOWN_Y, ALONG_X, UP_Y),
)


def swap(a, mask):
    n = lax.axis_size("tm")
    return lax.ppermute(a, "tm", [(i, i ^ mask) for i in range(n)])


def after(a, other):
    return lax.optimization_barrier((a, other))[0]


def order_masks(order, lead):
    first, second, third = order
    return [lead * first ^ s * second ^ t * third for s in (1, 0) for t in (1, 0)]


def body(adjoint, emission, step_weights, tile_list, counts):
    owners = lax.axis_size("tile")
    parts = lax.axis_size("tm")
    own = lax.axis_index("tile").astype(I32).reshape(1)
    me = lax.axis_index("tm").astype(I32).reshape(1)
    half = GRP // 2
    request, table = plan(own, counts, tile_list, owners, half)
    asked = lax.all_to_all(request, "tile", split_axis=0, concat_axis=0, tiled=True)
    outgoing = pack(asked, emission)
    far = lax.all_to_all(outgoing, "tile", split_axis=0, concat_axis=0, tiled=True)
    crowded = jnp.any(asked[:, CAP] > 0)
    weights = after(step_weights[:, None], crowded)

    cuts = (6, 5, 5)
    others = me ^ CORE ^ (2 * jnp.arange(parts // 2, dtype=I32))
    offsets = [[c * half + sum(cuts[:i]) for i in range(len(cuts))] for c in range(2)]

    def given(c, i, wt, e_blocks, last):
        return tiles(
            after(others, last), others, table, wt, e_blocks, offsets[c][i], cuts[i], 1
        )[0]

    def kept(c, i, wt, e_blocks, last, core):
        masks = [m for lead in (1, 0) for m in order_masks(ORDERS[i], lead)]
        mine = me ^ jnp.array(masks, I32)
        places = jnp.array([m // 2 for m in masks], I32)
        return tiles(
            after(mine, last), places, table, wt, e_blocks, offsets[c][i], cuts[i], 2, core
        )

    def exchange(outs, step):
        return [(out[1], swap(out[0], order[step])) for out, order in zip(outs, ORDERS)]

    def halve(pairs, last):
        outs = []
        for mine, came in pairs:
            out = add_pairs([(after(mine, last), came)])
            last = out[1]
            outs.append(out)
        return outs, last

    def first_kernels(c, wt, e_blocks):
        last, cores = wt, []
        for i in range(3):
            last = given(c, i, wt, e_blocks, last)
            cores.append(swap(last, CORE))
        return cores, last

    def second_kernels(c, wt, e_blocks, cores, last):
        outs = []
        for i in range(3):
            outs.append(kept(c, i, wt, e_blocks, last, cores[i]))
            last = outs[i][1]
        return outs, last

    wt, e_blocks = prep(after(weights, outgoing), adjoint, emission)
    cores, last = first_kernels(0, wt, e_blocks)
    early, last = second_kernels(0, wt, e_blocks, cores, last)
    early = exchange(early, 0)
    wt, e_blocks = prep(after(weights, last), adjoint, emission, far)
    cores, last = [], wt
    for i in range(3):
        last = given(1, i, wt, e_blocks, last)
        cores.append(swap(last, CORE))
        if i == 0:
            early, last = halve(early, last)
            early = exchange(early, 1)
    late = []
    for i in range(3):
        if i == 2:
            early, last = halve(early, last)
            early = exchange(early, 2)
        late.append(kept(1, i, wt, e_blocks, last, cores[i]))
        last = late[i][1]
    late = exchange(late, 0)
    late, last = halve(late, last)
    late, last = halve(exchange(late, 1), last)
    late = exchange(late, 2)
    firsts = tuple(offsets[0] + offsets[1])

    def crowded_group(early, late):
        wt, e_blocks = prep(weights, adjoint, emission, far)
        cores, last = first_kernels(0, wt, e_blocks)
        again, last = second_kernels(0, wt, e_blocks, cores, last)
        for step in range(2):
            again, last = halve(exchange(again, step), last)
        return finish(me, counts, table, exchange(again, 2) + late, firsts)

    def usual(early, late):
        return finish(me, counts, table, early + late, firsts)

    return lax.cond(crowded, crowded_group, usual, early, late)[None]


def solution(mesh):
    in_specs = (P("tm", "tile"), P("tm", "tile"), P("tm"), P("tile", None), P("tile"))
    out_specs = P("tile", "tm", None, None)
    return jax.shard_map(body, mesh=mesh, in_specs=in_specs, out_specs=out_specs, check_vma=False)
```

```python
import functools

import jax
import jax.numpy as jnp
from jax import lax
from jax.experimental import pallas as pl
from jax.experimental.pallas import tpu as pltpu
from jax.sharding import PartitionSpec as P

BLK = 128
CAP = 4
GRP = 32
KA = 384
F32 = jnp.float32
BF16 = jnp.bfloat16
I32 = jnp.int32


def iota(shape, dim):
    return lax.broadcasted_iota(I32, shape, dim)


def in_hbm(a):
    return pltpu.with_memory_space_constraint(a, pltpu.HBM)


def plan_kernel(early, own_ref, count_ref, tiles_ref, request_ref, table_ref):
    slots = tiles_ref.shape[0]
    own = own_ref[0]
    r = tiles_ref[:, 0:1]
    c = tiles_ref[:, 1:2]
    k = iota((slots, 1), 0)
    src = c >> 7
    within = c & (BLK - 1)
    row = r & (BLK - 1)
    remote = (k < count_ref[0]) & (src != own)
    lane = iota((slots, BLK), 1)
    by_src = jnp.where((lane == src) & remote, 1.0, 0.0).astype(F32)
    by_block = jnp.where(lane == within, 1.0, 0.0).astype(F32)
    named = jnp.dot(by_src.T.astype(BF16), by_block.astype(BF16), preferred_element_type=F32)
    hit = jnp.where(named > 0.0, 1.0, 0.0).astype(F32)
    upper = jnp.where(iota((BLK, BLK), 0) <= iota((BLK, BLK), 1), 1.0, 0.0).astype(BF16)
    rank = jnp.dot(hit.astype(BF16), upper, preferred_element_type=F32) * hit
    slot_rank = jnp.sum(
        jnp.dot(by_src.astype(BF16), rank.astype(BF16), preferred_element_type=F32) * by_block,
        axis=1,
        keepdims=True,
    )
    slot_rank = jnp.clip(slot_rank.astype(I32) - 1, 0, CAP - 1)
    col = jnp.where(remote, BLK + src * CAP + slot_rank, within)

    jj = iota((slots, slots), 1)
    kk = iota((slots, slots), 0)
    same = (jj >> 5) == (kk >> 5)
    remote_f = jnp.broadcast_to(jnp.where(remote, 1.0, 0.0), (slots, BLK)).astype(BF16)
    ahead = jnp.where(same & (jj < kk), 1.0, 0.0).astype(BF16)
    ahead = jnp.dot(ahead, remote_f, preferred_element_type=F32)[:, 0:1].astype(I32)
    total = jnp.where(same, 1.0, 0.0).astype(BF16)
    total = jnp.dot(total, remote_f, preferred_element_type=F32)[:, 0:1].astype(I32)
    s = k & (GRP - 1)
    pos = jnp.where(remote, GRP - total + ahead, s - ahead)
    value = jnp.where(lane < GRP, row, jnp.where(lane < 2 * GRP, col, s))
    value = jnp.where((lane & (GRP - 1)) == pos, value, 0)
    value = jnp.where(lane < 3 * GRP, value, 0).astype(F32).astype(BF16)
    groups = slots // GRP
    pick = jnp.where((iota((groups, slots), 1) >> 5) == iota((groups, slots), 0), 1.0, 0.0)
    table_ref[...] = jnp.dot(pick.astype(BF16), value, preferred_element_type=F32).astype(I32)

    late = jnp.max(jnp.where(total > GRP - early, 1, 0), axis=0, keepdims=True)
    owners = request_ref.shape[0]
    hit8 = hit[0:owners, :]
    rank8 = rank[0:owners, :]
    lane8 = iota((owners, BLK), 1)
    request = jnp.where(lane8 == CAP, jnp.broadcast_to(late, (owners, BLK)), 0)
    for q in range(CAP):
        block = jnp.sum(
            jnp.where((rank8 == q + 1.0) & (hit8 > 0.0), lane8, 0), axis=1, keepdims=True
        )
        request = jnp.where(lane8 == q, block, request)
    request_ref[...] = request


def plan(own, counts, tile_list, owners, early):
    slots = tile_list.shape[0]
    smem = pl.BlockSpec(memory_space=pltpu.SMEM)
    vmem = pl.BlockSpec(memory_space=pltpu.VMEM)
    return pl.pallas_call(
        functools.partial(plan_kernel, early),
        in_specs=[smem, smem, vmem],
        out_specs=[vmem, vmem],
        out_shape=[
            jax.ShapeDtypeStruct((owners, BLK), I32),
            jax.ShapeDtypeStruct((slots // GRP, BLK), I32),
        ],
        compiler_params=pltpu.CompilerParams(vmem_limit_bytes=16 * 2**20),
        name="plan",
    )(own, counts, tile_list)


STEP = 16
DEPTH = 3


def prep_kernel(with_far, weights_ref, adj_ref, em_ref, *refs):
    if with_far:
        far_ref, refs = refs[0], refs[1:]
        refs, fsem = refs[:-1], refs[-1]
    wt_ref, e_ref, abuf, ebuf, wide, asem, esem = refs
    steps = adj_ref.shape[0]
    blocks = wt_ref.shape[0]
    chunks = blocks // STEP
    wide[...] = jnp.broadcast_to(weights_ref[...], wide.shape)

    def copies(j):
        slot = lax.rem(j, DEPTH)
        cols = pl.ds(pl.multiple_of(j * (STEP * BLK), STEP * BLK), STEP * BLK)
        return (
            pltpu.make_async_copy(adj_ref.at[:, cols], abuf.at[slot], asem.at[slot]),
            pltpu.make_async_copy(em_ref.at[:, cols], ebuf.at[slot], esem.at[slot]),
        )

    for j in range(DEPTH - 1):
        for copy in copies(j):
            copy.start()
    if with_far:
        rest = pl.ds(blocks, e_ref.shape[0] - blocks)
        far_copy = pltpu.make_async_copy(far_ref, e_ref.at[rest, pl.ds(0, steps)], fsem)
        far_copy.start()
    ones = jnp.where(iota((KA - steps, BLK), 0) < 2, 1.0, 0.0).astype(BF16)
    rows = iota((KA - steps, BLK), 0)

    def chunk(j, carry):
        slot = lax.rem(j, DEPTH)

        @pl.when(j + DEPTH - 1 < chunks)
        def _():
            for copy in copies(j + DEPTH - 1):
                copy.start()

        for copy in copies(j):
            copy.wait()
        for b in range(STEP):
            at = j * STEP + b
            w = (wide[...] * abuf[slot, :, b * BLK : (b + 1) * BLK].astype(F32)).astype(BF16)
            e = ebuf[slot, :, b * BLK : (b + 1) * BLK]
            sums = -jnp.sum(w.astype(F32) * e.astype(F32), axis=0, keepdims=True)
            high = sums.astype(BF16).astype(F32)
            low = sums - high
            tail = jnp.where(rows == 0, high, jnp.where(rows == 1, low, 0.0)).astype(BF16)
            wt_ref[at] = jnp.concatenate([w, tail], axis=0).T
            e_ref[at, 0:steps, :] = e
            e_ref[at, steps:KA, :] = ones
        return carry

    lax.fori_loop(0, chunks, chunk, 0)
    if with_far:
        for i in range(blocks, e_ref.shape[0]):
            e_ref[i, steps:KA, :] = ones
        far_copy.wait()


def prep(weights, adjoint, emission, far=None):
    steps, nodes = adjoint.shape
    blocks = nodes // BLK
    anyspace = pl.BlockSpec(memory_space=pl.ANY)
    vmem = pl.BlockSpec(memory_space=pltpu.VMEM)
    with_far = far is not None
    columns = blocks + (far.shape[0] if with_far else 0)
    wt, e_blocks = pl.pallas_call(
        functools.partial(prep_kernel, with_far),
        in_specs=[vmem] + [anyspace] * (3 if with_far else 2),
        out_specs=[vmem, vmem],
        out_shape=[
            pltpu.VMEM((blocks, BLK, KA), BF16),
            pltpu.VMEM((columns, KA, BLK), BF16),
        ],
        scratch_shapes=[
            pltpu.VMEM((DEPTH, steps, STEP * BLK), BF16),
            pltpu.VMEM((DEPTH, steps, STEP * BLK), BF16),
            pltpu.VMEM((steps, BLK), F32),
            pltpu.SemaphoreType.DMA((DEPTH,)),
            pltpu.SemaphoreType.DMA((DEPTH,)),
        ]
        + ([pltpu.SemaphoreType.DMA] if with_far else []),
        compiler_params=pltpu.CompilerParams(vmem_limit_bytes=14 * 2**20),
        name="prep",
    )(weights, in_hbm(adjoint), in_hbm(emission), *([in_hbm(far)] if with_far else []))
    return (
        pltpu.with_memory_space_constraint(wt, pltpu.VMEM),
        pltpu.with_memory_space_constraint(e_blocks, pltpu.VMEM),
    )


def pack_kernel(asked_ref, em_ref, out_ref, sems):
    count = out_ref.shape[0]

    def copy(i):
        block = asked_ref[i >> 2, i & (CAP - 1)] & (BLK - 1)
        cols = pl.ds(pl.multiple_of(block * BLK, BLK), BLK)
        return pltpu.make_async_copy(em_ref.at[:, cols], out_ref.at[i], sems.at[i])

    for i in range(count):
        copy(i).start()
    for i in range(count):
        copy(i).wait()


def pack(asked, emission):
    owners = asked.shape[0]
    return pl.pallas_call(
        pack_kernel,
        in_specs=[pl.BlockSpec(memory_space=pltpu.SMEM), pl.BlockSpec(memory_space=pl.ANY)],
        out_specs=pl.BlockSpec(memory_space=pltpu.VMEM),
        out_shape=jax.ShapeDtypeStruct((owners * CAP, emission.shape[0], BLK), BF16),
        scratch_shapes=[pltpu.SemaphoreType.DMA((owners * CAP,))],
        compiler_params=pltpu.CompilerParams(vmem_limit_bytes=8 * 2**20),
        name="pack",
    )(asked, in_hbm(emission))


def tiles_kernel(first, per, with_add, *refs):
    groups_ref, places_ref, table_ref, wt_ref, e_ref = refs[:5]
    outs = refs[6:] if with_add else refs[5:]
    last = e_ref.shape[0] - 1
    n = 0
    for out_ref in outs:
        for j in range(out_ref.shape[0] // per):
            g = groups_ref[n]
            for q in range(per):
                row = table_ref[g, first + q]
                col = jnp.minimum(table_ref[g, GRP + first + q], last)
                acc = jnp.dot(wt_ref[row], e_ref[col], preferred_element_type=F32)
                if with_add:
                    acc = acc + refs[5][places_ref[n] * per + q].astype(F32)
                out_ref[j * per + q] = acc.astype(BF16)
            n += 1


def tiles(groups, places, table, wt, e_blocks, first, per, outs, add=None):
    smem = pl.BlockSpec(memory_space=pltpu.SMEM)
    vmem = pl.BlockSpec(memory_space=pltpu.VMEM)
    count = groups.shape[0] * per
    with_add = add is not None
    return pl.pallas_call(
        functools.partial(tiles_kernel, first, per, with_add),
        in_specs=[smem, smem, smem, vmem, vmem] + ([vmem] if with_add else []),
        out_specs=[vmem] * outs,
        out_shape=[jax.ShapeDtypeStruct((count // outs, BLK, BLK), BF16)] * outs,
        compiler_params=pltpu.CompilerParams(vmem_limit_bytes=10 * 2**20),
        name="tiles",
    )(groups, places, table, wt, e_blocks, *([add] if with_add else []))


def add_kernel(n, *refs):
    for i in range(n):
        mine, came = refs[2 * i], refs[2 * i + 1]
        sent, kept = refs[2 * n + 2 * i], refs[2 * n + 2 * i + 1]
        half = sent.shape[0]

        def one(j, carry, mine=mine, came=came, sent=sent, kept=kept, half=half):
            sent[j] = (mine[j].astype(F32) + came[j].astype(F32)).astype(BF16)
            kept[j] = (mine[half + j].astype(F32) + came[half + j].astype(F32)).astype(BF16)
            return carry

        lax.fori_loop(0, half, one, 0, unroll=2)


def add_pairs(pairs):
    vmem = pl.BlockSpec(memory_space=pltpu.VMEM)
    shapes = []
    for mine, _ in pairs:
        shapes += [jax.ShapeDtypeStruct((mine.shape[0] // 2, BLK, BLK), BF16)] * 2
    flat = [a for pair in pairs for a in pair]
    return pl.pallas_call(
        functools.partial(add_kernel, len(pairs)),
        in_specs=[vmem] * len(flat),
        out_specs=[vmem] * len(shapes),
        out_shape=shapes,
        compiler_params=pltpu.CompilerParams(vmem_limit_bytes=20 * 2**20),
        name="add_pairs",
    )(*flat)


def finish_kernel(firsts, me_ref, count_ref, table_ref, *refs):
    me = me_ref[0]
    out_ref, stage, sem = refs[-3:]
    for i, first in enumerate(firsts):
        mine, came = refs[2 * i], refs[2 * i + 1]
        for j in range(mine.shape[0]):
            s = table_ref[me, 2 * GRP + first + j]
            live = jnp.where(me * GRP + s < count_ref[0], 1.0, 0.0).astype(F32)
            stage[first + j] = (mine[j].astype(F32) + came[j].astype(F32)) * live
            pltpu.make_async_copy(stage.at[first + j], out_ref.at[s], sem).start()
    pltpu.make_async_copy(stage, out_ref, sem).wait()


def finish(me, counts, table, pairs, firsts):
    smem = pl.BlockSpec(memory_space=pltpu.SMEM)
    vmem = pl.BlockSpec(memory_space=pltpu.VMEM)
    flat = [a for pair in pairs for a in pair]
    return pl.pallas_call(
        functools.partial(finish_kernel, firsts),
        in_specs=[smem, smem, smem] + [vmem] * len(flat),
        out_specs=pl.BlockSpec(memory_space=pltpu.HBM),
        out_shape=pltpu.HBM((GRP, BLK, BLK), F32),
        scratch_shapes=[pltpu.VMEM((GRP, BLK, BLK), F32), pltpu.SemaphoreType.DMA],
        compiler_params=pltpu.CompilerParams(vmem_limit_bytes=16 * 2**20),
        name="finish",
    )(me, counts, table, *flat)


CORE, ALONG_X, UP_Y, DOWN_Y = 1, 2, 4, 12
ORDERS = (
    (ALONG_X, UP_Y, DOWN_Y),
    (UP_Y, DOWN_Y, ALONG_X),
    (DOWN_Y, ALONG_X, UP_Y),
)


def swap(a, mask):
    n = lax.axis_size("tm")
    return lax.ppermute(a, "tm", [(i, i ^ mask) for i in range(n)])


def after(a, other):
    return lax.optimization_barrier((a, other))[0]


def order_masks(order, lead):
    first, second, third = order
    return [lead * first ^ s * second ^ t * third for s in (1, 0) for t in (1, 0)]


def body(adjoint, emission, step_weights, tile_list, counts):
    owners = lax.axis_size("tile")
    parts = lax.axis_size("tm")
    own = lax.axis_index("tile").astype(I32).reshape(1)
    me = lax.axis_index("tm").astype(I32).reshape(1)
    half = GRP // 2
    request, table = plan(own, counts, tile_list, owners, half)
    asked = lax.all_to_all(request, "tile", split_axis=0, concat_axis=0, tiled=True)
    outgoing = pack(asked, emission)
    far = lax.all_to_all(outgoing, "tile", split_axis=0, concat_axis=0, tiled=True)
    crowded = jnp.any(asked[:, CAP] > 0)
    weights = after(step_weights[:, None], crowded)

    cuts = (6, 5, 5)
    others = me ^ CORE ^ (2 * jnp.arange(parts // 2, dtype=I32))
    offsets = [[c * half + sum(cuts[:i]) for i in range(len(cuts))] for c in range(2)]

    def given(c, i, wt, e_blocks, last):
        return tiles(
            after(others, last), others, table, wt, e_blocks, offsets[c][i], cuts[i], 1
        )[0]

    def kept(c, i, wt, e_blocks, last, core):
        masks = [m for lead in (1, 0) for m in order_masks(ORDERS[i], lead)]
        mine = me ^ jnp.array(masks, I32)
        places = jnp.array([m // 2 for m in masks], I32)
        return tiles(
            after(mine, last), places, table, wt, e_blocks, offsets[c][i], cuts[i], 2, core
        )

    def exchange(outs, step):
        return [(out[1], swap(out[0], order[step])) for out, order in zip(outs, ORDERS)]

    def halve(pairs, last):
        outs = []
        for mine, came in pairs:
            out = add_pairs([(after(mine, last), came)])
            last = out[1]
            outs.append(out)
        return outs, last

    def first_kernels(c, wt, e_blocks):
        last, cores = wt, []
        for i in range(3):
            last = given(c, i, wt, e_blocks, last)
            cores.append(swap(last, CORE))
        return cores, last

    def second_kernels(c, wt, e_blocks, cores, last):
        outs = []
        for i in range(3):
            outs.append(kept(c, i, wt, e_blocks, last, cores[i]))
            last = outs[i][1]
        return outs, last

    wt, e_blocks = prep(after(weights, outgoing), adjoint, emission)
    cores, last = first_kernels(0, wt, e_blocks)
    early, last = second_kernels(0, wt, e_blocks, cores, last)
    early = exchange(early, 0)
    wt, e_blocks = prep(after(weights, last), adjoint, emission, far)
    cores, last = [], wt
    for i in range(3):
        last = given(1, i, wt, e_blocks, last)
        cores.append(swap(last, CORE))
        if i == 0:
            early, last = halve(early, last)
            early = exchange(early, 1)
    late = []
    for i in range(3):
        if i == 2:
            early, last = halve(early, last)
            early = exchange(early, 2)
        late.append(kept(1, i, wt, e_blocks, last, cores[i]))
        last = late[i][1]
    late = exchange(late, 0)
    late, last = halve(late, last)
    late, last = halve(exchange(late, 1), last)
    late = exchange(late, 2)
    firsts = tuple(offsets[0] + offsets[1])

    def crowded_group(state):
        wt, e_blocks = prep(after(weights, state[1]), adjoint, emission, far)
        cores, last = first_kernels(0, wt, e_blocks)
        again, last = second_kernels(0, wt, e_blocks, cores, last)
        for step in range(2):
            again, last = halve(exchange(again, step), last)
        out = finish(me, counts, table, exchange(again, 2) + late, firsts)
        return jnp.zeros((), bool), out

    out = finish(me, counts, table, early + late, firsts)
    return lax.while_loop(lambda state: state[0], crowded_group, (crowded, out))[1][None]


def solution(mesh):
    in_specs = (P("tm", "tile"), P("tm", "tile"), P("tm"), P("tile", None), P("tile"))
    out_specs = P("tile", "tm", None, None)
    return jax.shard_map(body, mesh=mesh, in_specs=in_specs, out_specs=out_specs, check_vma=False)
```

```python
import functools

import jax
import jax.numpy as jnp
from jax import lax
from jax.experimental import pallas as pl
from jax.experimental.pallas import tpu as pltpu
from jax.sharding import PartitionSpec as P

BLK = 128
CAP = 4
GRP = 32
KA = 384
F32 = jnp.float32
BF16 = jnp.bfloat16
I32 = jnp.int32


def iota(shape, dim):
    return lax.broadcasted_iota(I32, shape, dim)


def in_hbm(a):
    return pltpu.with_memory_space_constraint(a, pltpu.HBM)


def plan_kernel(early, own_ref, count_ref, tiles_ref, request_ref, table_ref):
    slots = tiles_ref.shape[0]
    own = own_ref[0]
    r = tiles_ref[:, 0:1]
    c = tiles_ref[:, 1:2]
    k = iota((slots, 1), 0)
    src = c >> 7
    within = c & (BLK - 1)
    row = r & (BLK - 1)
    remote = (k < count_ref[0]) & (src != own)
    lane = iota((slots, BLK), 1)
    by_src = jnp.where((lane == src) & remote, 1.0, 0.0).astype(F32)
    by_block = jnp.where(lane == within, 1.0, 0.0).astype(F32)
    named = jnp.dot(by_src.T.astype(BF16), by_block.astype(BF16), preferred_element_type=F32)
    hit = jnp.where(named > 0.0, 1.0, 0.0).astype(F32)
    upper = jnp.where(iota((BLK, BLK), 0) <= iota((BLK, BLK), 1), 1.0, 0.0).astype(BF16)
    rank = jnp.dot(hit.astype(BF16), upper, preferred_element_type=F32) * hit
    slot_rank = jnp.sum(
        jnp.dot(by_src.astype(BF16), rank.astype(BF16), preferred_element_type=F32) * by_block,
        axis=1,
        keepdims=True,
    )
    slot_rank = jnp.clip(slot_rank.astype(I32) - 1, 0, CAP - 1)
    col = jnp.where(remote, BLK + src * CAP + slot_rank, within)

    jj = iota((slots, slots), 1)
    kk = iota((slots, slots), 0)
    same = (jj >> 5) == (kk >> 5)
    remote_f = jnp.broadcast_to(jnp.where(remote, 1.0, 0.0), (slots, BLK)).astype(BF16)
    ahead = jnp.where(same & (jj < kk), 1.0, 0.0).astype(BF16)
    ahead = jnp.dot(ahead, remote_f, preferred_element_type=F32)[:, 0:1].astype(I32)
    total = jnp.where(same, 1.0, 0.0).astype(BF16)
    total = jnp.dot(total, remote_f, preferred_element_type=F32)[:, 0:1].astype(I32)
    s = k & (GRP - 1)
    pos = jnp.where(remote, GRP - total + ahead, s - ahead)
    value = jnp.where(lane < GRP, row, jnp.where(lane < 2 * GRP, col, s))
    value = jnp.where((lane & (GRP - 1)) == pos, value, 0)
    value = jnp.where(lane < 3 * GRP, value, 0).astype(F32).astype(BF16)
    groups = slots // GRP
    pick = jnp.where((iota((groups, slots), 1) >> 5) == iota((groups, slots), 0), 1.0, 0.0)
    table_ref[...] = jnp.dot(pick.astype(BF16), value, preferred_element_type=F32).astype(I32)

    late = jnp.max(jnp.where(total > GRP - early, 1, 0), axis=0, keepdims=True)
    owners = request_ref.shape[0]
    hit8 = hit[0:owners, :]
    rank8 = rank[0:owners, :]
    lane8 = iota((owners, BLK), 1)
    request = jnp.where(lane8 == CAP, jnp.broadcast_to(late, (owners, BLK)), 0)
    for q in range(CAP):
        block = jnp.sum(
            jnp.where((rank8 == q + 1.0) & (hit8 > 0.0), lane8, 0), axis=1, keepdims=True
        )
        request = jnp.where(lane8 == q, block, request)
    request_ref[...] = request


def plan(own, counts, tile_list, owners, early):
    slots = tile_list.shape[0]
    smem = pl.BlockSpec(memory_space=pltpu.SMEM)
    vmem = pl.BlockSpec(memory_space=pltpu.VMEM)
    return pl.pallas_call(
        functools.partial(plan_kernel, early),
        in_specs=[smem, smem, vmem],
        out_specs=[vmem, vmem],
        out_shape=[
            jax.ShapeDtypeStruct((owners, BLK), I32),
            jax.ShapeDtypeStruct((slots // GRP, BLK), I32),
        ],
        compiler_params=pltpu.CompilerParams(vmem_limit_bytes=16 * 2**20),
        name="plan",
    )(own, counts, tile_list)


STEP = 16
DEPTH = 3


def prep_kernel(with_far, weights_ref, adj_ref, em_ref, *refs):
    if with_far:
        far_ref, refs = refs[0], refs[1:]
        refs, fsem = refs[:-1], refs[-1]
    wt_ref, e_ref, abuf, ebuf, wide, asem, esem = refs
    steps = adj_ref.shape[0]
    blocks = wt_ref.shape[0]
    chunks = blocks // STEP
    wide[...] = jnp.broadcast_to(weights_ref[...], wide.shape)

    def copies(j):
        slot = lax.rem(j, DEPTH)
        cols = pl.ds(pl.multiple_of(j * (STEP * BLK), STEP * BLK), STEP * BLK)
        return (
            pltpu.make_async_copy(adj_ref.at[:, cols], abuf.at[slot], asem.at[slot]),
            pltpu.make_async_copy(em_ref.at[:, cols], ebuf.at[slot], esem.at[slot]),
        )

    for j in range(DEPTH - 1):
        for copy in copies(j):
            copy.start()
    if with_far:
        rest = pl.ds(blocks, e_ref.shape[0] - blocks)
        far_copy = pltpu.make_async_copy(far_ref, e_ref.at[rest, pl.ds(0, steps)], fsem)
        far_copy.start()
    ones = jnp.where(iota((KA - steps, BLK), 0) < 2, 1.0, 0.0).astype(BF16)
    rows = iota((KA - steps, BLK), 0)

    def chunk(j, carry):
        slot = lax.rem(j, DEPTH)

        @pl.when(j + DEPTH - 1 < chunks)
        def _():
            for copy in copies(j + DEPTH - 1):
                copy.start()

        for copy in copies(j):
            copy.wait()
        for b in range(STEP):
            at = j * STEP + b
            w = (wide[...] * abuf[slot, :, b * BLK : (b + 1) * BLK].astype(F32)).astype(BF16)
            e = ebuf[slot, :, b * BLK : (b + 1) * BLK]
            sums = -jnp.sum(w.astype(F32) * e.astype(F32), axis=0, keepdims=True)
            high = sums.astype(BF16).astype(F32)
            low = sums - high
            tail = jnp.where(rows == 0, high, jnp.where(rows == 1, low, 0.0)).astype(BF16)
            wt_ref[at] = jnp.concatenate([w, tail], axis=0).T
            e_ref[at, 0:steps, :] = e
            e_ref[at, steps:KA, :] = ones
        return carry

    lax.fori_loop(0, chunks, chunk, 0)
    if with_far:
        for i in range(blocks, e_ref.shape[0]):
            e_ref[i, steps:KA, :] = ones
        far_copy.wait()


def prep(weights, adjoint, emission, far=None):
    steps, nodes = adjoint.shape
    blocks = nodes // BLK
    anyspace = pl.BlockSpec(memory_space=pl.ANY)
    vmem = pl.BlockSpec(memory_space=pltpu.VMEM)
    with_far = far is not None
    columns = blocks + (far.shape[0] if with_far else 0)
    wt, e_blocks = pl.pallas_call(
        functools.partial(prep_kernel, with_far),
        in_specs=[vmem] + [anyspace] * (3 if with_far else 2),
        out_specs=[vmem, vmem],
        out_shape=[
            pltpu.VMEM((blocks, BLK, KA), BF16),
            pltpu.VMEM((columns, KA, BLK), BF16),
        ],
        scratch_shapes=[
            pltpu.VMEM((DEPTH, steps, STEP * BLK), BF16),
            pltpu.VMEM((DEPTH, steps, STEP * BLK), BF16),
            pltpu.VMEM((steps, BLK), F32),
            pltpu.SemaphoreType.DMA((DEPTH,)),
            pltpu.SemaphoreType.DMA((DEPTH,)),
        ]
        + ([pltpu.SemaphoreType.DMA] if with_far else []),
        compiler_params=pltpu.CompilerParams(vmem_limit_bytes=14 * 2**20),
        name="prep",
    )(weights, in_hbm(adjoint), in_hbm(emission), *([in_hbm(far)] if with_far else []))
    return (
        pltpu.with_memory_space_constraint(wt, pltpu.VMEM),
        pltpu.with_memory_space_constraint(e_blocks, pltpu.VMEM),
    )


def pack_kernel(asked_ref, em_ref, out_ref, sems):
    count = out_ref.shape[0]

    def copy(i):
        block = asked_ref[i >> 2, i & (CAP - 1)] & (BLK - 1)
        cols = pl.ds(pl.multiple_of(block * BLK, BLK), BLK)
        return pltpu.make_async_copy(em_ref.at[:, cols], out_ref.at[i], sems.at[i])

    for i in range(count):
        copy(i).start()
    for i in range(count):
        copy(i).wait()


def pack(asked, emission):
    owners = asked.shape[0]
    return pl.pallas_call(
        pack_kernel,
        in_specs=[pl.BlockSpec(memory_space=pltpu.SMEM), pl.BlockSpec(memory_space=pl.ANY)],
        out_specs=pl.BlockSpec(memory_space=pltpu.VMEM),
        out_shape=jax.ShapeDtypeStruct((owners * CAP, emission.shape[0], BLK), BF16),
        scratch_shapes=[pltpu.SemaphoreType.DMA((owners * CAP,))],
        compiler_params=pltpu.CompilerParams(vmem_limit_bytes=8 * 2**20),
        name="pack",
    )(asked, in_hbm(emission))


def tiles_kernel(first, per, with_add, rolled, *refs):
    groups_ref, places_ref, table_ref, wt_ref, e_ref = refs[:5]
    outs = refs[6:] if with_add else refs[5:]
    last = e_ref.shape[0] - 1
    n = 0
    for out_ref in outs:
        size = out_ref.shape[0] // per

        def one(j, carry, out_ref=out_ref, n=n):
            g = groups_ref[n + j]
            for q in range(per):
                row = table_ref[g, first + q]
                col = jnp.minimum(table_ref[g, GRP + first + q], last)
                acc = jnp.dot(wt_ref[row], e_ref[col], preferred_element_type=F32)
                if with_add:
                    acc = acc + refs[5][places_ref[n + j] * per + q].astype(F32)
                out_ref[j * per + q] = acc.astype(BF16)
            return carry

        if rolled:
            lax.fori_loop(0, size, one, 0)
        else:
            for j in range(size):
                one(j, 0)
        n += size


def tiles(groups, places, table, wt, e_blocks, first, per, outs, rolled, add=None):
    smem = pl.BlockSpec(memory_space=pltpu.SMEM)
    vmem = pl.BlockSpec(memory_space=pltpu.VMEM)
    count = groups.shape[0] * per
    with_add = add is not None
    return pl.pallas_call(
        functools.partial(tiles_kernel, first, per, with_add, rolled),
        in_specs=[smem, smem, smem, vmem, vmem] + ([vmem] if with_add else []),
        out_specs=[vmem] * outs,
        out_shape=[jax.ShapeDtypeStruct((count // outs, BLK, BLK), BF16)] * outs,
        compiler_params=pltpu.CompilerParams(vmem_limit_bytes=10 * 2**20),
        name="tiles",
    )(groups, places, table, wt, e_blocks, *([add] if with_add else []))


def add_kernel(n, *refs):
    for i in range(n):
        mine, came = refs[2 * i], refs[2 * i + 1]
        sent, kept = refs[2 * n + 2 * i], refs[2 * n + 2 * i + 1]
        half = sent.shape[0]

        def one(j, carry, mine=mine, came=came, sent=sent, kept=kept, half=half):
            sent[j] = (mine[j].astype(F32) + came[j].astype(F32)).astype(BF16)
            kept[j] = (mine[half + j].astype(F32) + came[half + j].astype(F32)).astype(BF16)
            return carry

        lax.fori_loop(0, half, one, 0, unroll=2)


def add_pairs(pairs):
    vmem = pl.BlockSpec(memory_space=pltpu.VMEM)
    shapes = []
    for mine, _ in pairs:
        shapes += [jax.ShapeDtypeStruct((mine.shape[0] // 2, BLK, BLK), BF16)] * 2
    flat = [a for pair in pairs for a in pair]
    return pl.pallas_call(
        functools.partial(add_kernel, len(pairs)),
        in_specs=[vmem] * len(flat),
        out_specs=[vmem] * len(shapes),
        out_shape=shapes,
        compiler_params=pltpu.CompilerParams(vmem_limit_bytes=20 * 2**20),
        name="add_pairs",
    )(*flat)


def finish_kernel(firsts, me_ref, count_ref, table_ref, *refs):
    me = me_ref[0]
    out_ref, done_ref, stage, sem = refs[-4:]
    n = 0
    for i, first in enumerate(firsts):
        mine, came = refs[2 * i], refs[2 * i + 1]
        for j in range(mine.shape[0]):
            s = table_ref[me, 2 * GRP + first + j]
            live = jnp.where(me * GRP + s < count_ref[0], 1.0, 0.0).astype(F32)
            stage[n] = (mine[j].astype(F32) + came[j].astype(F32)) * live
            pltpu.make_async_copy(stage.at[n], out_ref.at[s], sem).start()
            n += 1
    done_ref[...] = jnp.zeros_like(done_ref)
    pltpu.make_async_copy(stage, out_ref.at[pl.ds(0, n)], sem).wait()


def finish(me, counts, table, pairs, firsts, out=None):
    smem = pl.BlockSpec(memory_space=pltpu.SMEM)
    vmem = pl.BlockSpec(memory_space=pltpu.VMEM)
    hbm = pl.BlockSpec(memory_space=pltpu.HBM)
    flat = [a for pair in pairs for a in pair]
    n = sum(mine.shape[0] for mine, _ in pairs)
    given = out is not None
    return pl.pallas_call(
        functools.partial(finish_kernel, firsts),
        in_specs=[smem, smem, smem] + [vmem] * len(flat)
        + ([hbm, pl.BlockSpec(memory_space=pl.ANY)] if given else []),
        out_specs=[hbm, vmem],
        out_shape=[pltpu.HBM((GRP, BLK, BLK), F32), jax.ShapeDtypeStruct((8, BLK), F32)],
        input_output_aliases={3 + len(flat): 0} if given else {},
        scratch_shapes=[pltpu.VMEM((n, BLK, BLK), F32), pltpu.SemaphoreType.DMA],
        compiler_params=pltpu.CompilerParams(vmem_limit_bytes=16 * 2**20),
        name="finish",
    )(me, counts, table, *flat, *(out if given else ()))


CORE, ALONG_X, UP_Y, DOWN_Y = 1, 2, 4, 12
ORDERS = (
    (ALONG_X, UP_Y, DOWN_Y),
    (UP_Y, DOWN_Y, ALONG_X),
    (DOWN_Y, ALONG_X, UP_Y),
)


def swap(a, mask):
    n = lax.axis_size("tm")
    return lax.ppermute(a, "tm", [(i, i ^ mask) for i in range(n)])


def after(a, other):
    return lax.optimization_barrier((a, other))[0]


def order_masks(order, lead):
    first, second, third = order
    return [lead * first ^ s * second ^ t * third for s in (1, 0) for t in (1, 0)]


def body(adjoint, emission, step_weights, tile_list, counts):
    owners = lax.axis_size("tile")
    parts = lax.axis_size("tm")
    own = lax.axis_index("tile").astype(I32).reshape(1)
    me = lax.axis_index("tm").astype(I32).reshape(1)
    cuts = ((6, 6, 6), (5, 5, 4))
    split = sum(cuts[0])
    request, table = plan(own, counts, tile_list, owners, split)
    asked = lax.all_to_all(request, "tile", split_axis=0, concat_axis=0, tiled=True)
    outgoing = pack(asked, emission)
    far = lax.all_to_all(outgoing, "tile", split_axis=0, concat_axis=0, tiled=True)
    crowded = jnp.any(asked[:, CAP] > 0)
    weights = step_weights[:, None]

    others = me ^ CORE ^ (2 * jnp.arange(parts // 2, dtype=I32))
    offsets = [[c * split + sum(cuts[c][:i]) for i in range(3)] for c in range(2)]

    def given(c, i, wt, e_blocks, last, rolled=False):
        return tiles(
            after(others, last), others, table, wt, e_blocks, offsets[c][i], cuts[c][i], 1, rolled
        )[0]

    def kept(c, i, wt, e_blocks, last, core, rolled=False):
        masks = [m for lead in (1, 0) for m in order_masks(ORDERS[i], lead)]
        mine = me ^ jnp.array(masks, I32)
        places = jnp.array([m // 2 for m in masks], I32)
        return tiles(
            after(mine, last), places, table, wt, e_blocks, offsets[c][i], cuts[c][i], 2, rolled, core
        )

    def exchange(outs, step):
        return [(out[1], swap(out[0], order[step])) for out, order in zip(outs, ORDERS)]

    def halve(pairs, last):
        outs = []
        for mine, came in pairs:
            out = add_pairs([(after(mine, last), came)])
            last = out[1]
            outs.append(out)
        return outs, last

    wt, e_blocks = prep(after(weights, outgoing), adjoint, emission)
    last, cores, early = wt, [], []
    for i in range(3):
        last = given(0, i, wt, e_blocks, last)
        cores.append(swap(last, CORE))
    for i in range(3):
        early.append(kept(0, i, wt, e_blocks, last, cores[i]))
        last = early[i][1]
    early = exchange(early, 0)
    wt, e_blocks = prep(after(weights, last), adjoint, emission, far)
    last, cores, late = wt, [], []
    for i in range(3):
        last = given(1, i, wt, e_blocks, last)
        cores.append(swap(last, CORE))
        if i == 0:
            early, last = halve(early, last)
            early = exchange(early, 1)
    for i in range(3):
        if i == 2:
            early, last = halve(early, last)
            early = exchange(early, 2)
        late.append(kept(1, i, wt, e_blocks, last, cores[i]))
        last = late[i][1]
    late = exchange(late, 0)
    late, last = halve(late, (last, crowded))
    out, done = finish(after(me, last), counts, table, early, tuple(offsets[0]))
    late, last = halve(exchange(late, 1), done)
    late = exchange(late, 2)
    out, _ = finish(me, counts, table, late, tuple(offsets[1]), (out, done))

    def crowded_group(state):
        out = state[1]
        wt, e_blocks = prep(after(weights, out), adjoint, emission, far)
        last, cores, again = wt, [], []
        for i in range(3):
            last = given(0, i, wt, e_blocks, last, True)
            cores.append(swap(last, CORE))
        for i in range(3):
            again.append(kept(0, i, wt, e_blocks, last, cores[i], True))
            last = again[i][1]
        for step in range(2):
            again, last = halve(exchange(again, step), last)
        out, _ = finish(me, counts, table, exchange(again, 2), tuple(offsets[0]), (out, counts))
        return jnp.zeros((), bool), out

    return lax.while_loop(lambda state: state[0], crowded_group, (crowded, out))[1][None]


def solution(mesh):
    in_specs = (P("tm", "tile"), P("tm", "tile"), P("tm"), P("tile", None), P("tile"))
    out_specs = P("tile", "tm", None, None)
    return jax.shard_map(body, mesh=mesh, in_specs=in_specs, out_specs=out_specs, check_vma=False)
```

```python
import functools

import jax
import jax.numpy as jnp
from jax import lax
from jax.experimental import pallas as pl
from jax.experimental.pallas import tpu as pltpu
from jax.sharding import PartitionSpec as P

BLK = 128
CAP = 4
GRP = 32
KA = 384
F32 = jnp.float32
BF16 = jnp.bfloat16
I32 = jnp.int32


def iota(shape, dim):
    return lax.broadcasted_iota(I32, shape, dim)


def in_hbm(a):
    return pltpu.with_memory_space_constraint(a, pltpu.HBM)


def plan_kernel(early, own_ref, count_ref, tiles_ref, request_ref, table_ref):
    slots = tiles_ref.shape[0]
    own = own_ref[0]
    r = tiles_ref[:, 0:1]
    c = tiles_ref[:, 1:2]
    k = iota((slots, 1), 0)
    src = c >> 7
    within = c & (BLK - 1)
    row = r & (BLK - 1)
    remote = (k < count_ref[0]) & (src != own)
    lane = iota((slots, BLK), 1)
    by_src = jnp.where((lane == src) & remote, 1.0, 0.0).astype(F32)
    by_block = jnp.where(lane == within, 1.0, 0.0).astype(F32)
    named = jnp.dot(by_src.T.astype(BF16), by_block.astype(BF16), preferred_element_type=F32)
    hit = jnp.where(named > 0.0, 1.0, 0.0).astype(F32)
    upper = jnp.where(iota((BLK, BLK), 0) <= iota((BLK, BLK), 1), 1.0, 0.0).astype(BF16)
    rank = jnp.dot(hit.astype(BF16), upper, preferred_element_type=F32) * hit
    slot_rank = jnp.sum(
        jnp.dot(by_src.astype(BF16), rank.astype(BF16), preferred_element_type=F32) * by_block,
        axis=1,
        keepdims=True,
    )
    slot_rank = jnp.clip(slot_rank.astype(I32) - 1, 0, CAP - 1)
    col = jnp.where(remote, BLK + src * CAP + slot_rank, within)

    jj = iota((slots, slots), 1)
    kk = iota((slots, slots), 0)
    same = (jj >> 5) == (kk >> 5)
    remote_f = jnp.broadcast_to(jnp.where(remote, 1.0, 0.0), (slots, BLK)).astype(BF16)
    ahead = jnp.where(same & (jj < kk), 1.0, 0.0).astype(BF16)
    ahead = jnp.dot(ahead, remote_f, preferred_element_type=F32)[:, 0:1].astype(I32)
    total = jnp.where(same, 1.0, 0.0).astype(BF16)
    total = jnp.dot(total, remote_f, preferred_element_type=F32)[:, 0:1].astype(I32)
    s = k & (GRP - 1)
    pos = jnp.where(remote, GRP - total + ahead, s - ahead)
    value = jnp.where(lane < GRP, row, jnp.where(lane < 2 * GRP, col, s))
    value = jnp.where((lane & (GRP - 1)) == pos, value, 0)
    value = jnp.where(lane < 3 * GRP, value, 0).astype(F32).astype(BF16)
    groups = slots // GRP
    pick = jnp.where((iota((groups, slots), 1) >> 5) == iota((groups, slots), 0), 1.0, 0.0)
    table_ref[...] = jnp.dot(pick.astype(BF16), value, preferred_element_type=F32).astype(I32)

    late = jnp.max(jnp.where(total > GRP - early, 1, 0), axis=0, keepdims=True)
    owners = request_ref.shape[0]
    hit8 = hit[0:owners, :]
    rank8 = rank[0:owners, :]
    lane8 = iota((owners, BLK), 1)
    request = jnp.where(lane8 == CAP, jnp.broadcast_to(late, (owners, BLK)), 0)
    for q in range(CAP):
        block = jnp.sum(
            jnp.where((rank8 == q + 1.0) & (hit8 > 0.0), lane8, 0), axis=1, keepdims=True
        )
        request = jnp.where(lane8 == q, block, request)
    request_ref[...] = request


def plan(own, counts, tile_list, owners, early):
    slots = tile_list.shape[0]
    smem = pl.BlockSpec(memory_space=pltpu.SMEM)
    vmem = pl.BlockSpec(memory_space=pltpu.VMEM)
    return pl.pallas_call(
        functools.partial(plan_kernel, early),
        in_specs=[smem, smem, vmem],
        out_specs=[vmem, vmem],
        out_shape=[
            jax.ShapeDtypeStruct((owners, BLK), I32),
            jax.ShapeDtypeStruct((slots // GRP, BLK), I32),
        ],
        compiler_params=pltpu.CompilerParams(vmem_limit_bytes=16 * 2**20),
        name="plan",
    )(own, counts, tile_list)


STEP = 16
DEPTH = 3


def prep_kernel(with_far, weights_ref, adj_ref, em_ref, *refs):
    if with_far:
        far_ref, refs = refs[0], refs[1:]
        refs, fsem = refs[:-1], refs[-1]
    wt_ref, e_ref, abuf, ebuf, wide, asem, esem = refs
    steps = adj_ref.shape[0]
    blocks = wt_ref.shape[0]
    chunks = blocks // STEP
    wide[...] = jnp.broadcast_to(weights_ref[...], wide.shape)

    def copies(j):
        slot = lax.rem(j, DEPTH)
        cols = pl.ds(pl.multiple_of(j * (STEP * BLK), STEP * BLK), STEP * BLK)
        return (
            pltpu.make_async_copy(adj_ref.at[:, cols], abuf.at[slot], asem.at[slot]),
            pltpu.make_async_copy(em_ref.at[:, cols], ebuf.at[slot], esem.at[slot]),
        )

    for j in range(DEPTH - 1):
        for copy in copies(j):
            copy.start()
    if with_far:
        rest = pl.ds(blocks, e_ref.shape[0] - blocks)
        far_copy = pltpu.make_async_copy(far_ref, e_ref.at[rest, pl.ds(0, steps)], fsem)
        far_copy.start()
    ones = jnp.where(iota((KA - steps, BLK), 0) < 2, 1.0, 0.0).astype(BF16)
    rows = iota((KA - steps, BLK), 0)

    def chunk(j, carry):
        slot = lax.rem(j, DEPTH)

        @pl.when(j + DEPTH - 1 < chunks)
        def _():
            for copy in copies(j + DEPTH - 1):
                copy.start()

        for copy in copies(j):
            copy.wait()
        for b in range(STEP):
            at = j * STEP + b
            w = (wide[...] * abuf[slot, :, b * BLK : (b + 1) * BLK].astype(F32)).astype(BF16)
            e = ebuf[slot, :, b * BLK : (b + 1) * BLK]
            sums = -jnp.sum(w.astype(F32) * e.astype(F32), axis=0, keepdims=True)
            high = sums.astype(BF16).astype(F32)
            low = sums - high
            tail = jnp.where(rows == 0, high, jnp.where(rows == 1, low, 0.0)).astype(BF16)
            wt_ref[at] = jnp.concatenate([w, tail], axis=0).T
            e_ref[at, 0:steps, :] = e
            e_ref[at, steps:KA, :] = ones
        return carry

    lax.fori_loop(0, chunks, chunk, 0)
    if with_far:
        for i in range(blocks, e_ref.shape[0]):
            e_ref[i, steps:KA, :] = ones
        far_copy.wait()


def prep(weights, adjoint, emission, far=None):
    steps, nodes = adjoint.shape
    blocks = nodes // BLK
    anyspace = pl.BlockSpec(memory_space=pl.ANY)
    vmem = pl.BlockSpec(memory_space=pltpu.VMEM)
    with_far = far is not None
    columns = blocks + (far.shape[0] if with_far else 0)
    wt, e_blocks = pl.pallas_call(
        functools.partial(prep_kernel, with_far),
        in_specs=[vmem] + [anyspace] * (3 if with_far else 2),
        out_specs=[vmem, vmem],
        out_shape=[
            pltpu.VMEM((blocks, BLK, KA), BF16),
            pltpu.VMEM((columns, KA, BLK), BF16),
        ],
        scratch_shapes=[
            pltpu.VMEM((DEPTH, steps, STEP * BLK), BF16),
            pltpu.VMEM((DEPTH, steps, STEP * BLK), BF16),
            pltpu.VMEM((steps, BLK), F32),
            pltpu.SemaphoreType.DMA((DEPTH,)),
            pltpu.SemaphoreType.DMA((DEPTH,)),
        ]
        + ([pltpu.SemaphoreType.DMA] if with_far else []),
        compiler_params=pltpu.CompilerParams(vmem_limit_bytes=14 * 2**20),
        name="prep",
    )(weights, in_hbm(adjoint), in_hbm(emission), *([in_hbm(far)] if with_far else []))
    return (
        pltpu.with_memory_space_constraint(wt, pltpu.VMEM),
        pltpu.with_memory_space_constraint(e_blocks, pltpu.VMEM),
    )


def pack_kernel(asked_ref, em_ref, out_ref, sems):
    count = out_ref.shape[0]

    def copy(i):
        block = asked_ref[i >> 2, i & (CAP - 1)] & (BLK - 1)
        cols = pl.ds(pl.multiple_of(block * BLK, BLK), BLK)
        return pltpu.make_async_copy(em_ref.at[:, cols], out_ref.at[i], sems.at[i])

    for i in range(count):
        copy(i).start()
    for i in range(count):
        copy(i).wait()


def pack(asked, emission):
    owners = asked.shape[0]
    return pl.pallas_call(
        pack_kernel,
        in_specs=[pl.BlockSpec(memory_space=pltpu.SMEM), pl.BlockSpec(memory_space=pl.ANY)],
        out_specs=pl.BlockSpec(memory_space=pltpu.VMEM),
        out_shape=jax.ShapeDtypeStruct((owners * CAP, emission.shape[0], BLK), BF16),
        scratch_shapes=[pltpu.SemaphoreType.DMA((owners * CAP,))],
        compiler_params=pltpu.CompilerParams(vmem_limit_bytes=8 * 2**20),
        name="pack",
    )(asked, in_hbm(emission))


def tiles_kernel(first, per, with_add, rolled, *refs):
    groups_ref, places_ref, table_ref, wt_ref, e_ref = refs[:5]
    outs = refs[6:] if with_add else refs[5:]
    last = e_ref.shape[0] - 1
    n = 0
    for out_ref in outs:
        size = out_ref.shape[0] // per

        def one(j, carry, out_ref=out_ref, n=n):
            g = groups_ref[n + j]
            for q in range(per):
                row = table_ref[g, first + q]
                col = jnp.minimum(table_ref[g, GRP + first + q], last)
                acc = jnp.dot(wt_ref[row], e_ref[col], preferred_element_type=F32)
                if with_add:
                    acc = acc + refs[5][places_ref[n + j] * per + q].astype(F32)
                out_ref[j * per + q] = acc.astype(BF16)
            return carry

        if rolled:
            lax.fori_loop(0, size, one, 0)
        else:
            for j in range(size):
                one(j, 0)
        n += size


def tiles(groups, places, table, wt, e_blocks, first, per, outs, rolled, add=None):
    smem = pl.BlockSpec(memory_space=pltpu.SMEM)
    vmem = pl.BlockSpec(memory_space=pltpu.VMEM)
    count = groups.shape[0] * per
    with_add = add is not None
    return pl.pallas_call(
        functools.partial(tiles_kernel, first, per, with_add, rolled),
        in_specs=[smem, smem, smem, vmem, vmem] + ([vmem] if with_add else []),
        out_specs=[vmem] * outs,
        out_shape=[jax.ShapeDtypeStruct((count // outs, BLK, BLK), BF16)] * outs,
        compiler_params=pltpu.CompilerParams(vmem_limit_bytes=10 * 2**20),
        name="tiles",
    )(groups, places, table, wt, e_blocks, *([add] if with_add else []))


def add_kernel(n, *refs):
    for i in range(n):
        mine, came = refs[2 * i], refs[2 * i + 1]
        sent, kept = refs[2 * n + 2 * i], refs[2 * n + 2 * i + 1]
        half = sent.shape[0]

        def one(j, carry, mine=mine, came=came, sent=sent, kept=kept, half=half):
            sent[j] = (mine[j].astype(F32) + came[j].astype(F32)).astype(BF16)
            kept[j] = (mine[half + j].astype(F32) + came[half + j].astype(F32)).astype(BF16)
            return carry

        lax.fori_loop(0, half, one, 0, unroll=2)


def add_pairs(pairs):
    vmem = pl.BlockSpec(memory_space=pltpu.VMEM)
    shapes = []
    for mine, _ in pairs:
        shapes += [jax.ShapeDtypeStruct((mine.shape[0] // 2, BLK, BLK), BF16)] * 2
    flat = [a for pair in pairs for a in pair]
    return pl.pallas_call(
        functools.partial(add_kernel, len(pairs)),
        in_specs=[vmem] * len(flat),
        out_specs=[vmem] * len(shapes),
        out_shape=shapes,
        compiler_params=pltpu.CompilerParams(vmem_limit_bytes=20 * 2**20),
        name="add_pairs",
    )(*flat)


def finish_kernel(firsts, me_ref, count_ref, table_ref, *refs):
    me = me_ref[0]
    out_ref, done_ref, stage, sem = refs[-4:]
    n = 0
    for i, first in enumerate(firsts):
        mine, came = refs[2 * i], refs[2 * i + 1]
        for j in range(mine.shape[0]):
            s = table_ref[me, 2 * GRP + first + j]
            live = jnp.where(me * GRP + s < count_ref[0], 1.0, 0.0).astype(F32)
            stage[n] = (mine[j].astype(F32) + came[j].astype(F32)) * live
            pltpu.make_async_copy(stage.at[n], out_ref.at[s], sem).start()
            n += 1
    done_ref[...] = jnp.zeros_like(done_ref)
    pltpu.make_async_copy(stage, out_ref.at[pl.ds(0, n)], sem).wait()


def finish(me, counts, table, pairs, firsts, out=None):
    smem = pl.BlockSpec(memory_space=pltpu.SMEM)
    vmem = pl.BlockSpec(memory_space=pltpu.VMEM)
    hbm = pl.BlockSpec(memory_space=pltpu.HBM)
    flat = [a for pair in pairs for a in pair]
    n = sum(mine.shape[0] for mine, _ in pairs)
    given = out is not None
    return pl.pallas_call(
        functools.partial(finish_kernel, firsts),
        in_specs=[smem, smem, smem] + [vmem] * len(flat)
        + ([hbm, pl.BlockSpec(memory_space=pl.ANY)] if given else []),
        out_specs=[hbm, vmem],
        out_shape=[pltpu.HBM((GRP, BLK, BLK), F32), jax.ShapeDtypeStruct((8, BLK), F32)],
        input_output_aliases={3 + len(flat): 0} if given else {},
        scratch_shapes=[pltpu.VMEM((n, BLK, BLK), F32), pltpu.SemaphoreType.DMA],
        compiler_params=pltpu.CompilerParams(vmem_limit_bytes=16 * 2**20),
        name="finish",
    )(me, counts, table, *flat, *(out if given else ()))


CORE, ALONG_X, UP_Y, DOWN_Y = 1, 2, 4, 12
ORDERS = (
    (ALONG_X, UP_Y, DOWN_Y),
    (UP_Y, DOWN_Y, ALONG_X),
    (DOWN_Y, ALONG_X, UP_Y),
)


def swap(a, mask):
    n = lax.axis_size("tm")
    return lax.ppermute(a, "tm", [(i, i ^ mask) for i in range(n)])


def after(a, other):
    return lax.optimization_barrier((a, other))[0]


def order_masks(order, lead):
    first, second, third = order
    return [lead * first ^ s * second ^ t * third for s in (1, 0) for t in (1, 0)]


def body(adjoint, emission, step_weights, tile_list, counts):
    owners = lax.axis_size("tile")
    parts = lax.axis_size("tm")
    own = lax.axis_index("tile").astype(I32).reshape(1)
    me = lax.axis_index("tm").astype(I32).reshape(1)
    cuts = ((6, 6, 6), (5, 5, 4))
    split = sum(cuts[0])
    request, table = plan(own, counts, tile_list, owners, split)
    asked = lax.all_to_all(request, "tile", split_axis=0, concat_axis=0, tiled=True)
    outgoing = pack(asked, emission)
    far = lax.all_to_all(outgoing, "tile", split_axis=0, concat_axis=0, tiled=True)
    crowded = jnp.any(asked[:, CAP] > 0)
    weights = step_weights[:, None]

    others = me ^ CORE ^ (2 * jnp.arange(parts // 2, dtype=I32))
    offsets = [[c * split + sum(cuts[c][:i]) for i in range(3)] for c in range(2)]

    def given(c, i, wt, e_blocks, last, rolled=False):
        return tiles(
            after(others, last), others, table, wt, e_blocks, offsets[c][i], cuts[c][i], 1, rolled
        )[0]

    def kept(c, i, wt, e_blocks, last, core, rolled=False):
        masks = [m for lead in (1, 0) for m in order_masks(ORDERS[i], lead)]
        mine = me ^ jnp.array(masks, I32)
        places = jnp.array([m // 2 for m in masks], I32)
        return tiles(
            after(mine, last), places, table, wt, e_blocks, offsets[c][i], cuts[c][i], 2, rolled, core
        )

    def exchange(outs, step):
        return [(out[1], swap(out[0], order[step])) for out, order in zip(outs, ORDERS)]

    def halve(pairs, last):
        outs = []
        for mine, came in pairs:
            out = add_pairs([(after(mine, last), came)])
            last = out[1]
            outs.append(out)
        return outs, last

    wt, e_blocks = prep(after(weights, outgoing), adjoint, emission)
    last, cores, early = wt, [], []
    for i in range(3):
        last = given(0, i, wt, e_blocks, last)
        cores.append(swap(last, CORE))
    for i in range(3):
        early.append(kept(0, i, wt, e_blocks, last, cores[i]))
        last = early[i][1]
    early = exchange(early, 0)
    wt, e_blocks = prep(after(weights, last), adjoint, emission, far)
    last, cores, late = wt, [], []
    halved = []
    for i in range(3):
        last = given(1, i, wt, e_blocks, last)
        cores.append(swap(last, CORE))
        for j in ((0,), (1, 2), ())[i]:
            some, last = halve(early[j : j + 1], last)
            halved += some
    early = exchange(halved, 1)
    for i in range(3):
        if i == 2:
            early, last = halve(early, last)
            early = exchange(early, 2)
        late.append(kept(1, i, wt, e_blocks, last, cores[i]))
        last = late[i][1]
    late = exchange(late, 0)
    late, last = halve(late, (last, crowded))
    late, last = halve(exchange(late, 1), last)
    late = exchange(late, 2)
    out, done = finish(after(me, last), counts, table, early, tuple(offsets[0]))
    out, _ = finish(me, counts, table, late, tuple(offsets[1]), (out, done))

    def crowded_group(state):
        out = state[1]
        wt, e_blocks = prep(after(weights, out), adjoint, emission, far)
        last, cores, again = wt, [], []
        for i in range(3):
            last = given(0, i, wt, e_blocks, last, True)
            cores.append(swap(last, CORE))
        for i in range(3):
            again.append(kept(0, i, wt, e_blocks, last, cores[i], True))
            last = again[i][1]
        for step in range(2):
            again, last = halve(exchange(again, step), last)
        out, _ = finish(me, counts, table, exchange(again, 2), tuple(offsets[0]), (out, counts))
        return jnp.zeros((), bool), out

    return lax.while_loop(lambda state: state[0], crowded_group, (crowded, out))[1][None]


def solution(mesh):
    in_specs = (P("tm", "tile"), P("tm", "tile"), P("tm"), P("tile", None), P("tile"))
    out_specs = P("tile", "tm", None, None)
    return jax.shard_map(body, mesh=mesh, in_specs=in_specs, out_specs=out_specs, check_vma=False)
```

```python
import functools

import jax
import jax.numpy as jnp
from jax import lax
from jax.experimental import pallas as pl
from jax.experimental.pallas import tpu as pltpu
from jax.sharding import PartitionSpec as P

BLK = 128
CAP = 4
GRP = 32
KA = 384
F32 = jnp.float32
BF16 = jnp.bfloat16
I32 = jnp.int32


def iota(shape, dim):
    return lax.broadcasted_iota(I32, shape, dim)


def in_hbm(a):
    return pltpu.with_memory_space_constraint(a, pltpu.HBM)


def plan_kernel(early, own_ref, count_ref, tiles_ref, request_ref, table_ref):
    slots = tiles_ref.shape[1]
    own = own_ref[0]
    both = jnp.concatenate([tiles_ref[...].astype(F32), jnp.zeros((6, slots), F32)], axis=0)
    both = both.T.astype(I32)
    r = both[:, 0:1]
    c = both[:, 1:2]
    k = iota((slots, 1), 0)
    src = c >> 7
    within = c & (BLK - 1)
    row = r & (BLK - 1)
    remote = (k < count_ref[0]) & (src != own)
    lane = iota((slots, BLK), 1)
    by_src = jnp.where((lane == src) & remote, 1.0, 0.0).astype(F32)
    by_block = jnp.where(lane == within, 1.0, 0.0).astype(F32)
    named = jnp.dot(by_src.T.astype(BF16), by_block.astype(BF16), preferred_element_type=F32)
    hit = jnp.where(named > 0.0, 1.0, 0.0).astype(F32)
    upper = jnp.where(iota((BLK, BLK), 0) <= iota((BLK, BLK), 1), 1.0, 0.0).astype(BF16)
    rank = jnp.dot(hit.astype(BF16), upper, preferred_element_type=F32) * hit
    slot_rank = jnp.sum(
        jnp.dot(by_src.astype(BF16), rank.astype(BF16), preferred_element_type=F32) * by_block,
        axis=1,
        keepdims=True,
    )
    slot_rank = jnp.clip(slot_rank.astype(I32) - 1, 0, CAP - 1)
    col = jnp.where(remote, BLK + src * CAP + slot_rank, within)

    jj = iota((slots, slots), 1)
    kk = iota((slots, slots), 0)
    same = (jj >> 5) == (kk >> 5)
    remote_f = jnp.broadcast_to(jnp.where(remote, 1.0, 0.0), (slots, BLK)).astype(BF16)
    ahead = jnp.where(same & (jj < kk), 1.0, 0.0).astype(BF16)
    ahead = jnp.dot(ahead, remote_f, preferred_element_type=F32)[:, 0:1].astype(I32)
    total = jnp.where(same, 1.0, 0.0).astype(BF16)
    total = jnp.dot(total, remote_f, preferred_element_type=F32)[:, 0:1].astype(I32)
    s = k & (GRP - 1)
    pos = jnp.where(remote, GRP - total + ahead, s - ahead)
    value = jnp.where(lane < GRP, row, jnp.where(lane < 2 * GRP, col, s))
    value = jnp.where((lane & (GRP - 1)) == pos, value, 0)
    value = jnp.where(lane < 3 * GRP, value, 0).astype(F32).astype(BF16)
    groups = slots // GRP
    pick = jnp.where((iota((groups, slots), 1) >> 5) == iota((groups, slots), 0), 1.0, 0.0)
    table_ref[...] = jnp.dot(pick.astype(BF16), value, preferred_element_type=F32).astype(I32)

    late = jnp.max(jnp.where(total > GRP - early, 1, 0), axis=0, keepdims=True)
    owners = request_ref.shape[0]
    hit8 = hit[0:owners, :]
    rank8 = rank[0:owners, :]
    lane8 = iota((owners, BLK), 1)
    request = jnp.where(lane8 == CAP, jnp.broadcast_to(late, (owners, BLK)), 0)
    for q in range(CAP):
        block = jnp.sum(
            jnp.where((rank8 == q + 1.0) & (hit8 > 0.0), lane8, 0), axis=1, keepdims=True
        )
        request = jnp.where(lane8 == q, block, request)
    request_ref[...] = request


def plan(own, counts, tile_list, owners, early):
    slots = tile_list.shape[0]
    smem = pl.BlockSpec(memory_space=pltpu.SMEM)
    vmem = pl.BlockSpec(memory_space=pltpu.VMEM)
    return pl.pallas_call(
        functools.partial(plan_kernel, early),
        in_specs=[smem, smem, vmem],
        out_specs=[vmem, vmem],
        out_shape=[
            jax.ShapeDtypeStruct((owners, BLK), I32),
            jax.ShapeDtypeStruct((slots // GRP, BLK), I32),
        ],
        compiler_params=pltpu.CompilerParams(vmem_limit_bytes=16 * 2**20),
        name="plan",
    )(own, counts, tile_list.T)


STEP = 16
DEPTH = 3


def prep_kernel(with_far, weights_ref, adj_ref, em_ref, *refs):
    if with_far:
        far_ref, refs = refs[0], refs[1:]
        refs, fsem = refs[:-1], refs[-1]
    wt_ref, e_ref, abuf, ebuf, wide, asem, esem = refs
    steps = adj_ref.shape[0]
    blocks = wt_ref.shape[0]
    chunks = blocks // STEP
    wide[...] = jnp.broadcast_to(weights_ref[...], wide.shape)

    def copies(j):
        slot = lax.rem(j, DEPTH)
        cols = pl.ds(pl.multiple_of(j * (STEP * BLK), STEP * BLK), STEP * BLK)
        return (
            pltpu.make_async_copy(adj_ref.at[:, cols], abuf.at[slot], asem.at[slot]),
            pltpu.make_async_copy(em_ref.at[:, cols], ebuf.at[slot], esem.at[slot]),
        )

    for j in range(DEPTH - 1):
        for copy in copies(j):
            copy.start()
    if with_far:
        rest = pl.ds(blocks, e_ref.shape[0] - blocks)
        far_copy = pltpu.make_async_copy(far_ref, e_ref.at[rest, pl.ds(0, steps)], fsem)
        far_copy.start()
    ones = jnp.where(iota((KA - steps, BLK), 0) < 2, 1.0, 0.0).astype(BF16)
    rows = iota((KA - steps, BLK), 0)

    def chunk(j, carry):
        slot = lax.rem(j, DEPTH)

        @pl.when(j + DEPTH - 1 < chunks)
        def _():
            for copy in copies(j + DEPTH - 1):
                copy.start()

        for copy in copies(j):
            copy.wait()
        for b in range(STEP):
            at = j * STEP + b
            w = (wide[...] * abuf[slot, :, b * BLK : (b + 1) * BLK].astype(F32)).astype(BF16)
            e = ebuf[slot, :, b * BLK : (b + 1) * BLK]
            sums = -jnp.sum(w.astype(F32) * e.astype(F32), axis=0, keepdims=True)
            high = sums.astype(BF16).astype(F32)
            low = sums - high
            tail = jnp.where(rows == 0, high, jnp.where(rows == 1, low, 0.0)).astype(BF16)
            wt_ref[at] = jnp.concatenate([w, tail], axis=0).T
            e_ref[at, 0:steps, :] = e
            e_ref[at, steps:KA, :] = ones
        return carry

    lax.fori_loop(0, chunks, chunk, 0)
    if with_far:
        for i in range(blocks, e_ref.shape[0]):
            e_ref[i, steps:KA, :] = ones
        far_copy.wait()


def prep(weights, adjoint, emission, far=None):
    steps, nodes = adjoint.shape
    blocks = nodes // BLK
    anyspace = pl.BlockSpec(memory_space=pl.ANY)
    vmem = pl.BlockSpec(memory_space=pltpu.VMEM)
    with_far = far is not None
    columns = blocks + (far.shape[0] if with_far else 0)
    wt, e_blocks = pl.pallas_call(
        functools.partial(prep_kernel, with_far),
        in_specs=[vmem] + [anyspace] * (3 if with_far else 2),
        out_specs=[vmem, vmem],
        out_shape=[
            pltpu.VMEM((blocks, BLK, KA), BF16),
            pltpu.VMEM((columns, KA, BLK), BF16),
        ],
        scratch_shapes=[
            pltpu.VMEM((DEPTH, steps, STEP * BLK), BF16),
            pltpu.VMEM((DEPTH, steps, STEP * BLK), BF16),
            pltpu.VMEM((steps, BLK), F32),
            pltpu.SemaphoreType.DMA((DEPTH,)),
            pltpu.SemaphoreType.DMA((DEPTH,)),
        ]
        + ([pltpu.SemaphoreType.DMA] if with_far else []),
        compiler_params=pltpu.CompilerParams(vmem_limit_bytes=14 * 2**20),
        name="prep",
    )(weights, in_hbm(adjoint), in_hbm(emission), *([in_hbm(far)] if with_far else []))
    return (
        pltpu.with_memory_space_constraint(wt, pltpu.VMEM),
        pltpu.with_memory_space_constraint(e_blocks, pltpu.VMEM),
    )


def pack_kernel(own_ref, asked_ref, em_ref, out_ref, sems):
    count = out_ref.shape[0]

    def copy(i):
        block = asked_ref[i >> 2, i & (CAP - 1)] & (BLK - 1)
        cols = pl.ds(pl.multiple_of(block * BLK, BLK), BLK)
        return pltpu.make_async_copy(em_ref.at[:, cols], out_ref.at[i], sems.at[i])

    for i in range(count):

        @pl.when(i // CAP != own_ref[0])
        def _():
            copy(i).start()

    for i in range(count):

        @pl.when(i // CAP != own_ref[0])
        def _():
            copy(i).wait()


def pack(own, asked, emission):
    owners = asked.shape[0]
    return pl.pallas_call(
        pack_kernel,
        in_specs=[pl.BlockSpec(memory_space=pltpu.SMEM)] * 2
        + [pl.BlockSpec(memory_space=pl.ANY)],
        out_specs=pl.BlockSpec(memory_space=pltpu.VMEM),
        out_shape=jax.ShapeDtypeStruct((owners * CAP, emission.shape[0], BLK), BF16),
        scratch_shapes=[pltpu.SemaphoreType.DMA((owners * CAP,))],
        compiler_params=pltpu.CompilerParams(vmem_limit_bytes=8 * 2**20),
        name="pack",
    )(own, asked, in_hbm(emission))


def tiles_kernel(first, per, with_add, rolled, *refs):
    groups_ref, places_ref, table_ref, wt_ref, e_ref = refs[:5]
    outs = refs[6:] if with_add else refs[5:]
    last = e_ref.shape[0] - 1
    n = 0
    for out_ref in outs:
        size = out_ref.shape[0] // per

        def one(j, carry, out_ref=out_ref, n=n):
            g = groups_ref[n + j]
            for q in range(per):
                row = table_ref[g, first + q]
                col = jnp.minimum(table_ref[g, GRP + first + q], last)
                acc = jnp.dot(wt_ref[row], e_ref[col], preferred_element_type=F32)
                if with_add:
                    acc = acc + refs[5][places_ref[n + j] * per + q].astype(F32)
                out_ref[j * per + q] = acc.astype(BF16)
            return carry

        if rolled:
            lax.fori_loop(0, size, one, 0)
        else:
            for j in range(size):
                one(j, 0)
        n += size


def tiles(groups, places, table, wt, e_blocks, first, per, outs, rolled, add=None):
    smem = pl.BlockSpec(memory_space=pltpu.SMEM)
    vmem = pl.BlockSpec(memory_space=pltpu.VMEM)
    count = groups.shape[0] * per
    with_add = add is not None
    return pl.pallas_call(
        functools.partial(tiles_kernel, first, per, with_add, rolled),
        in_specs=[smem, smem, smem, vmem, vmem] + ([vmem] if with_add else []),
        out_specs=[vmem] * outs,
        out_shape=[jax.ShapeDtypeStruct((count // outs, BLK, BLK), BF16)] * outs,
        compiler_params=pltpu.CompilerParams(vmem_limit_bytes=10 * 2**20),
        name="tiles",
    )(groups, places, table, wt, e_blocks, *([add] if with_add else []))


def add_kernel(n, *refs):
    for i in range(n):
        mine, came = refs[2 * i], refs[2 * i + 1]
        sent, kept = refs[2 * n + 2 * i], refs[2 * n + 2 * i + 1]
        half = sent.shape[0]

        def one(j, carry, mine=mine, came=came, sent=sent, kept=kept, half=half):
            sent[j] = (mine[j].astype(F32) + came[j].astype(F32)).astype(BF16)
            kept[j] = (mine[half + j].astype(F32) + came[half + j].astype(F32)).astype(BF16)
            return carry

        lax.fori_loop(0, half, one, 0, unroll=2)


def add_pairs(pairs):
    vmem = pl.BlockSpec(memory_space=pltpu.VMEM)
    shapes = []
    for mine, _ in pairs:
        shapes += [jax.ShapeDtypeStruct((mine.shape[0] // 2, BLK, BLK), BF16)] * 2
    flat = [a for pair in pairs for a in pair]
    return pl.pallas_call(
        functools.partial(add_kernel, len(pairs)),
        in_specs=[vmem] * len(flat),
        out_specs=[vmem] * len(shapes),
        out_shape=shapes,
        compiler_params=pltpu.CompilerParams(vmem_limit_bytes=20 * 2**20),
        name="add_pairs",
    )(*flat)


def finish_kernel(firsts, me_ref, count_ref, table_ref, *refs):
    me = me_ref[0]
    out_ref, done_ref, stage, sem = refs[-4:]
    n = 0
    for i, first in enumerate(firsts):
        mine, came = refs[2 * i], refs[2 * i + 1]
        for j in range(mine.shape[0]):
            s = table_ref[me, 2 * GRP + first + j]
            live = jnp.where(me * GRP + s < count_ref[0], 1.0, 0.0).astype(F32)
            stage[n] = (mine[j].astype(F32) + came[j].astype(F32)) * live
            pltpu.make_async_copy(stage.at[n], out_ref.at[s], sem).start()
            n += 1
    done_ref[...] = jnp.zeros_like(done_ref)
    pltpu.make_async_copy(stage, out_ref.at[pl.ds(0, n)], sem).wait()


def finish(me, counts, table, pairs, firsts, out=None):
    smem = pl.BlockSpec(memory_space=pltpu.SMEM)
    vmem = pl.BlockSpec(memory_space=pltpu.VMEM)
    hbm = pl.BlockSpec(memory_space=pltpu.HBM)
    flat = [a for pair in pairs for a in pair]
    n = sum(mine.shape[0] for mine, _ in pairs)
    given = out is not None
    return pl.pallas_call(
        functools.partial(finish_kernel, firsts),
        in_specs=[smem, smem, smem] + [vmem] * len(flat)
        + ([hbm, pl.BlockSpec(memory_space=pl.ANY)] if given else []),
        out_specs=[hbm, vmem],
        out_shape=[pltpu.HBM((GRP, BLK, BLK), F32), jax.ShapeDtypeStruct((8, BLK), F32)],
        input_output_aliases={3 + len(flat): 0} if given else {},
        scratch_shapes=[pltpu.VMEM((n, BLK, BLK), F32), pltpu.SemaphoreType.DMA],
        compiler_params=pltpu.CompilerParams(vmem_limit_bytes=16 * 2**20),
        name="finish",
    )(me, counts, table, *flat, *(out if given else ()))


CORE, ALONG_X, UP_Y, DOWN_Y = 1, 2, 4, 12
ORDERS = (
    (ALONG_X, UP_Y, DOWN_Y),
    (UP_Y, DOWN_Y, ALONG_X),
    (DOWN_Y, ALONG_X, UP_Y),
)


def swap(a, mask):
    n = lax.axis_size("tm")
    return lax.ppermute(a, "tm", [(i, i ^ mask) for i in range(n)])


def after(a, other):
    return lax.optimization_barrier((a, other))[0]


def order_masks(order, lead):
    first, second, third = order
    return [lead * first ^ s * second ^ t * third for s in (1, 0) for t in (1, 0)]


def body(adjoint, emission, step_weights, tile_list, counts):
    owners = lax.axis_size("tile")
    parts = lax.axis_size("tm")
    own = lax.axis_index("tile").astype(I32).reshape(1)
    me = lax.axis_index("tm").astype(I32).reshape(1)
    cuts = ((6, 6, 6), (5, 5, 4))
    split = sum(cuts[0])
    request, table = plan(own, counts, tile_list, owners, split)
    asked = lax.all_to_all(request, "tile", split_axis=0, concat_axis=0, tiled=True)
    outgoing = pack(own, asked, emission)
    far = lax.all_to_all(outgoing, "tile", split_axis=0, concat_axis=0, tiled=True)
    crowded = jnp.any(asked[:, CAP] > 0)
    weights = step_weights[:, None]

    others = me ^ CORE ^ (2 * jnp.arange(parts // 2, dtype=I32))
    offsets = [[c * split + sum(cuts[c][:i]) for i in range(3)] for c in range(2)]

    def given(c, i, wt, e_blocks, last, rolled=False):
        return tiles(
            after(others, last), others, table, wt, e_blocks, offsets[c][i], cuts[c][i], 1, rolled
        )[0]

    def kept(c, i, wt, e_blocks, last, core, rolled=False):
        masks = [m for lead in (1, 0) for m in order_masks(ORDERS[i], lead)]
        mine = me ^ jnp.array(masks, I32)
        places = jnp.array([m // 2 for m in masks], I32)
        return tiles(
            after(mine, last), places, table, wt, e_blocks, offsets[c][i], cuts[c][i], 2, rolled, core
        )

    def exchange(outs, step):
        return [(out[1], swap(out[0], order[step])) for out, order in zip(outs, ORDERS)]

    def halve(pairs, last):
        outs = []
        for mine, came in pairs:
            out = add_pairs([(after(mine, last), came)])
            last = out[1]
            outs.append(out)
        return outs, last

    wt, e_blocks = prep(after(weights, outgoing), adjoint, emission)
    last, cores, early = wt, [], []
    for i in range(3):
        last = given(0, i, wt, e_blocks, last)
        cores.append(swap(last, CORE))
    for i in range(3):
        early.append(kept(0, i, wt, e_blocks, last, cores[i]))
        last = early[i][1]
    early = exchange(early, 0)
    wt, e_blocks = prep(after(weights, last), adjoint, emission, far)
    last, cores, late = wt, [], []
    halved = []
    for i in range(3):
        last = given(1, i, wt, e_blocks, last)
        cores.append(swap(last, CORE))
        for j in ((0,), (1, 2), ())[i]:
            some, last = halve(early[j : j + 1], last)
            halved += some
    early = exchange(halved, 1)
    for i in range(3):
        if i == 2:
            early, last = halve(early, last)
            early = exchange(early, 2)
        late.append(kept(1, i, wt, e_blocks, last, cores[i]))
        last = late[i][1]
    late = exchange(late, 0)
    late, last = halve(late, (last, crowded))
    late, last = halve(exchange(late, 1), last)
    late = exchange(late, 2)
    out, done = finish(after(me, last), counts, table, early, tuple(offsets[0]))
    out, _ = finish(me, counts, table, late, tuple(offsets[1]), (out, done))

    def crowded_group(state):
        out = state[1]
        wt, e_blocks = prep(after(weights, out), adjoint, emission, far)
        last, cores, again = wt, [], []
        for i in range(3):
            last = given(0, i, wt, e_blocks, last, True)
            cores.append(swap(last, CORE))
        for i in range(3):
            again.append(kept(0, i, wt, e_blocks, last, cores[i], True))
            last = again[i][1]
        for step in range(2):
            again, last = halve(exchange(again, step), last)
        out, _ = finish(me, counts, table, exchange(again, 2), tuple(offsets[0]), (out, counts))
        return jnp.zeros((), bool), out

    return lax.while_loop(lambda state: state[0], crowded_group, (crowded, out))[1][None]


def solution(mesh):
    in_specs = (P("tm", "tile"), P("tm", "tile"), P("tm"), P("tile", None), P("tile"))
    out_specs = P("tile", "tm", None, None)
    return jax.shard_map(body, mesh=mesh, in_specs=in_specs, out_specs=out_specs, check_vma=False)
```

```python
import functools

import jax
import jax.numpy as jnp
from jax import lax
from jax.experimental import pallas as pl
from jax.experimental.pallas import tpu as pltpu
from jax.sharding import PartitionSpec as P

BLK = 128
CAP = 4
GRP = 32
KA = 384
F32 = jnp.float32
BF16 = jnp.bfloat16
I32 = jnp.int32


def iota(shape, dim):
    return lax.broadcasted_iota(I32, shape, dim)


def in_hbm(a):
    return pltpu.with_memory_space_constraint(a, pltpu.HBM)


def plan_kernel(early, own_ref, count_ref, tiles_ref, request_ref, table_ref):
    slots = tiles_ref.shape[1]
    own = own_ref[0]
    both = jnp.concatenate([tiles_ref[...].astype(F32), jnp.zeros((6, slots), F32)], axis=0)
    both = both.T.astype(I32)
    r = both[:, 0:1]
    c = both[:, 1:2]
    k = iota((slots, 1), 0)
    src = c >> 7
    within = c & (BLK - 1)
    row = r & (BLK - 1)
    remote = (k < count_ref[0]) & (src != own)
    lane = iota((slots, BLK), 1)
    by_src = jnp.where((lane == src) & remote, 1.0, 0.0).astype(F32)
    by_block = jnp.where(lane == within, 1.0, 0.0).astype(F32)
    named = jnp.dot(by_src.T.astype(BF16), by_block.astype(BF16), preferred_element_type=F32)
    hit = jnp.where(named > 0.0, 1.0, 0.0).astype(F32)
    upper = jnp.where(iota((BLK, BLK), 0) <= iota((BLK, BLK), 1), 1.0, 0.0).astype(BF16)
    rank = jnp.dot(hit.astype(BF16), upper, preferred_element_type=F32) * hit
    slot_rank = jnp.sum(
        jnp.dot(by_src.astype(BF16), rank.astype(BF16), preferred_element_type=F32) * by_block,
        axis=1,
        keepdims=True,
    )
    slot_rank = jnp.clip(slot_rank.astype(I32) - 1, 0, CAP - 1)
    col = jnp.where(remote, BLK + src * CAP + slot_rank, within)

    jj = iota((slots, slots), 1)
    kk = iota((slots, slots), 0)
    same = (jj >> 5) == (kk >> 5)
    remote_f = jnp.broadcast_to(jnp.where(remote, 1.0, 0.0), (slots, BLK)).astype(BF16)
    ahead = jnp.where(same & (jj < kk), 1.0, 0.0).astype(BF16)
    ahead = jnp.dot(ahead, remote_f, preferred_element_type=F32)[:, 0:1].astype(I32)
    total = jnp.where(same, 1.0, 0.0).astype(BF16)
    total = jnp.dot(total, remote_f, preferred_element_type=F32)[:, 0:1].astype(I32)
    s = k & (GRP - 1)
    pos = jnp.where(remote, GRP - total + ahead, s - ahead)
    value = jnp.where(lane < GRP, row, jnp.where(lane < 2 * GRP, col, s))
    value = jnp.where((lane & (GRP - 1)) == pos, value, 0)
    value = jnp.where(lane < 3 * GRP, value, 0).astype(F32).astype(BF16)
    groups = slots // GRP
    pick = jnp.where((iota((groups, slots), 1) >> 5) == iota((groups, slots), 0), 1.0, 0.0)
    table_ref[...] = jnp.dot(pick.astype(BF16), value, preferred_element_type=F32).astype(I32)

    late = jnp.max(jnp.where(total > GRP - early, 1, 0), axis=0, keepdims=True)
    owners = request_ref.shape[0]
    hit8 = hit[0:owners, :]
    rank8 = rank[0:owners, :]
    lane8 = iota((owners, BLK), 1)
    request = jnp.where(lane8 == CAP, jnp.broadcast_to(late, (owners, BLK)), 0)
    for q in range(CAP):
        block = jnp.sum(
            jnp.where((rank8 == q + 1.0) & (hit8 > 0.0), lane8, 0), axis=1, keepdims=True
        )
        request = jnp.where(lane8 == q, block, request)
    request_ref[...] = request


def plan(own, counts, tile_list, owners, early):
    slots = tile_list.shape[0]
    smem = pl.BlockSpec(memory_space=pltpu.SMEM)
    vmem = pl.BlockSpec(memory_space=pltpu.VMEM)
    return pl.pallas_call(
        functools.partial(plan_kernel, early),
        in_specs=[smem, smem, vmem],
        out_specs=[vmem, vmem],
        out_shape=[
            jax.ShapeDtypeStruct((owners, BLK), I32),
            jax.ShapeDtypeStruct((slots // GRP, BLK), I32),
        ],
        compiler_params=pltpu.CompilerParams(vmem_limit_bytes=16 * 2**20),
        name="plan",
    )(own, counts, tile_list.T)


STEP = 16
DEPTH = 3


def prep_kernel(with_far, weights_ref, adj_ref, em_ref, *refs):
    if with_far:
        far_ref, refs = refs[0], refs[1:]
        refs, fsem = refs[:-1], refs[-1]
    wt_ref, e_ref, abuf, ebuf, wide, asem, esem = refs
    steps = adj_ref.shape[0]
    blocks = wt_ref.shape[0]
    chunks = blocks // STEP
    wide[...] = jnp.broadcast_to(weights_ref[...], wide.shape)

    def copies(j):
        slot = lax.rem(j, DEPTH)
        cols = pl.ds(pl.multiple_of(j * (STEP * BLK), STEP * BLK), STEP * BLK)
        return (
            pltpu.make_async_copy(adj_ref.at[:, cols], abuf.at[slot], asem.at[slot]),
            pltpu.make_async_copy(em_ref.at[:, cols], ebuf.at[slot], esem.at[slot]),
        )

    for j in range(DEPTH - 1):
        for copy in copies(j):
            copy.start()
    if with_far:
        rest = pl.ds(blocks, e_ref.shape[0] - blocks)
        far_copy = pltpu.make_async_copy(far_ref, e_ref.at[rest, pl.ds(0, steps)], fsem)
        far_copy.start()
    ones = jnp.where(iota((KA - steps, BLK), 0) < 2, 1.0, 0.0).astype(BF16)
    rows = iota((KA - steps, BLK), 0)

    def chunk(j, carry):
        slot = lax.rem(j, DEPTH)

        @pl.when(j + DEPTH - 1 < chunks)
        def _():
            for copy in copies(j + DEPTH - 1):
                copy.start()

        for copy in copies(j):
            copy.wait()
        for b in range(STEP):
            at = j * STEP + b
            w = (wide[...] * abuf[slot, :, b * BLK : (b + 1) * BLK].astype(F32)).astype(BF16)
            e = ebuf[slot, :, b * BLK : (b + 1) * BLK]
            sums = -jnp.sum(w.astype(F32) * e.astype(F32), axis=0, keepdims=True)
            high = sums.astype(BF16).astype(F32)
            low = sums - high
            tail = jnp.where(rows == 0, high, jnp.where(rows == 1, low, 0.0)).astype(BF16)
            wt_ref[at] = jnp.concatenate([w, tail], axis=0).T
            e_ref[at, 0:steps, :] = e
            e_ref[at, steps:KA, :] = ones
        return carry

    lax.fori_loop(0, chunks, chunk, 0)
    if with_far:
        for i in range(blocks, e_ref.shape[0]):
            e_ref[i, steps:KA, :] = ones
        far_copy.wait()


def prep(weights, adjoint, emission, far=None):
    steps, nodes = adjoint.shape
    blocks = nodes // BLK
    anyspace = pl.BlockSpec(memory_space=pl.ANY)
    vmem = pl.BlockSpec(memory_space=pltpu.VMEM)
    with_far = far is not None
    columns = blocks + (far.shape[0] if with_far else 0)
    wt, e_blocks = pl.pallas_call(
        functools.partial(prep_kernel, with_far),
        in_specs=[vmem] + [anyspace] * (3 if with_far else 2),
        out_specs=[vmem, vmem],
        out_shape=[
            pltpu.VMEM((blocks, BLK, KA), BF16),
            pltpu.VMEM((columns, KA, BLK), BF16),
        ],
        scratch_shapes=[
            pltpu.VMEM((DEPTH, steps, STEP * BLK), BF16),
            pltpu.VMEM((DEPTH, steps, STEP * BLK), BF16),
            pltpu.VMEM((steps, BLK), F32),
            pltpu.SemaphoreType.DMA((DEPTH,)),
            pltpu.SemaphoreType.DMA((DEPTH,)),
        ]
        + ([pltpu.SemaphoreType.DMA] if with_far else []),
        compiler_params=pltpu.CompilerParams(vmem_limit_bytes=14 * 2**20),
        name="prep",
    )(weights, in_hbm(adjoint), in_hbm(emission), *([in_hbm(far)] if with_far else []))
    return (
        pltpu.with_memory_space_constraint(wt, pltpu.VMEM),
        pltpu.with_memory_space_constraint(e_blocks, pltpu.VMEM),
    )


def pack_kernel(own_ref, asked_ref, em_ref, out_ref, sems):
    count = out_ref.shape[0]

    def copy(i):
        block = asked_ref[i >> 2, i & (CAP - 1)] & (BLK - 1)
        cols = pl.ds(pl.multiple_of(block * BLK, BLK), BLK)
        return pltpu.make_async_copy(em_ref.at[:, cols], out_ref.at[i], sems.at[i])

    for i in range(count):

        @pl.when(i // CAP != own_ref[0])
        def _():
            copy(i).start()

    for i in range(count):

        @pl.when(i // CAP != own_ref[0])
        def _():
            copy(i).wait()


def pack(own, asked, emission):
    owners = asked.shape[0]
    return pl.pallas_call(
        pack_kernel,
        in_specs=[pl.BlockSpec(memory_space=pltpu.SMEM)] * 2
        + [pl.BlockSpec(memory_space=pl.ANY)],
        out_specs=pl.BlockSpec(memory_space=pltpu.VMEM),
        out_shape=jax.ShapeDtypeStruct((owners * CAP, emission.shape[0], BLK), BF16),
        scratch_shapes=[pltpu.SemaphoreType.DMA((owners * CAP,))],
        compiler_params=pltpu.CompilerParams(vmem_limit_bytes=8 * 2**20),
        name="pack",
    )(own, asked, in_hbm(emission))


def tiles_kernel(first, per, with_add, rolled, *refs):
    groups_ref, places_ref, table_ref, wt_ref, e_ref = refs[:5]
    outs = refs[6:] if with_add else refs[5:]
    last = e_ref.shape[0] - 1
    n = 0
    for out_ref in outs:
        size = out_ref.shape[0] // per

        def one(j, carry, out_ref=out_ref, n=n):
            g = groups_ref[n + j]
            for q in range(per):
                row = table_ref[g, first + q]
                col = jnp.minimum(table_ref[g, GRP + first + q], last)
                acc = jnp.dot(wt_ref[row], e_ref[col], preferred_element_type=F32)
                if with_add:
                    acc = acc + refs[5][places_ref[n + j] * per + q].astype(F32)
                out_ref[j * per + q] = acc.astype(BF16)
            return carry

        if rolled:
            lax.fori_loop(0, size, one, 0)
        else:
            for j in range(size):
                one(j, 0)
        n += size


def tiles(groups, places, table, wt, e_blocks, first, per, outs, rolled, add=None):
    smem = pl.BlockSpec(memory_space=pltpu.SMEM)
    vmem = pl.BlockSpec(memory_space=pltpu.VMEM)
    count = groups.shape[0] * per
    with_add = add is not None
    return pl.pallas_call(
        functools.partial(tiles_kernel, first, per, with_add, rolled),
        in_specs=[smem, smem, smem, vmem, vmem] + ([vmem] if with_add else []),
        out_specs=[vmem] * outs,
        out_shape=[jax.ShapeDtypeStruct((count // outs, BLK, BLK), BF16)] * outs,
        compiler_params=pltpu.CompilerParams(vmem_limit_bytes=10 * 2**20),
        name="tiles",
    )(groups, places, table, wt, e_blocks, *([add] if with_add else []))


def add_kernel(n, *refs):
    for i in range(n):
        mine, came = refs[2 * i], refs[2 * i + 1]
        sent, kept = refs[2 * n + 2 * i], refs[2 * n + 2 * i + 1]
        half = sent.shape[0]

        def one(j, carry, mine=mine, came=came, sent=sent, kept=kept, half=half):
            sent[j] = (mine[j].astype(F32) + came[j].astype(F32)).astype(BF16)
            kept[j] = (mine[half + j].astype(F32) + came[half + j].astype(F32)).astype(BF16)
            return carry

        lax.fori_loop(0, half, one, 0, unroll=2)


def add_pairs(pairs):
    vmem = pl.BlockSpec(memory_space=pltpu.VMEM)
    shapes = []
    for mine, _ in pairs:
        shapes += [jax.ShapeDtypeStruct((mine.shape[0] // 2, BLK, BLK), BF16)] * 2
    flat = [a for pair in pairs for a in pair]
    return pl.pallas_call(
        functools.partial(add_kernel, len(pairs)),
        in_specs=[vmem] * len(flat),
        out_specs=[vmem] * len(shapes),
        out_shape=shapes,
        compiler_params=pltpu.CompilerParams(vmem_limit_bytes=20 * 2**20),
        name="add_pairs",
    )(*flat)


def finish_kernel(firsts, me_ref, count_ref, table_ref, *refs):
    me = me_ref[0]
    out_ref, done_ref, stage, sem = refs[-4:]
    n = 0
    for i, first in enumerate(firsts):
        mine, came = refs[2 * i], refs[2 * i + 1]
        for j in range(mine.shape[0]):
            s = table_ref[me, 2 * GRP + first + j]
            live = jnp.where(me * GRP + s < count_ref[0], 1.0, 0.0).astype(F32)
            stage[n] = (mine[j].astype(F32) + came[j].astype(F32)) * live
            pltpu.make_async_copy(stage.at[n], out_ref.at[s], sem).start()
            n += 1
    done_ref[...] = jnp.zeros_like(done_ref)
    pltpu.make_async_copy(stage, out_ref.at[pl.ds(0, n)], sem).wait()


def finish(me, counts, table, pairs, firsts, out=None):
    smem = pl.BlockSpec(memory_space=pltpu.SMEM)
    vmem = pl.BlockSpec(memory_space=pltpu.VMEM)
    hbm = pl.BlockSpec(memory_space=pltpu.HBM)
    flat = [a for pair in pairs for a in pair]
    n = sum(mine.shape[0] for mine, _ in pairs)
    given = out is not None
    return pl.pallas_call(
        functools.partial(finish_kernel, firsts),
        in_specs=[smem, smem, smem] + [vmem] * len(flat)
        + ([hbm, pl.BlockSpec(memory_space=pl.ANY)] if given else []),
        out_specs=[hbm, vmem],
        out_shape=[pltpu.HBM((GRP, BLK, BLK), F32), jax.ShapeDtypeStruct((8, BLK), F32)],
        input_output_aliases={3 + len(flat): 0} if given else {},
        scratch_shapes=[pltpu.VMEM((n, BLK, BLK), F32), pltpu.SemaphoreType.DMA],
        compiler_params=pltpu.CompilerParams(vmem_limit_bytes=16 * 2**20),
        name="finish",
    )(me, counts, table, *flat, *(out if given else ()))


CORE, ALONG_X, UP_Y, DOWN_Y = 1, 2, 4, 12
ORDERS = (
    (ALONG_X, UP_Y, DOWN_Y),
    (UP_Y, DOWN_Y, ALONG_X),
    (DOWN_Y, ALONG_X, UP_Y),
)
TURNS = (ORDERS, ORDERS[1:] + ORDERS[:1])


def swap(a, mask):
    n = lax.axis_size("tm")
    return lax.ppermute(a, "tm", [(i, i ^ mask) for i in range(n)])


def after(a, other):
    return lax.optimization_barrier((a, other))[0]


def order_masks(order, lead):
    first, second, third = order
    return [lead * first ^ s * second ^ t * third for s in (1, 0) for t in (1, 0)]


def body(adjoint, emission, step_weights, tile_list, counts):
    owners = lax.axis_size("tile")
    parts = lax.axis_size("tm")
    own = lax.axis_index("tile").astype(I32).reshape(1)
    me = lax.axis_index("tm").astype(I32).reshape(1)
    cuts = ((6, 6, 6), (5, 5, 4))
    split = sum(cuts[0])
    request, table = plan(own, counts, tile_list, owners, split)
    asked = lax.all_to_all(request, "tile", split_axis=0, concat_axis=0, tiled=True)
    outgoing = pack(own, asked, emission)
    far = lax.all_to_all(outgoing, "tile", split_axis=0, concat_axis=0, tiled=True)
    crowded = jnp.any(asked[:, CAP] > 0)
    weights = step_weights[:, None]

    others = me ^ CORE ^ (2 * jnp.arange(parts // 2, dtype=I32))
    offsets = [[c * split + sum(cuts[c][:i]) for i in range(3)] for c in range(2)]

    def given(c, i, wt, e_blocks, last, rolled=False):
        return tiles(
            after(others, last), others, table, wt, e_blocks, offsets[c][i], cuts[c][i], 1, rolled
        )[0]

    def kept(c, i, wt, e_blocks, last, core, rolled=False):
        masks = [m for lead in (1, 0) for m in order_masks(TURNS[c][i], lead)]
        mine = me ^ jnp.array(masks, I32)
        places = jnp.array([m // 2 for m in masks], I32)
        return tiles(
            after(mine, last), places, table, wt, e_blocks, offsets[c][i], cuts[c][i], 2, rolled, core
        )

    def exchange(c, outs, step):
        return [(out[1], swap(out[0], order[step])) for out, order in zip(outs, TURNS[c])]

    def halve(pairs, last):
        outs = []
        for mine, came in pairs:
            out = add_pairs([(after(mine, last), came)])
            last = out[1]
            outs.append(out)
        return outs, last

    wt, e_blocks = prep(after(weights, outgoing), adjoint, emission)
    last, cores, early = wt, [], []
    for i in range(3):
        last = given(0, i, wt, e_blocks, last)
        cores.append(swap(last, CORE))
    for i in range(3):
        early.append(kept(0, i, wt, e_blocks, last, cores[i]))
        last = early[i][1]
    early = exchange(0, early, 0)
    wt, e_blocks = prep(after(weights, last), adjoint, emission, far)
    last, cores, late = wt, [], []
    halved = []
    for i in range(3):
        last = given(1, i, wt, e_blocks, last)
        cores.append(swap(last, CORE))
        for j in ((0,), (1, 2), ())[i]:
            some, last = halve(early[j : j + 1], last)
            halved += some
    early = exchange(0, halved, 1)
    for i in range(3):
        if i == 2:
            early, last = halve(early, last)
            early = exchange(0, early, 2)
        late.append(kept(1, i, wt, e_blocks, last, cores[i]))
        last = late[i][1]
    late = exchange(1, late, 0)
    late, last = halve(late, (last, crowded))
    late, last = halve(exchange(1, late, 1), last)
    late = exchange(1, late, 2)
    out, done = finish(after(me, last), counts, table, early, tuple(offsets[0]))
    out, _ = finish(me, counts, table, late, tuple(offsets[1]), (out, done))

    def crowded_group(state):
        out = state[1]
        wt, e_blocks = prep(after(weights, out), adjoint, emission, far)
        last, cores, again = wt, [], []
        for i in range(3):
            last = given(0, i, wt, e_blocks, last, True)
            cores.append(swap(last, CORE))
        for i in range(3):
            again.append(kept(0, i, wt, e_blocks, last, cores[i], True))
            last = again[i][1]
        for step in range(2):
            again, last = halve(exchange(0, again, step), last)
        out, _ = finish(me, counts, table, exchange(0, again, 2), tuple(offsets[0]), (out, counts))
        return jnp.zeros((), bool), out

    return lax.while_loop(lambda state: state[0], crowded_group, (crowded, out))[1][None]


def solution(mesh):
    in_specs = (P("tm", "tile"), P("tm", "tile"), P("tm"), P("tile", None), P("tile"))
    out_specs = P("tile", "tm", None, None)
    return jax.shard_map(body, mesh=mesh, in_specs=in_specs, out_specs=out_specs, check_vma=False)
```

```python
import functools

import jax
import jax.numpy as jnp
from jax import lax
from jax.experimental import pallas as pl
from jax.experimental.pallas import tpu as pltpu
from jax.sharding import PartitionSpec as P

BLK = 128
CAP = 4
GRP = 32
KA = 384
F32 = jnp.float32
BF16 = jnp.bfloat16
I32 = jnp.int32


def iota(shape, dim):
    return lax.broadcasted_iota(I32, shape, dim)


def in_hbm(a):
    return pltpu.with_memory_space_constraint(a, pltpu.HBM)


def plan_kernel(early, own_ref, count_ref, tiles_ref, request_ref, table_ref):
    slots = tiles_ref.shape[1]
    own = own_ref[0]
    both = jnp.concatenate([tiles_ref[...].astype(F32), jnp.zeros((6, slots), F32)], axis=0)
    both = both.T.astype(I32)
    r = both[:, 0:1]
    c = both[:, 1:2]
    k = iota((slots, 1), 0)
    src = c >> 7
    within = c & (BLK - 1)
    row = r & (BLK - 1)
    remote = (k < count_ref[0]) & (src != own)
    lane = iota((slots, BLK), 1)
    by_src = jnp.where((lane == src) & remote, 1.0, 0.0).astype(F32)
    by_block = jnp.where(lane == within, 1.0, 0.0).astype(F32)
    named = jnp.dot(by_src.T.astype(BF16), by_block.astype(BF16), preferred_element_type=F32)
    hit = jnp.where(named > 0.0, 1.0, 0.0).astype(F32)
    upper = jnp.where(iota((BLK, BLK), 0) <= iota((BLK, BLK), 1), 1.0, 0.0).astype(BF16)
    rank = jnp.dot(hit.astype(BF16), upper, preferred_element_type=F32) * hit
    slot_rank = jnp.sum(
        jnp.dot(by_src.astype(BF16), rank.astype(BF16), preferred_element_type=F32) * by_block,
        axis=1,
        keepdims=True,
    )
    slot_rank = jnp.clip(slot_rank.astype(I32) - 1, 0, CAP - 1)
    col = jnp.where(remote, BLK + src * CAP + slot_rank, within)

    jj = iota((slots, slots), 1)
    kk = iota((slots, slots), 0)
    same = (jj >> 5) == (kk >> 5)
    remote_f = jnp.broadcast_to(jnp.where(remote, 1.0, 0.0), (slots, BLK)).astype(BF16)
    ahead = jnp.where(same & (jj < kk), 1.0, 0.0).astype(BF16)
    ahead = jnp.dot(ahead, remote_f, preferred_element_type=F32)[:, 0:1].astype(I32)
    total = jnp.where(same, 1.0, 0.0).astype(BF16)
    total = jnp.dot(total, remote_f, preferred_element_type=F32)[:, 0:1].astype(I32)
    s = k & (GRP - 1)
    pos = jnp.where(remote, GRP - total + ahead, s - ahead)
    value = jnp.where(lane < GRP, row, jnp.where(lane < 2 * GRP, col, s))
    value = jnp.where((lane & (GRP - 1)) == pos, value, 0)
    value = jnp.where(lane < 3 * GRP, value, 0).astype(F32).astype(BF16)
    groups = slots // GRP
    pick = jnp.where((iota((groups, slots), 1) >> 5) == iota((groups, slots), 0), 1.0, 0.0)
    table_ref[...] = jnp.dot(pick.astype(BF16), value, preferred_element_type=F32).astype(I32)

    late = jnp.max(jnp.where(total > GRP - early, 1, 0), axis=0, keepdims=True)
    owners = request_ref.shape[0]
    hit8 = hit[0:owners, :]
    rank8 = rank[0:owners, :]
    lane8 = iota((owners, BLK), 1)
    request = jnp.where(lane8 == CAP, jnp.broadcast_to(late, (owners, BLK)), 0)
    for q in range(CAP):
        block = jnp.sum(
            jnp.where((rank8 == q + 1.0) & (hit8 > 0.0), lane8, 0), axis=1, keepdims=True
        )
        request = jnp.where(lane8 == q, block, request)
    request_ref[...] = request


def plan(own, counts, tile_list, owners, early):
    slots = tile_list.shape[0]
    smem = pl.BlockSpec(memory_space=pltpu.SMEM)
    vmem = pl.BlockSpec(memory_space=pltpu.VMEM)
    return pl.pallas_call(
        functools.partial(plan_kernel, early),
        in_specs=[smem, smem, vmem],
        out_specs=[vmem, vmem],
        out_shape=[
            jax.ShapeDtypeStruct((owners, BLK), I32),
            jax.ShapeDtypeStruct((slots // GRP, BLK), I32),
        ],
        compiler_params=pltpu.CompilerParams(vmem_limit_bytes=16 * 2**20),
        name="plan",
    )(own, counts, tile_list.T)


STEP = 16
DEPTH = 3
PARTS = 2


def prep_kernel(with_far, weights_ref, adj_ref, em_ref, *refs):
    if with_far:
        far_ref, refs = refs[0], refs[1:]
        refs, fsem = refs[:-1], refs[-1]
    wt_ref, e_ref, abuf, ebuf, wide, asem, esem = refs
    steps = adj_ref.shape[0]
    blocks = wt_ref.shape[0]
    chunks = blocks // STEP
    part = STEP // PARTS * BLK

    def copies(j, h):
        slot = lax.rem(j, DEPTH)
        cols = pl.ds(pl.multiple_of(j * (STEP * BLK) + h * part, part), part)
        here = pl.ds(h * part, part)
        return (
            pltpu.make_async_copy(adj_ref.at[:, cols], abuf.at[slot, :, here], asem.at[slot, h]),
            pltpu.make_async_copy(em_ref.at[:, cols], ebuf.at[slot, :, here], esem.at[slot, h]),
        )

    def start(j):
        for h in range(PARTS):
            for copy in copies(j, h):
                copy.start()

    for j in range(DEPTH - 1):
        start(j)
    wide[...] = jnp.broadcast_to(weights_ref[...], wide.shape)
    if with_far:
        rest = pl.ds(blocks, e_ref.shape[0] - blocks)
        far_copy = pltpu.make_async_copy(far_ref, e_ref.at[rest, pl.ds(0, steps)], fsem)
        far_copy.start()
    ones = jnp.where(iota((KA - steps, BLK), 0) < 2, 1.0, 0.0).astype(BF16)
    rows = iota((KA - steps, BLK), 0)

    def chunk(j, carry):
        slot = lax.rem(j, DEPTH)

        @pl.when(j + DEPTH - 1 < chunks)
        def _():
            start(j + DEPTH - 1)

        for b in range(STEP):
            if b % (STEP // PARTS) == 0:
                for copy in copies(j, b // (STEP // PARTS)):
                    copy.wait()
            at = j * STEP + b
            w = (wide[...] * abuf[slot, :, b * BLK : (b + 1) * BLK].astype(F32)).astype(BF16)
            e = ebuf[slot, :, b * BLK : (b + 1) * BLK]
            sums = -jnp.sum(w.astype(F32) * e.astype(F32), axis=0, keepdims=True)
            high = sums.astype(BF16).astype(F32)
            low = sums - high
            tail = jnp.where(rows == 0, high, jnp.where(rows == 1, low, 0.0)).astype(BF16)
            wt_ref[at] = jnp.concatenate([w, tail], axis=0).T
            e_ref[at, 0:steps, :] = e
            e_ref[at, steps:KA, :] = ones
        return carry

    lax.fori_loop(0, chunks, chunk, 0)
    if with_far:
        for i in range(blocks, e_ref.shape[0]):
            e_ref[i, steps:KA, :] = ones
        far_copy.wait()


def prep(weights, adjoint, emission, far=None):
    steps, nodes = adjoint.shape
    blocks = nodes // BLK
    anyspace = pl.BlockSpec(memory_space=pl.ANY)
    vmem = pl.BlockSpec(memory_space=pltpu.VMEM)
    with_far = far is not None
    columns = blocks + (far.shape[0] if with_far else 0)
    wt, e_blocks = pl.pallas_call(
        functools.partial(prep_kernel, with_far),
        in_specs=[vmem] + [anyspace] * (3 if with_far else 2),
        out_specs=[vmem, vmem],
        out_shape=[
            pltpu.VMEM((blocks, BLK, KA), BF16),
            pltpu.VMEM((columns, KA, BLK), BF16),
        ],
        scratch_shapes=[
            pltpu.VMEM((DEPTH, steps, STEP * BLK), BF16),
            pltpu.VMEM((DEPTH, steps, STEP * BLK), BF16),
            pltpu.VMEM((steps, BLK), F32),
            pltpu.SemaphoreType.DMA((DEPTH, PARTS)),
            pltpu.SemaphoreType.DMA((DEPTH, PARTS)),
        ]
        + ([pltpu.SemaphoreType.DMA] if with_far else []),
        compiler_params=pltpu.CompilerParams(vmem_limit_bytes=14 * 2**20),
        name="prep",
    )(weights, in_hbm(adjoint), in_hbm(emission), *([in_hbm(far)] if with_far else []))
    return (
        pltpu.with_memory_space_constraint(wt, pltpu.VMEM),
        pltpu.with_memory_space_constraint(e_blocks, pltpu.VMEM),
    )


def pack_kernel(own_ref, asked_ref, em_ref, out_ref, sems):
    count = out_ref.shape[0]

    def copy(i):
        block = asked_ref[i >> 2, i & (CAP - 1)] & (BLK - 1)
        cols = pl.ds(pl.multiple_of(block * BLK, BLK), BLK)
        return pltpu.make_async_copy(em_ref.at[:, cols], out_ref.at[i], sems.at[i])

    for i in range(count):

        @pl.when(i // CAP != own_ref[0])
        def _():
            copy(i).start()

    for i in range(count):

        @pl.when(i // CAP != own_ref[0])
        def _():
            copy(i).wait()


def pack(own, asked, emission):
    owners = asked.shape[0]
    return pl.pallas_call(
        pack_kernel,
        in_specs=[pl.BlockSpec(memory_space=pltpu.SMEM)] * 2
        + [pl.BlockSpec(memory_space=pl.ANY)],
        out_specs=pl.BlockSpec(memory_space=pltpu.VMEM),
        out_shape=jax.ShapeDtypeStruct((owners * CAP, emission.shape[0], BLK), BF16),
        scratch_shapes=[pltpu.SemaphoreType.DMA((owners * CAP,))],
        compiler_params=pltpu.CompilerParams(vmem_limit_bytes=8 * 2**20),
        name="pack",
    )(own, asked, in_hbm(emission))


def tiles_kernel(first, per, with_add, rolled, *refs):
    groups_ref, places_ref, table_ref, wt_ref, e_ref = refs[:5]
    outs = refs[6:] if with_add else refs[5:]
    last = e_ref.shape[0] - 1
    n = 0
    for out_ref in outs:
        size = out_ref.shape[0] // per

        def one(j, carry, out_ref=out_ref, n=n):
            g = groups_ref[n + j]
            for q in range(per):
                row = table_ref[g, first + q]
                col = jnp.minimum(table_ref[g, GRP + first + q], last)
                acc = jnp.dot(wt_ref[row], e_ref[col], preferred_element_type=F32)
                if with_add:
                    acc = acc + refs[5][places_ref[n + j] * per + q].astype(F32)
                out_ref[j * per + q] = acc.astype(BF16)
            return carry

        if rolled:
            lax.fori_loop(0, size, one, 0)
        else:
            for j in range(size):
                one(j, 0)
        n += size


def tiles(groups, places, table, wt, e_blocks, first, per, outs, rolled, add=None, to_hbm=False):
    smem = pl.BlockSpec(memory_space=pltpu.SMEM)
    vmem = pl.BlockSpec(memory_space=pltpu.VMEM)
    shape = (groups.shape[0] * per // outs, BLK, BLK)
    with_add = add is not None
    return pl.pallas_call(
        functools.partial(tiles_kernel, first, per, with_add, rolled),
        in_specs=[smem, smem, smem, vmem, vmem] + ([vmem] if with_add else []),
        out_specs=[vmem] * outs,
        out_shape=[(pltpu.HBM if to_hbm else jax.ShapeDtypeStruct)(shape, BF16)] * outs,
        compiler_params=pltpu.CompilerParams(vmem_limit_bytes=10 * 2**20),
        name="tiles",
    )(groups, places, table, wt, e_blocks, *([add] if with_add else []))


def add_kernel(n, *refs):
    for i in range(n):
        mine, came = refs[2 * i], refs[2 * i + 1]
        sent, kept = refs[2 * n + 2 * i], refs[2 * n + 2 * i + 1]
        half = sent.shape[0]

        def one(j, carry, mine=mine, came=came, sent=sent, kept=kept, half=half):
            sent[j] = (mine[j].astype(F32) + came[j].astype(F32)).astype(BF16)
            kept[j] = (mine[half + j].astype(F32) + came[half + j].astype(F32)).astype(BF16)
            return carry

        lax.fori_loop(0, half, one, 0, unroll=2)


def add_pairs(pairs):
    vmem = pl.BlockSpec(memory_space=pltpu.VMEM)
    shapes = []
    for mine, _ in pairs:
        shapes += [jax.ShapeDtypeStruct((mine.shape[0] // 2, BLK, BLK), BF16)] * 2
    flat = [a for pair in pairs for a in pair]
    return pl.pallas_call(
        functools.partial(add_kernel, len(pairs)),
        in_specs=[vmem] * len(flat),
        out_specs=[vmem] * len(shapes),
        out_shape=shapes,
        compiler_params=pltpu.CompilerParams(vmem_limit_bytes=20 * 2**20),
        name="add_pairs",
    )(*flat)


def finish_kernel(firsts, me_ref, count_ref, table_ref, *refs):
    me = me_ref[0]
    out_ref, done_ref, stage, sem = refs[-4:]
    n = 0
    for i, first in enumerate(firsts):
        mine, came = refs[2 * i], refs[2 * i + 1]
        for j in range(mine.shape[0]):
            s = table_ref[me, 2 * GRP + first + j]
            live = jnp.where(me * GRP + s < count_ref[0], 1.0, 0.0).astype(F32)
            stage[n] = (mine[j].astype(F32) + came[j].astype(F32)) * live
            pltpu.make_async_copy(stage.at[n], out_ref.at[s], sem).start()
            n += 1
    done_ref[...] = jnp.zeros_like(done_ref)
    pltpu.make_async_copy(stage, out_ref.at[pl.ds(0, n)], sem).wait()


def finish(me, counts, table, pairs, firsts, out=None):
    smem = pl.BlockSpec(memory_space=pltpu.SMEM)
    vmem = pl.BlockSpec(memory_space=pltpu.VMEM)
    hbm = pl.BlockSpec(memory_space=pltpu.HBM)
    flat = [a for pair in pairs for a in pair]
    n = sum(mine.shape[0] for mine, _ in pairs)
    given = out is not None
    return pl.pallas_call(
        functools.partial(finish_kernel, firsts),
        in_specs=[smem, smem, smem] + [vmem] * len(flat)
        + ([hbm, pl.BlockSpec(memory_space=pl.ANY)] if given else []),
        out_specs=[hbm, vmem],
        out_shape=[pltpu.HBM((GRP, BLK, BLK), F32), jax.ShapeDtypeStruct((8, BLK), F32)],
        input_output_aliases={3 + len(flat): 0} if given else {},
        scratch_shapes=[pltpu.VMEM((n, BLK, BLK), F32), pltpu.SemaphoreType.DMA],
        compiler_params=pltpu.CompilerParams(vmem_limit_bytes=16 * 2**20),
        name="finish",
    )(me, counts, table, *flat, *(out if given else ()))


CORE, ALONG_X, UP_Y, DOWN_Y = 1, 2, 4, 12
ORDERS = (
    (ALONG_X, UP_Y, DOWN_Y),
    (UP_Y, DOWN_Y, ALONG_X),
    (DOWN_Y, ALONG_X, UP_Y),
)
TURNS = (ORDERS, ORDERS[1:] + ORDERS[:1])


def swap(a, mask):
    n = lax.axis_size("tm")
    return lax.ppermute(a, "tm", [(i, i ^ mask) for i in range(n)])


def after(a, other):
    return lax.optimization_barrier((a, other))[0]


def order_masks(order, lead):
    first, second, third = order
    return [lead * first ^ s * second ^ t * third for s in (1, 0) for t in (1, 0)]


def body(adjoint, emission, step_weights, tile_list, counts):
    owners = lax.axis_size("tile")
    parts = lax.axis_size("tm")
    own = lax.axis_index("tile").astype(I32).reshape(1)
    me = lax.axis_index("tm").astype(I32).reshape(1)
    cuts = ((6, 6, 6), (5, 5, 4))
    split = sum(cuts[0])
    request, table = plan(own, counts, tile_list, owners, split)
    asked = lax.all_to_all(request, "tile", split_axis=0, concat_axis=0, tiled=True)
    outgoing = pack(own, asked, emission)
    far = lax.all_to_all(outgoing, "tile", split_axis=0, concat_axis=0, tiled=True)
    crowded = jnp.any(asked[:, CAP] > 0)
    weights = step_weights[:, None]

    others = me ^ CORE ^ (2 * jnp.arange(parts // 2, dtype=I32))
    offsets = [[c * split + sum(cuts[c][:i]) for i in range(3)] for c in range(2)]

    def given(c, i, wt, e_blocks, last, rolled=False):
        return tiles(
            after(others, last), others, table, wt, e_blocks, offsets[c][i], cuts[c][i], 1, rolled
        )[0]

    def kept(c, i, wt, e_blocks, last, core, rolled=False):
        masks = [m for lead in (1, 0) for m in order_masks(TURNS[c][i], lead)]
        mine = me ^ jnp.array(masks, I32)
        places = jnp.array([m // 2 for m in masks], I32)
        return tiles(
            after(mine, last), places, table, wt, e_blocks, offsets[c][i], cuts[c][i], 2, rolled, core, c == 0
        )

    def exchange(c, outs, step):
        return [(out[1], swap(out[0], order[step])) for out, order in zip(outs, TURNS[c])]

    def halve(pairs, last):
        outs = []
        for mine, came in pairs:
            out = add_pairs([(after(mine, last), came)])
            last = out[1]
            outs.append(out)
        return outs, last

    wt, e_blocks = prep(after(weights, outgoing), adjoint, emission)
    last, cores, early = wt, [], []
    for i in range(3):
        last = given(0, i, wt, e_blocks, last)
        cores.append(swap(last, CORE))
    for i in range(3):
        early.append(kept(0, i, wt, e_blocks, last, cores[i]))
        last = early[i][1]
    early = exchange(0, early, 0)
    wt, e_blocks = prep(after(weights, last), adjoint, emission, far)
    last, cores, late = wt, [], []
    halved = []
    for i in range(3):
        last = given(1, i, wt, e_blocks, last)
        cores.append(swap(last, CORE))
        for j in ((0,), (1, 2), ())[i]:
            some, last = halve(early[j : j + 1], last)
            halved += some
    early = exchange(0, halved, 1)
    for i in range(3):
        if i == 2:
            early, last = halve(early, last)
            early = exchange(0, early, 2)
        late.append(kept(1, i, wt, e_blocks, last, cores[i]))
        last = late[i][1]
    late = exchange(1, late, 0)
    late, last = halve(late, (last, crowded))
    late, last = halve(exchange(1, late, 1), last)
    late = exchange(1, late, 2)
    out, done = finish(after(me, last), counts, table, early, tuple(offsets[0]))
    out, _ = finish(me, counts, table, late, tuple(offsets[1]), (out, done))

    def crowded_group(state):
        out = state[1]
        wt, e_blocks = prep(after(weights, out), adjoint, emission, far)
        last, cores, again = wt, [], []
        for i in range(3):
            last = given(0, i, wt, e_blocks, last, True)
            cores.append(swap(last, CORE))
        for i in range(3):
            again.append(kept(0, i, wt, e_blocks, last, cores[i], True))
            last = again[i][1]
        for step in range(2):
            again, last = halve(exchange(0, again, step), last)
        out, _ = finish(me, counts, table, exchange(0, again, 2), tuple(offsets[0]), (out, counts))
        return jnp.zeros((), bool), out

    return lax.while_loop(lambda state: state[0], crowded_group, (crowded, out))[1][None]


def solution(mesh):
    in_specs = (P("tm", "tile"), P("tm", "tile"), P("tm"), P("tile", None), P("tile"))
    out_specs = P("tile", "tm", None, None)
    return jax.shard_map(body, mesh=mesh, in_specs=in_specs, out_specs=out_specs, check_vma=False)
```

```python
import functools

import jax
import jax.numpy as jnp
from jax import lax
from jax.experimental import pallas as pl
from jax.experimental.pallas import tpu as pltpu
from jax.sharding import PartitionSpec as P

BLK = 128
CAP = 4
GRP = 32
KA = 384
F32 = jnp.float32
BF16 = jnp.bfloat16
I32 = jnp.int32


def iota(shape, dim):
    return lax.broadcasted_iota(I32, shape, dim)


def in_hbm(a):
    return pltpu.with_memory_space_constraint(a, pltpu.HBM)


def plan_kernel(early, own_ref, count_ref, tiles_ref, request_ref, table_ref):
    slots = tiles_ref.shape[1]
    own = own_ref[0]
    both = jnp.concatenate([tiles_ref[...].astype(F32), jnp.zeros((6, slots), F32)], axis=0)
    both = both.T.astype(I32)
    r = both[:, 0:1]
    c = both[:, 1:2]
    k = iota((slots, 1), 0)
    src = c >> 7
    within = c & (BLK - 1)
    row = r & (BLK - 1)
    remote = (k < count_ref[0]) & (src != own)
    lane = iota((slots, BLK), 1)
    by_src = jnp.where((lane == src) & remote, 1.0, 0.0).astype(F32)
    by_block = jnp.where(lane == within, 1.0, 0.0).astype(F32)
    named = jnp.dot(by_src.T.astype(BF16), by_block.astype(BF16), preferred_element_type=F32)
    hit = jnp.where(named > 0.0, 1.0, 0.0).astype(F32)
    upper = jnp.where(iota((BLK, BLK), 0) <= iota((BLK, BLK), 1), 1.0, 0.0).astype(BF16)
    rank = jnp.dot(hit.astype(BF16), upper, preferred_element_type=F32) * hit
    slot_rank = jnp.sum(
        jnp.dot(by_src.astype(BF16), rank.astype(BF16), preferred_element_type=F32) * by_block,
        axis=1,
        keepdims=True,
    )
    slot_rank = jnp.clip(slot_rank.astype(I32) - 1, 0, CAP - 1)
    col = jnp.where(remote, BLK + src * CAP + slot_rank, within)

    jj = iota((slots, slots), 1)
    kk = iota((slots, slots), 0)
    same = (jj >> 5) == (kk >> 5)
    remote_f = jnp.broadcast_to(jnp.where(remote, 1.0, 0.0), (slots, BLK)).astype(BF16)
    ahead = jnp.where(same & (jj < kk), 1.0, 0.0).astype(BF16)
    ahead = jnp.dot(ahead, remote_f, preferred_element_type=F32)[:, 0:1].astype(I32)
    total = jnp.where(same, 1.0, 0.0).astype(BF16)
    total = jnp.dot(total, remote_f, preferred_element_type=F32)[:, 0:1].astype(I32)
    s = k & (GRP - 1)
    pos = jnp.where(remote, GRP - total + ahead, s - ahead)
    value = jnp.where(lane < GRP, row, jnp.where(lane < 2 * GRP, col, s))
    value = jnp.where((lane & (GRP - 1)) == pos, value, 0)
    value = jnp.where(lane < 3 * GRP, value, 0).astype(F32).astype(BF16)
    groups = slots // GRP
    pick = jnp.where((iota((groups, slots), 1) >> 5) == iota((groups, slots), 0), 1.0, 0.0)
    table_ref[...] = jnp.dot(pick.astype(BF16), value, preferred_element_type=F32).astype(I32)

    late = jnp.max(jnp.where(total > GRP - early, 1, 0), axis=0, keepdims=True)
    owners = request_ref.shape[0]
    hit8 = hit[0:owners, :]
    rank8 = rank[0:owners, :]
    lane8 = iota((owners, BLK), 1)
    request = jnp.where(lane8 == CAP, jnp.broadcast_to(late, (owners, BLK)), 0)
    for q in range(CAP):
        block = jnp.sum(
            jnp.where((rank8 == q + 1.0) & (hit8 > 0.0), lane8, 0), axis=1, keepdims=True
        )
        request = jnp.where(lane8 == q, block, request)
    request_ref[...] = request


def plan(own, counts, tile_list, owners, early):
    slots = tile_list.shape[0]
    smem = pl.BlockSpec(memory_space=pltpu.SMEM)
    vmem = pl.BlockSpec(memory_space=pltpu.VMEM)
    return pl.pallas_call(
        functools.partial(plan_kernel, early),
        in_specs=[smem, smem, vmem],
        out_specs=[vmem, vmem],
        out_shape=[
            jax.ShapeDtypeStruct((owners, BLK), I32),
            jax.ShapeDtypeStruct((slots // GRP, BLK), I32),
        ],
        compiler_params=pltpu.CompilerParams(vmem_limit_bytes=16 * 2**20),
        name="plan",
    )(own, counts, tile_list.T)


STEP = 16
DEPTH = 3
PARTS = 2


def prep_kernel(with_far, weights_ref, adj_ref, em_ref, *refs):
    if with_far:
        far_ref, refs = refs[0], refs[1:]
        refs, fsem = refs[:-1], refs[-1]
    wt_ref, e_ref, abuf, ebuf, wide, asem, esem = refs
    steps = adj_ref.shape[0]
    blocks = wt_ref.shape[0]
    chunks = blocks // STEP
    part = STEP // PARTS * BLK

    def copies(j, h):
        slot = lax.rem(j, DEPTH)
        cols = pl.ds(pl.multiple_of(j * (STEP * BLK) + h * part, part), part)
        here = pl.ds(h * part, part)
        return (
            pltpu.make_async_copy(adj_ref.at[:, cols], abuf.at[slot, :, here], asem.at[slot, h]),
            pltpu.make_async_copy(em_ref.at[:, cols], ebuf.at[slot, :, here], esem.at[slot, h]),
        )

    def start(j):
        for h in range(PARTS):
            for copy in copies(j, h):
                copy.start()

    for j in range(DEPTH - 1):
        start(j)
    wide[...] = jnp.broadcast_to(weights_ref[...], wide.shape)
    if with_far:
        rest = pl.ds(blocks, e_ref.shape[0] - blocks)
        far_copy = pltpu.make_async_copy(far_ref, e_ref.at[rest, pl.ds(0, steps)], fsem)
        far_copy.start()
    ones = jnp.where(iota((KA - steps, BLK), 0) < 2, 1.0, 0.0).astype(BF16)
    rows = iota((KA - steps, BLK), 0)

    def chunk(j, carry):
        slot = lax.rem(j, DEPTH)

        @pl.when(j + DEPTH - 1 < chunks)
        def _():
            start(j + DEPTH - 1)

        for b in range(STEP):
            if b % (STEP // PARTS) == 0:
                for copy in copies(j, b // (STEP // PARTS)):
                    copy.wait()
            at = j * STEP + b
            w = (wide[...] * abuf[slot, :, b * BLK : (b + 1) * BLK].astype(F32)).astype(BF16)
            e = ebuf[slot, :, b * BLK : (b + 1) * BLK]
            sums = -jnp.sum(w.astype(F32) * e.astype(F32), axis=0, keepdims=True)
            high = sums.astype(BF16).astype(F32)
            low = sums - high
            tail = jnp.where(rows == 0, high, jnp.where(rows == 1, low, 0.0)).astype(BF16)
            wt_ref[at] = jnp.concatenate([w, tail], axis=0).T
            e_ref[at, 0:steps, :] = e
            e_ref[at, steps:KA, :] = ones
        return carry

    lax.fori_loop(0, chunks, chunk, 0)
    if with_far:
        for i in range(blocks, e_ref.shape[0]):
            e_ref[i, steps:KA, :] = ones
        far_copy.wait()


def prep(weights, adjoint, emission, far=None):
    steps, nodes = adjoint.shape
    blocks = nodes // BLK
    anyspace = pl.BlockSpec(memory_space=pl.ANY)
    vmem = pl.BlockSpec(memory_space=pltpu.VMEM)
    with_far = far is not None
    columns = blocks + (far.shape[0] if with_far else 0)
    wt, e_blocks = pl.pallas_call(
        functools.partial(prep_kernel, with_far),
        in_specs=[vmem] + [anyspace] * (3 if with_far else 2),
        out_specs=[vmem, vmem],
        out_shape=[
            pltpu.VMEM((blocks, BLK, KA), BF16),
            pltpu.VMEM((columns, KA, BLK), BF16),
        ],
        scratch_shapes=[
            pltpu.VMEM((DEPTH, steps, STEP * BLK), BF16),
            pltpu.VMEM((DEPTH, steps, STEP * BLK), BF16),
            pltpu.VMEM((steps, BLK), F32),
            pltpu.SemaphoreType.DMA((DEPTH, PARTS)),
            pltpu.SemaphoreType.DMA((DEPTH, PARTS)),
        ]
        + ([pltpu.SemaphoreType.DMA] if with_far else []),
        compiler_params=pltpu.CompilerParams(vmem_limit_bytes=14 * 2**20),
        name="prep",
    )(weights, in_hbm(adjoint), in_hbm(emission), *([in_hbm(far)] if with_far else []))
    return (
        pltpu.with_memory_space_constraint(wt, pltpu.VMEM),
        pltpu.with_memory_space_constraint(e_blocks, pltpu.VMEM),
    )


def pack_kernel(own_ref, asked_ref, em_ref, out_ref, sems):
    count = out_ref.shape[0]

    def copy(i):
        block = asked_ref[i >> 2, i & (CAP - 1)] & (BLK - 1)
        cols = pl.ds(pl.multiple_of(block * BLK, BLK), BLK)
        return pltpu.make_async_copy(em_ref.at[:, cols], out_ref.at[i], sems.at[i])

    for i in range(count):

        @pl.when(i // CAP != own_ref[0])
        def _():
            copy(i).start()

    for i in range(count):

        @pl.when(i // CAP != own_ref[0])
        def _():
            copy(i).wait()


def pack(own, asked, emission):
    owners = asked.shape[0]
    return pl.pallas_call(
        pack_kernel,
        in_specs=[pl.BlockSpec(memory_space=pltpu.SMEM)] * 2
        + [pl.BlockSpec(memory_space=pl.ANY)],
        out_specs=pl.BlockSpec(memory_space=pltpu.VMEM),
        out_shape=jax.ShapeDtypeStruct((owners * CAP, emission.shape[0], BLK), BF16),
        scratch_shapes=[pltpu.SemaphoreType.DMA((owners * CAP,))],
        compiler_params=pltpu.CompilerParams(vmem_limit_bytes=8 * 2**20),
        name="pack",
    )(own, asked, in_hbm(emission))


def tiles_kernel(first, per, with_add, rolled, *refs):
    groups_ref, places_ref, table_ref, wt_ref, e_ref = refs[:5]
    outs = refs[6:] if with_add else refs[5:]
    last = e_ref.shape[0] - 1
    n = 0
    for out_ref in outs:
        size = out_ref.shape[0] // per

        def one(j, carry, out_ref=out_ref, n=n):
            g = groups_ref[n + j]
            for q in range(per):
                row = table_ref[g, first + q]
                col = jnp.minimum(table_ref[g, GRP + first + q], last)
                acc = jnp.dot(wt_ref[row], e_ref[col], preferred_element_type=F32)
                if with_add:
                    acc = acc + refs[5][places_ref[n + j] * per + q].astype(F32)
                out_ref[j * per + q] = acc.astype(BF16)
            return carry

        if rolled:
            lax.fori_loop(0, size, one, 0)
        else:
            for j in range(size):
                one(j, 0)
        n += size


def tiles(groups, places, table, wt, e_blocks, first, per, outs, rolled, add=None, to_hbm=False):
    smem = pl.BlockSpec(memory_space=pltpu.SMEM)
    vmem = pl.BlockSpec(memory_space=pltpu.VMEM)
    shape = (groups.shape[0] * per // outs, BLK, BLK)
    with_add = add is not None
    return pl.pallas_call(
        functools.partial(tiles_kernel, first, per, with_add, rolled),
        in_specs=[smem, smem, smem, vmem, vmem] + ([vmem] if with_add else []),
        out_specs=[vmem] * outs,
        out_shape=[(pltpu.HBM if to_hbm else jax.ShapeDtypeStruct)(shape, BF16)] * outs,
        compiler_params=pltpu.CompilerParams(vmem_limit_bytes=10 * 2**20),
        name="tiles",
    )(groups, places, table, wt, e_blocks, *([add] if with_add else []))


def add_kernel(n, *refs):
    for i in range(n):
        mine, came = refs[2 * i], refs[2 * i + 1]
        sent, kept = refs[2 * n + 2 * i], refs[2 * n + 2 * i + 1]
        half = sent.shape[0]

        def one(j, carry, mine=mine, came=came, sent=sent, kept=kept, half=half):
            sent[j] = (mine[j].astype(F32) + came[j].astype(F32)).astype(BF16)
            kept[j] = (mine[half + j].astype(F32) + came[half + j].astype(F32)).astype(BF16)
            return carry

        lax.fori_loop(0, half, one, 0, unroll=2)


def add_pairs(pairs):
    vmem = pl.BlockSpec(memory_space=pltpu.VMEM)
    shapes = []
    for mine, _ in pairs:
        shapes += [jax.ShapeDtypeStruct((mine.shape[0] // 2, BLK, BLK), BF16)] * 2
    flat = [a for pair in pairs for a in pair]
    return pl.pallas_call(
        functools.partial(add_kernel, len(pairs)),
        in_specs=[vmem] * len(flat),
        out_specs=[vmem] * len(shapes),
        out_shape=shapes,
        compiler_params=pltpu.CompilerParams(vmem_limit_bytes=20 * 2**20),
        name="add_pairs",
    )(*flat)


def finish_kernel(firsts, me_ref, count_ref, table_ref, *refs):
    me = me_ref[0]
    out_ref, done_ref, stage, sem = refs[-4:]
    n = 0
    for i, first in enumerate(firsts):
        mine, came = refs[2 * i], refs[2 * i + 1]
        for j in range(mine.shape[0]):
            s = table_ref[me, 2 * GRP + first + j]
            live = jnp.where(me * GRP + s < count_ref[0], 1.0, 0.0).astype(F32)
            stage[n] = (mine[j].astype(F32) + came[j].astype(F32)) * live
            pltpu.make_async_copy(stage.at[n], out_ref.at[s], sem).start()
            n += 1
    done_ref[...] = jnp.zeros_like(done_ref)
    pltpu.make_async_copy(stage, out_ref.at[pl.ds(0, n)], sem).wait()


def finish(me, counts, table, pairs, firsts, out=None):
    smem = pl.BlockSpec(memory_space=pltpu.SMEM)
    vmem = pl.BlockSpec(memory_space=pltpu.VMEM)
    hbm = pl.BlockSpec(memory_space=pltpu.HBM)
    flat = [a for pair in pairs for a in pair]
    n = sum(mine.shape[0] for mine, _ in pairs)
    given = out is not None
    return pl.pallas_call(
        functools.partial(finish_kernel, firsts),
        in_specs=[smem, smem, smem] + [vmem] * len(flat)
        + ([hbm, pl.BlockSpec(memory_space=pl.ANY)] if given else []),
        out_specs=[hbm, vmem],
        out_shape=[pltpu.HBM((GRP, BLK, BLK), F32), jax.ShapeDtypeStruct((8, BLK), F32)],
        input_output_aliases={3 + len(flat): 0} if given else {},
        scratch_shapes=[pltpu.VMEM((n, BLK, BLK), F32), pltpu.SemaphoreType.DMA],
        compiler_params=pltpu.CompilerParams(vmem_limit_bytes=16 * 2**20),
        name="finish",
    )(me, counts, table, *flat, *(out if given else ()))


CORE, ALONG_X, UP_Y, DOWN_Y = 1, 2, 4, 12
ORDERS = (
    (ALONG_X, UP_Y, DOWN_Y),
    (UP_Y, DOWN_Y, ALONG_X),
    (DOWN_Y, ALONG_X, UP_Y),
)
TURNS = (ORDERS, ORDERS[1:] + ORDERS[:1])


def swap(a, mask):
    n = lax.axis_size("tm")
    return lax.ppermute(a, "tm", [(i, i ^ mask) for i in range(n)])


def after(a, other):
    return lax.optimization_barrier((a, other))[0]


def order_masks(order, lead):
    first, second, third = order
    return [lead * first ^ s * second ^ t * third for s in (1, 0) for t in (1, 0)]


def body(adjoint, emission, step_weights, tile_list, counts):
    owners = lax.axis_size("tile")
    parts = lax.axis_size("tm")
    own = lax.axis_index("tile").astype(I32).reshape(1)
    me = lax.axis_index("tm").astype(I32).reshape(1)
    cuts = ((6, 6, 6), (5, 5, 4))
    split = sum(cuts[0])
    request, table = plan(own, counts, tile_list, owners, split)
    asked = lax.all_to_all(request, "tile", split_axis=0, concat_axis=0, tiled=True)
    outgoing = pack(own, asked, emission)
    far = lax.all_to_all(outgoing, "tile", split_axis=0, concat_axis=0, tiled=True)
    crowded = jnp.any(asked[:, CAP] > 0)
    weights = step_weights[:, None]

    others = me ^ CORE ^ (2 * jnp.arange(parts // 2, dtype=I32))
    offsets = [[c * split + sum(cuts[c][:i]) for i in range(3)] for c in range(2)]

    def given(c, i, wt, e_blocks, last, rolled=False):
        return tiles(
            after(others, last), others, table, wt, e_blocks, offsets[c][i], cuts[c][i], 1, rolled
        )[0]

    def kept(c, i, wt, e_blocks, last, core, rolled=False):
        masks = [m for lead in (1, 0) for m in order_masks(TURNS[c][i], lead)]
        mine = me ^ jnp.array(masks, I32)
        places = jnp.array([m // 2 for m in masks], I32)
        return tiles(
            after(mine, last), places, table, wt, e_blocks, offsets[c][i], cuts[c][i], 2, rolled, core, (c, i) == (0, 2)
        )

    def exchange(c, outs, step):
        return [(out[1], swap(out[0], order[step])) for out, order in zip(outs, TURNS[c])]

    def halve(pairs, last):
        outs = []
        for mine, came in pairs:
            out = add_pairs([(after(mine, last), came)])
            last = out[1]
            outs.append(out)
        return outs, last

    wt, e_blocks = prep(after(weights, outgoing), adjoint, emission)
    last, cores, early = wt, [], []
    for i in range(3):
        last = given(0, i, wt, e_blocks, last)
        cores.append(swap(last, CORE))
    for i in range(3):
        early.append(kept(0, i, wt, e_blocks, last, cores[i]))
        last = early[i][1]
    early = exchange(0, early, 0)
    wt, e_blocks = prep(after(weights, last), adjoint, emission, far)
    last, cores, late = wt, [], []
    halved = []
    for i in range(3):
        last = given(1, i, wt, e_blocks, last)
        cores.append(swap(last, CORE))
        for j in ((0,), (1, 2), ())[i]:
            some, last = halve(early[j : j + 1], last)
            halved += some
    early = exchange(0, halved, 1)
    for i in range(3):
        if i == 2:
            early, last = halve(early, last)
            early = exchange(0, early, 2)
        late.append(kept(1, i, wt, e_blocks, last, cores[i]))
        last = late[i][1]
    late = exchange(1, late, 0)
    late, last = halve(late, (last, crowded))
    late, last = halve(exchange(1, late, 1), last)
    late = exchange(1, late, 2)
    out, done = finish(after(me, last), counts, table, early, tuple(offsets[0]))
    out, _ = finish(me, counts, table, late, tuple(offsets[1]), (out, done))

    def crowded_group(state):
        out = state[1]
        wt, e_blocks = prep(after(weights, out), adjoint, emission, far)
        last, cores, again = wt, [], []
        for i in range(3):
            last = given(0, i, wt, e_blocks, last, True)
            cores.append(swap(last, CORE))
        for i in range(3):
            again.append(kept(0, i, wt, e_blocks, last, cores[i], True))
            last = again[i][1]
        for step in range(2):
            again, last = halve(exchange(0, again, step), last)
        out, _ = finish(me, counts, table, exchange(0, again, 2), tuple(offsets[0]), (out, counts))
        return jnp.zeros((), bool), out

    return lax.while_loop(lambda state: state[0], crowded_group, (crowded, out))[1][None]


def solution(mesh):
    in_specs = (P("tm", "tile"), P("tm", "tile"), P("tm"), P("tile", None), P("tile"))
    out_specs = P("tile", "tm", None, None)
    return jax.shard_map(body, mesh=mesh, in_specs=in_specs, out_specs=out_specs, check_vma=False)
```
